32 devices in a mesh: samp: 4 (over y, x), snp: 8 (over z, core).
Axes of the slice: x: 2, y: 2, z: 4, core: 2. Of those that a mesh axis runs over, the one named last changes fastest.
Arguments:
- dosage: bfloat16 [8192, 4096], P('samp', 'snp'), may hold values from 0 to 2
- band_width: int32 [8], P('snp'), may hold values from 1 to 3, as said below
- marginal: float32 [4096, 64], P('snp'), may hold values from -6 to 6
- penalty: float32 [64], replicated, may hold values from 4 to 16
Outputs:
- effects: float32 [4096, 64], P('snp')
- residual: float32 [4096, 64], P('snp')
The draws below stay inside these ranges and needn't reach their ends.
Inputs may be any that keep to these rules, and one draw needn't show every extreme that they name: `band_width`: every draw has a block with 3 neighbours and one with a single neighbour.
All inputs are finite; a program needn't handle non-finite values.
Results may differ from the reference program's by a relative error of at most 0.00087.
Values may be sent and summed in bfloat16 or wider, within the bound.
No kernel may reach another device: no remote copies, remote signals or barrier semaphores. Data moves between devices by JAX's collectives and lax.ppermute only.
A program may use at most 64 MiB of HBM per device.

```python
import math
import jax
import jax.numpy as jnp
from jax import lax

BLK = 512
WMAX = 3
TRAITS = 64
ITERS = 2
SAMPLES = 8192
NBLK = 8
SNPS = 4096


def draw_dosage(key, part):
    subkeys = jax.random.split(jax.random.fold_in(key, 11), 4)
    decay_rate = math.exp(-1.0 / 128.0)
    innovations = jax.random.normal(subkeys[0], (SNPS, SAMPLES), jnp.float32)

    def advance(carry, fresh):
        updated = decay_rate * carry + math.sqrt(1.0 - decay_rate * decay_rate) * fresh
        return (updated, updated)
    starting = jax.random.normal(subkeys[1], (SAMPLES,), jnp.float32)
    _, ancestry_walk = lax.scan(advance, starting, innovations)
    local_noise = jax.random.normal(subkeys[2], (SAMPLES, SNPS), jnp.float32)
    frequency = jax.random.uniform(subkeys[3], (SNPS,), jnp.float32, -1.2, 1.2)
    latent = 0.9 * ancestry_walk.T + 0.7 * local_noise + frequency
    return (2.0 * jax.nn.sigmoid(latent)).astype(jnp.bfloat16)


def draw_band_width(key, part):
    subkeys = jax.random.split(jax.random.fold_in(key, 23), 2)
    widths = jax.random.randint(subkeys[0], (NBLK,), 1, WMAX + 1)
    shuffled = jax.random.permutation(subkeys[1], NBLK)
    return widths.at[shuffled[0]].set(WMAX).at[shuffled[1]].set(1).astype(jnp.int32)


def shard_levels(rng, dims, shards, low, largest):
    level, own = 1.0, jax.random.fold_in(rng, 6)
    for position, shards_of in shards:
        draws = jnp.exp(jax.random.uniform(jax.random.fold_in(own, position), (shards_of,), jnp.float32, low / len(shards), largest / len(shards)))
        level = level * jnp.repeat(draws, dims[position] // shards_of).reshape([-1 if axis == position else 1 for axis in range(len(dims))])
    return level


def gaussian(stream_key, shape, width, limit, shards=(), kind=jnp.bfloat16):
    array = jax.random.normal(stream_key, shape, jnp.float32) * width
    if len(shards) > 0:
        array = shard_levels(stream_key, shape, shards, -0.22, 0.18) * array
    return jnp.clip(array, min=-limit, max=limit).astype(kind)


def setup_inputs(seed: int = 0) -> dict:
    key_list = jax.random.split(jax.random.key(seed), 5)
    dosage = draw_dosage(jax.random.fold_in(key_list[4], 71), 0)
    band_width = draw_band_width(jax.random.fold_in(key_list[4], 71), 0)
    marginal = gaussian(key_list[2], (SNPS, TRAITS), 1.0, 6.0, ((0, 8),), jnp.float32)
    penalty = jnp.clip(jnp.exp(jax.random.uniform(key_list[3], (TRAITS,), jnp.float32, math.log(4.0), math.log(16.0))), 4.0, 16.0)
    return dict(dosage=dosage, band_width=band_width, marginal=marginal, penalty=penalty)


def reference(dosage, band_width, marginal, penalty):
    samples = dosage.shape[0]
    genotype = dosage.astype(jnp.float32)
    center = lax.optimization_barrier(jnp.sum(genotype, 0)) / samples
    spread = lax.optimization_barrier(jnp.sum(genotype * genotype, 0)) / samples - center * center
    scaled = ((genotype - center) * lax.rsqrt(spread + 1e-05)).astype(jnp.bfloat16)
    padded = jnp.concatenate([scaled, jnp.zeros((samples, WMAX * BLK), jnp.bfloat16)], 1)
    offsets = jnp.arange((WMAX + 1) * BLK, dtype=jnp.int32) // BLK

    def band_rows(index):
        start = (index * BLK).astype(jnp.int32)
        own_cols = lax.dynamic_slice_in_dim(scaled, start, BLK, 1)
        wide_cols = lax.dynamic_slice_in_dim(padded, start, (WMAX + 1) * BLK, 1)
        gram = jnp.dot(own_cols.T, wide_cols, preferred_element_type=jnp.float32)
        return jnp.where(offsets[None, :] <= band_width[index], gram, 0.0) / samples
    ld_band = lax.map(band_rows, jnp.arange(NBLK, dtype=jnp.int32))
    highest = lax.Precision.HIGHEST

    def operate(direction):
        blocks = direction.reshape(NBLK, BLK, direction.shape[1])
        padded_dir = jnp.concatenate([blocks, jnp.zeros((WMAX, BLK, blocks.shape[2]), blocks.dtype)], 0)
        result = jnp.zeros_like(blocks)
        for offset in range(WMAX + 1):
            ld_block = ld_band[:, :, offset * BLK:(offset + 1) * BLK]
            result = result + jnp.einsum('iab,ibt->iat', ld_block, padded_dir[offset:offset + NBLK], precision=highest)
            if offset > 0:
                moved = jnp.einsum('iab,iat->ibt', ld_block, blocks, precision=highest)
                result = result.at[offset:].add(moved[:NBLK - offset])
        return result.reshape(direction.shape) + penalty * direction
    effects = jnp.zeros_like(marginal)
    residual = marginal
    direction = marginal
    norm_now = lax.optimization_barrier(jnp.sum(residual * residual, 0))
    for sweep in range(ITERS):
        imaged = operate(direction)
        step_size = norm_now / lax.optimization_barrier(jnp.sum(direction * imaged, 0))
        effects = effects + step_size * direction
        residual = residual - step_size * imaged
        norm_next = lax.optimization_barrier(jnp.sum(residual * residual, 0))
        direction = residual + norm_next / norm_now * direction
        norm_now = norm_next
    return (effects, residual)
```

```python
import jax
import jax.numpy as jnp
from jax import lax
from jax.sharding import PartitionSpec as P


AUX = 128


def permute(value, axis, pairs):
    return lax.ppermute(value, axis, pairs)


def swap(value, axis, bit):
    return permute(value, axis, [(i, i ^ bit) for i in range(lax.axis_size(axis))])


def shift(value, distance):
    count = lax.axis_size("snp")
    return permute(value, "snp", [(i, i + distance) for i in range(count) if 0 <= i + distance < count])


def far_shift(value):
    count = lax.axis_size("snp")
    up = [(i, i + 3) for i in range(1, count, 2) if i + 3 < count]
    down = [(i, i - 3) for i in range(0, count, 2) if i - 3 >= 0]
    return permute(value, "snp", up + down)


def sum_over(value, axis):
    count = lax.axis_size(axis)
    if count & (count - 1):
        return lax.psum(value, axis)
    bit = 1
    while bit < count:
        value = value + swap(value, axis, bit)
        bit *= 2
    return value


def two_terms(value):
    high = lax.reduce_precision(value, 8, 7)
    low = value - high
    return jnp.concatenate([high.astype(jnp.bfloat16), low.astype(jnp.bfloat16)], 0)


def product(value, scaled, contract):
    rows = value.shape[0]
    both = lax.dot_general(
        two_terms(value), scaled, (((1,), (contract,)), ((), ())), preferred_element_type=jnp.float32
    )
    return both[:rows] + both[rows:]


def pack(value, width):
    peak = jnp.maximum(jnp.max(jnp.abs(value), 1, keepdims=True), 1e-30)
    exponent = jnp.floor(jnp.log2(peak))
    coded = (value * jnp.exp2(-exponent)).astype(jnp.float16)
    lane = lax.broadcasted_iota(jnp.int32, (value.shape[0], AUX), 1)
    extra = jnp.where(lane == 0, exponent, jnp.where(lane == 1, width, 0.0)).astype(jnp.float16)
    return jnp.concatenate([coded, extra], 1)


def unpack(coded):
    count = coded.shape[1] - AUX
    exponent = coded[:, count : count + 1].astype(jnp.float32)
    width = coded[:, count + 1 : count + 2].astype(jnp.float32)
    return coded[:, :count].astype(jnp.float32) * jnp.exp2(exponent), width


def window(own, width, partner_width, odd):
    coded = pack(own, width)
    below = shift(coded, 2)
    above = shift(coded, -2)
    far = far_shift(coded)
    below, below_width = unpack(below)
    above, _ = unpack(above)
    pick = lambda even_case, odd_case: jnp.where(odd, odd_case, even_case)
    give = (
        own * (pick(width, partner_width) >= 1)
        + below * (below_width >= pick(3.0, 1.0))
        + above * (partner_width >= pick(1.0, 3.0))
    )
    given = swap(give, "snp", 1)
    far, far_width = unpack(far)
    return (
        own
        + below * (below_width >= 2)
        + above * (width >= 2)
        + given
        + far * (pick(far_width, width) >= 3)
    )


def shards(dosage, band_width, marginal, penalty):
    samples = dosage.shape[0] * lax.axis_size("samp")
    odd = lax.axis_index("snp") % 2 == 1
    width = band_width.astype(jnp.float32).reshape(1, 1)
    partner_width = swap(jnp.broadcast_to(width, (8, 128)), "snp", 1)[:1, :1]
    genotype = dosage.astype(jnp.float32)
    sums = sum_over(jnp.stack([jnp.sum(genotype, 0), jnp.sum(genotype * genotype, 0)]), "samp")
    center = sums[0] / samples
    spread = sums[1] / samples - center * center
    scaled = ((genotype - center) * lax.rsqrt(spread + 1e-05)).astype(jnp.bfloat16)
    start = marginal.T
    shrink = penalty[:, None]

    def operate(value):
        mixed = window(product(value, scaled, 1), width, partner_width, odd)
        return sum_over(product(mixed, scaled, 0), "samp") / samples

    first = operate(start)
    second = operate(first)
    dot = lambda a, b: jnp.sum(a * b, 1, keepdims=True)
    parts = jnp.concatenate([dot(start, start), dot(start, first), dot(first, first), dot(first, second)], 1)
    parts = sum_over(parts, "snp")
    bb, bw, ww, wu = (parts[:, k : k + 1] for k in range(4))
    ratio = bw / bb
    step = 1.0 / (ratio + shrink)
    norm = step * step * (ww - ratio * bw)
    bend = norm / bb
    curve = step * step * (ratio * (ratio * bw - 2.0 * ww) + wu) + shrink * norm - bend * norm / step
    step2 = jnp.where(curve > 0, norm / curve, 0.0)
    rest = step * (ratio * start - first)
    direction = rest + bend * start
    image = step * (ratio * first - second) + bend * first + shrink * direction
    effects = step * start + step2 * direction
    residual = rest - step2 * image
    return (effects.T, residual.T)


def solution(mesh):
    in_specs = (P("samp", "snp"), P("snp"), P("snp", None), P())
    out_specs = (P("snp", None), P("snp", None))
    return jax.shard_map(shards, mesh=mesh, in_specs=in_specs, out_specs=out_specs, check_vma=False)
```

```python
import jax
import jax.numpy as jnp
from jax import lax
from jax.sharding import PartitionSpec as P


AUX = 128


def permute(value, axis, pairs):
    return lax.ppermute(value, axis, pairs)


def swap(value, axis, bit):
    return permute(value, axis, [(i, i ^ bit) for i in range(lax.axis_size(axis))])


def shift(value, distance):
    count = lax.axis_size("snp")
    return permute(value, "snp", [(i, i + distance) for i in range(count) if 0 <= i + distance < count])


def forward(value):
    count = lax.axis_size("snp")
    up = [(i, i + 1) for i in range(1, count, 2) if i + 1 < count]
    down = [(i, i - 1) for i in range(0, count, 2) if i - 1 >= 0]
    return permute(value, "snp", up + down)


def snp_sum(value):
    count = lax.axis_size("snp")
    if count & (count - 1):
        return lax.psum(value, "snp")
    bit = 1
    while bit < count:
        value = value + swap(value, "snp", bit)
        bit *= 2
    return value


def samp_sum(value):
    rows, count = lax.axis_size("samp"), lax.axis_size("snp")
    if rows & (rows - 1):
        return lax.psum(value, "samp")
    bits = [1 << k for k in range(rows.bit_length() - 1)]
    for even_bit, odd_bit in zip(bits, bits[::-1]):
        pairs = [
            (row * count + col, (row ^ (odd_bit if col % 2 else even_bit)) * count + col)
            for row in range(rows)
            for col in range(count)
        ]
        value = value + permute(value, ("samp", "snp"), pairs)
    return value


def two_terms(value):
    high = lax.reduce_precision(value, 8, 7)
    low = value - high
    return jnp.concatenate([high.astype(jnp.bfloat16), low.astype(jnp.bfloat16)], 0)


def product(value, scaled, contract):
    rows = value.shape[0]
    both = lax.dot_general(
        two_terms(value), scaled, (((1,), (contract,)), ((), ())), preferred_element_type=jnp.float32
    )
    return both[:rows] + both[rows:]


def pack(value, width):
    peak = jnp.maximum(jnp.max(jnp.abs(value), 1, keepdims=True), 1e-30)
    exponent = jnp.floor(jnp.log2(peak))
    coded = (value * jnp.exp2(-exponent)).astype(jnp.float16)
    lane = lax.broadcasted_iota(jnp.int32, (value.shape[0], AUX), 1)
    extra = jnp.where(lane == 0, exponent, jnp.where(lane == 1, width, 0.0)).astype(jnp.float16)
    return jnp.concatenate([coded, extra], 1)


def unpack(coded):
    count = coded.shape[1] - AUX
    exponent = coded[:, count : count + 1].astype(jnp.float32)
    width = coded[:, count + 1 : count + 2].astype(jnp.float32)
    return coded[:, :count].astype(jnp.float32) * jnp.exp2(exponent), width


def window(own, width, partner_width, odd):
    coded = pack(own, width)
    below_coded = shift(coded, 2)
    above_coded = shift(coded, -2)
    far = forward(jnp.where(odd, below_coded, above_coded))
    below, below_width = unpack(below_coded)
    above, _ = unpack(above_coded)
    pick = lambda even_case, odd_case: jnp.where(odd, odd_case, even_case)
    give = (
        own * (pick(width, partner_width) >= 1)
        + below * (below_width >= pick(3.0, 1.0))
        + above * (partner_width >= pick(1.0, 3.0))
    )
    given = swap(give, "snp", 1)
    far, far_width = unpack(far)
    return (
        own
        + below * (below_width >= 2)
        + above * (width >= 2)
        + given
        + far * (pick(far_width, width) >= 3)
    )


def shards(dosage, band_width, marginal, penalty):
    samples = dosage.shape[0] * lax.axis_size("samp")
    odd = lax.axis_index("snp") % 2 == 1
    width = band_width.astype(jnp.float32).reshape(1, 1)
    partner_width = swap(jnp.broadcast_to(width, (8, 128)), "snp", 1)[:1, :1]
    genotype = dosage.astype(jnp.float32)
    sums = jnp.stack([jnp.sum(genotype, 0), jnp.sum(genotype * genotype, 0)])
    sums, partner_width = lax.optimization_barrier((sums, partner_width))
    sums = samp_sum(sums)
    center = sums[0] / samples
    spread = sums[1] / samples - center * center
    scaled = ((genotype - center) * lax.rsqrt(spread + 1e-05)).astype(jnp.bfloat16)
    start = marginal.T
    shrink = penalty[:, None]

    def operate(value):
        mixed = window(product(value, scaled, 1), width, partner_width, odd)
        return samp_sum(product(mixed, scaled, 0)) / samples

    first = operate(start)
    second = operate(first)
    dot = lambda a, b: jnp.sum(a * b, 1, keepdims=True)
    parts = jnp.concatenate([dot(start, start), dot(start, first), dot(first, first), dot(first, second)], 1)
    parts = snp_sum(parts)
    bb, bw, ww, wu = (parts[:, k : k + 1] for k in range(4))
    ratio = bw / bb
    step = 1.0 / (ratio + shrink)
    norm = step * step * (ww - ratio * bw)
    bend = norm / bb
    curve = step * step * (ratio * (ratio * bw - 2.0 * ww) + wu) + shrink * norm - bend * norm / step
    step2 = jnp.where(curve > 0, norm / curve, 0.0)
    rest = step * (ratio * start - first)
    direction = rest + bend * start
    image = step * (ratio * first - second) + bend * first + shrink * direction
    effects = step * start + step2 * direction
    residual = rest - step2 * image
    return (effects.T, residual.T)


def solution(mesh):
    in_specs = (P("samp", "snp"), P("snp"), P("snp", None), P())
    out_specs = (P("snp", None), P("snp", None))
    return jax.shard_map(shards, mesh=mesh, in_specs=in_specs, out_specs=out_specs, check_vma=False)
```

```python
import jax
import jax.numpy as jnp
from jax import lax
from jax.sharding import PartitionSpec as P


AUX = 128


def swap(value, axis, bits):
    return lax.ppermute(value, axis, [(i, i ^ bits) for i in range(lax.axis_size(axis))])


def crossing(value, rising):
    count = lax.axis_size("snp")
    pairs = []
    for i in range(count):
        target = i + 2 if i % 2 == rising else i - 2
        pairs.append((i, target if 0 <= target < count else i ^ 1))
    return lax.ppermute(value, "snp", pairs)


def forward(value):
    count = lax.axis_size("snp")
    pairs = [(i, i + 1) for i in range(1, count - 1, 2)] + [(i, i - 1) for i in range(2, count, 2)]
    return lax.ppermute(value, "snp", pairs)


def group_sum(value, axis, bits):
    for bit in bits:
        if isinstance(bit, int):
            value = value + swap(value, axis, bit)
        else:
            low, high = bit
            one, two, three = (swap(value, axis, k) for k in (low, high, low + high))
            value = (value + one) + (two + three)
    return value


def stages(bits):
    return [(bits[k], bits[k + 1]) if k + 1 < len(bits) else bits[k] for k in range(0, len(bits), 2)]


def axis_bits(axis):
    return [1 << k for k in range(lax.axis_size(axis).bit_length() - 1)]


def samp_sum(value):
    return group_sum(value, "samp", stages(axis_bits("samp")))


def snp_sum(value):
    bits = axis_bits("snp")
    return group_sum(value, "snp", bits[:1] + stages(bits[1:]))


def two_terms(value):
    high = lax.reduce_precision(value, 8, 7)
    low = value - high
    return jnp.concatenate([high.astype(jnp.bfloat16), low.astype(jnp.bfloat16)], 0)


def product(value, scaled, contract):
    rows = value.shape[0]
    both = lax.dot_general(
        two_terms(value), scaled, (((1,), (contract,)), ((), ())), preferred_element_type=jnp.float32
    )
    return both[:rows] + both[rows:]


def pack(value, width):
    peak = jnp.maximum(jnp.max(jnp.abs(value), 1, keepdims=True), 1e-30)
    exponent = jnp.floor(jnp.log2(peak))
    coded = (value * jnp.exp2(-exponent)).astype(jnp.float16)
    lane = lax.broadcasted_iota(jnp.int32, (value.shape[0], AUX), 1)
    extra = jnp.where(lane == 0, exponent, jnp.where(lane == 1, width, 0.0)).astype(jnp.float16)
    return jnp.concatenate([coded, extra], 1)


def unpack(coded):
    count = coded.shape[1] - AUX
    exponent = coded[:, count : count + 1].astype(jnp.float32)
    width = coded[:, count + 1 : count + 2].astype(jnp.float32)
    return coded[:, :count].astype(jnp.float32), jnp.exp2(exponent), width


def window(own, width, partner_width, place):
    odd, has_below, has_above, has_far = place
    coded = pack(own, width)
    outer_coded = crossing(coded, 1)
    inner_coded = crossing(coded, 0)
    far_coded = forward(outer_coded)
    inner_coded, far_coded = lax.optimization_barrier((inner_coded, far_coded))
    outer, outer_scale, outer_width = unpack(outer_coded)
    inner, inner_scale, inner_width = unpack(inner_coded)
    far, far_scale, far_width = unpack(far_coded)
    at_least = lambda value, least, use: jnp.where((value >= least) & use, 1.0, 0.0)
    choose = lambda even_case, odd_case: jnp.where(odd, odd_case, even_case)
    outer_use, inner_use = choose(has_above, has_below), choose(has_below, has_above)
    give_own = at_least(choose(width, partner_width), 1, True)
    give_outer = outer_scale * at_least(choose(partner_width, outer_width), 1, outer_use)
    give_inner = inner_scale * at_least(choose(inner_width, partner_width), 3, inner_use)
    take_outer = outer_scale * at_least(choose(width, outer_width), 2, outer_use)
    take_inner = inner_scale * at_least(choose(inner_width, width), 2, inner_use)
    take_far = far_scale * at_least(choose(far_width, width), 3, has_far)
    given = swap(own * give_own + outer * give_outer + inner * give_inner, "snp", 1)
    return own + outer * take_outer + inner * take_inner + given + far * take_far


def shards(dosage, band_width, marginal, penalty):
    groups, count = lax.axis_size("samp"), lax.axis_size("snp")
    samples = dosage.shape[0] * groups
    index = lax.axis_index("snp")
    odd = (index & 1) == 1
    has_below, has_above = index >= 2, index < count - 2
    place = (odd, has_below, has_above, jnp.where(odd, index < count - 3, index >= 3))
    genotype = dosage.astype(jnp.float32)
    sums = jnp.stack([jnp.sum(genotype, 0), jnp.sum(genotype * genotype, 0)])
    width = band_width.astype(jnp.float32).reshape(1, 1)
    sums, wide = lax.optimization_barrier((sums, jnp.broadcast_to(width, (8, 128))))
    partner_wide = swap(wide, "snp", 1)
    sums, partner_wide = lax.optimization_barrier((samp_sum(sums), partner_wide))
    partner_width = partner_wide[:1, :1]
    center = sums[0] / samples
    spread = sums[1] / samples - center * center
    scaled = ((genotype - center) * lax.rsqrt(spread + 1e-05)).astype(jnp.bfloat16)
    start = marginal.T
    shrink = penalty[:, None]
    dot = lambda a, b: jnp.sum(a * b, 1, keepdims=True)

    def operate(value):
        spanned = product(value, scaled, 1)
        mixed = window(spanned, width, partner_width, place)
        return samp_sum(product(mixed, scaled, 0)) / samples, dot(spanned, mixed) / samples

    first, _ = operate(start)
    second, curved = operate(first)
    parts = [dot(start, start) / groups, dot(start, first) / groups, dot(first, first) / groups, curved]
    parts = samp_sum(snp_sum(jnp.concatenate(parts, 1)))
    bb, bw, ww, wu = (parts[:, k : k + 1] for k in range(4))
    ratio = bw / bb
    step = 1.0 / (ratio + shrink)
    norm = step * step * (ww - ratio * bw)
    bend = norm / bb
    curve = step * step * (ratio * (ratio * bw - 2.0 * ww) + wu) + shrink * norm - bend * norm / step
    step2 = jnp.where(curve > 0, norm / curve, 0.0)
    rest = step * (ratio * start - first)
    direction = rest + bend * start
    image = step * (ratio * first - second) + bend * first + shrink * direction
    effects = step * start + step2 * direction
    residual = rest - step2 * image
    return (effects.T, residual.T)


def solution(mesh):
    in_specs = (P("samp", "snp"), P("snp"), P("snp", None), P())
    out_specs = (P("snp", None), P("snp", None))
    return jax.shard_map(shards, mesh=mesh, in_specs=in_specs, out_specs=out_specs, check_vma=False)
```

```python
import functools

import jax
import jax.numpy as jnp
from jax import lax
from jax.experimental import pallas as pl
from jax.experimental.pallas import tpu as pltpu
from jax.sharding import PartitionSpec as P


AUX = 128
CHUNK = 512
UNIT = 14


def swap(value, axis, bits):
    return lax.ppermute(value, axis, [(i, i ^ bits) for i in range(lax.axis_size(axis))])


def crossing(value, rising):
    count = lax.axis_size("snp")
    pairs = []
    for i in range(count):
        target = i + 2 if i % 2 == rising else i - 2
        pairs.append((i, target if 0 <= target < count else i ^ 1))
    return lax.ppermute(value, "snp", pairs)


def forward(value):
    count = lax.axis_size("snp")
    pairs = [(i, i + 1) for i in range(3, count - 1, 2)] + [(i, i - 1) for i in range(2, count - 2, 2)]
    pairs += [(1, 0), (0, 2), (count - 2, count - 1), (count - 1, count - 3)]
    return lax.ppermute(value, "snp", pairs)


def partners(value, axis, low, high):
    return [swap(value, axis, k) for k in (low, high, low + high)]


def total(parts):
    own, one, two, three = parts
    return (own + one) + (two + three)


def call(body, out_shape, *args, smem=()):
    specs = [
        pl.BlockSpec(memory_space=pltpu.SMEM if k in smem else pltpu.VMEM) for k in range(len(args))
    ]
    outs = [jax.ShapeDtypeStruct(shape, kind) for shape, kind in out_shape]
    return pl.pallas_call(
        body,
        out_shape=outs,
        in_specs=specs,
        out_specs=[pl.BlockSpec(memory_space=pltpu.VMEM) for _ in outs],
        compiler_params=pltpu.CompilerParams(vmem_limit_bytes=32 << 20),
    )(*args)


def two_terms(value):
    high = value.astype(jnp.bfloat16)
    low = (value - high.astype(jnp.float32)).astype(jnp.bfloat16)
    return jnp.concatenate([high, low], 0)


def stats_kernel(width_ref, dosage_ref, sums_ref):
    row = lax.broadcasted_iota(jnp.int32, (8, 1), 0)
    acc = jnp.zeros((8, dosage_ref.shape[1]), jnp.float32)
    square = acc
    rows = CHUNK // 4
    for k in range(dosage_ref.shape[0] // rows):
        part = dosage_ref[pl.ds(k * rows, rows)].astype(jnp.float32)
        part = part.reshape(rows // 8, 8, part.shape[1])
        acc = acc + jnp.sum(part, 0)
        square = square + jnp.sum(part * part, 0)
    first = jnp.sum(acc, 0, keepdims=True)
    second = jnp.sum(square, 0, keepdims=True)
    width = width_ref[0].astype(jnp.float32)
    sums_ref[...] = jnp.where(row == 0, first, jnp.where(row == 1, second, width))


def encode(own_ref, coded_ref, width):
    samples = own_ref.shape[1]
    peak = jnp.max(jnp.abs(own_ref[...]), 1, keepdims=True)
    exponent = jnp.floor(jnp.log2(jnp.maximum(peak, 1e-30)))
    scale = jnp.exp2(UNIT - exponent)
    for k in range(0, samples, CHUNK):
        part = jnp.clip(jnp.round(own_ref[:, pl.ds(k, CHUNK)] * scale), -32767.0, 32767.0)
        coded_ref[:, pl.ds(k, CHUNK)] = part.astype(jnp.int32).astype(jnp.int16)
    lane = lax.broadcasted_iota(jnp.int32, (own_ref.shape[0], AUX), 1)
    extra = jnp.where(lane == 0, exponent, jnp.where(lane == 1, width, 0.0))
    coded_ref[:, pl.ds(samples, AUX)] = extra.astype(jnp.int32).astype(jnp.int16)


def decode(coded_ref, use):
    samples = coded_ref.shape[1] - AUX
    extra = coded_ref[:, pl.ds(samples, AUX)].astype(jnp.int32).astype(jnp.float32)
    return jnp.where(use, jnp.exp2(extra[:, :1] - UNIT), 0.0), extra[:, 1:2]


def values(coded_ref, k):
    return coded_ref[:, pl.ds(k, CHUNK)].astype(jnp.int32).astype(jnp.float32)


def project(value, scaled_ref, own_ref):
    rows = value.shape[0]
    terms = two_terms(value)
    for k in range(0, scaled_ref.shape[0], CHUNK):
        both = lax.dot_general(
            terms, scaled_ref[pl.ds(k, CHUNK)], (((1,), (1,)), ((), ())), preferred_element_type=jnp.float32
        )
        own_ref[:, pl.ds(k, CHUNK)] = both[:rows] + both[rows:]


def first_kernel(samples, width_ref, s0, s1, s2, s3, dosage_ref, start_ref, scaled_ref, own_ref, coded_ref):
    sums = total([s[0:2] for s in (s0, s1, s2, s3)])
    center = sums[0:1] / samples
    spread = sums[1:2] / samples - center * center
    factor = lax.rsqrt(spread + 1e-05)
    for k in range(0, dosage_ref.shape[0], CHUNK):
        part = dosage_ref[pl.ds(k, CHUNK)].astype(jnp.float32)
        scaled_ref[pl.ds(k, CHUNK)] = ((part - center) * factor).astype(jnp.bfloat16)
    project(start_ref[...], scaled_ref, own_ref)
    encode(own_ref, coded_ref, width_ref[0].astype(jnp.float32))


def next_kernel(
    samples, groups, width_ref, z0, z1, z2, z3, start_ref, scaled_ref, first_ref, parts_ref, own_ref, coded_ref
):
    first = total([z[...] for z in (z0, z1, z2, z3)]) / samples
    first_ref[...] = first
    start = start_ref[...]
    lane = lax.broadcasted_iota(jnp.int32, parts_ref.shape, 1)
    parts = jnp.zeros(parts_ref.shape, jnp.float32)
    for k, (a, b) in enumerate(((start, start), (start, first), (first, first))):
        parts = jnp.where(lane == k, jnp.sum(a * b, 1, keepdims=True) / groups, parts)
    parts_ref[...] = parts
    project(first, scaled_ref, own_ref)
    encode(own_ref, coded_ref, width_ref[0].astype(jnp.float32))


def place(count):
    index = lax.axis_index("snp")
    odd = (index & 1) == 1
    below, above = index >= 2, index < count - 2
    outer = jnp.where(odd, below.astype(jnp.int32), above.astype(jnp.int32)) == 1
    inner = jnp.where(odd, above.astype(jnp.int32), below.astype(jnp.int32)) == 1
    far = jnp.where(odd, (index < count - 3).astype(jnp.int32), (index >= 3).astype(jnp.int32)) == 1
    return odd, outer, inner, far


def gate(scale, odd, even_width, odd_width, least):
    return jnp.where(jnp.where(odd, odd_width, even_width) >= least, scale, 0.0)


def give_kernel(count, width_ref, near_ref, own_ref, outer_ref, inner_ref, give_ref):
    odd, use_outer, use_inner, _ = place(count)
    width = width_ref[0].astype(jnp.float32)
    near = near_ref[2:3, 0:1]
    outer_scale, outer_width = decode(outer_ref, use_outer)
    inner_scale, inner_width = decode(inner_ref, use_inner)
    own_scale = gate(1.0, odd, width, near, 1)
    outer_scale = gate(outer_scale, odd, near, outer_width, 1)
    inner_scale = gate(inner_scale, odd, inner_width, near, 3)
    for k in range(0, own_ref.shape[1], CHUNK):
        give_ref[:, pl.ds(k, CHUNK)] = (
            own_ref[:, pl.ds(k, CHUNK)] * own_scale
            + values(outer_ref, k) * outer_scale
            + values(inner_ref, k) * inner_scale
        )


def window_kernel(
    samples, count, width_ref, own_ref, outer_ref, inner_ref, far_ref, given_ref, scaled_ref, *refs
):
    odd, use_outer, use_inner, use_far = place(count)
    width = width_ref[0].astype(jnp.float32)
    outer_scale, outer_width = decode(outer_ref, use_outer)
    inner_scale, inner_width = decode(inner_ref, use_inner)
    far_scale, far_width = decode(far_ref, use_far)
    outer_scale = gate(outer_scale, odd, width, outer_width, 2)
    inner_scale = gate(inner_scale, odd, inner_width, width, 2)
    far_scale = gate(far_scale, odd, far_width, width, 3)
    out_ref = refs[-1]
    rows = own_ref.shape[0]
    acc = jnp.zeros((2 * rows, scaled_ref.shape[1]), jnp.float32)
    curved = jnp.zeros((rows, CHUNK), jnp.float32)
    for k in range(0, own_ref.shape[1], CHUNK):
        own = own_ref[:, pl.ds(k, CHUNK)]
        mixed = (
            own
            + given_ref[:, pl.ds(k, CHUNK)]
            + values(outer_ref, k) * outer_scale
            + values(inner_ref, k) * inner_scale
            + values(far_ref, k) * far_scale
        )
        acc = acc + jnp.dot(
            two_terms(mixed), scaled_ref[pl.ds(k, CHUNK)], preferred_element_type=jnp.float32
        )
        curved = curved + own * mixed
    out_ref[...] = acc[:rows] + acc[rows:]
    if len(refs) == 3:
        parts_ref, sums_ref = refs[:2]
        lane = lax.broadcasted_iota(jnp.int32, parts_ref.shape, 1)
        sums_ref[...] = jnp.where(lane == 3, jnp.sum(curved, 1, keepdims=True) / samples, parts_ref[...])


def last_kernel(samples, shrink_ref, p0, p1, p2, p3, z0, z1, z2, z3, start_ref, first_ref, effects_ref, residual_ref):
    parts = total([p[...] for p in (p0, p1, p2, p3)])
    bb, bw, ww, wu = (parts[:, k : k + 1] for k in range(4))
    shrink = shrink_ref[...]
    start, first = start_ref[...], first_ref[...]
    second = total([z[...] for z in (z0, z1, z2, z3)]) / samples
    ratio = bw / bb
    step = 1.0 / (ratio + shrink)
    norm = step * step * (ww - ratio * bw)
    bend = norm / bb
    curve = step * step * (ratio * (ratio * bw - 2.0 * ww) + wu) + shrink * norm - bend * norm / step
    step2 = jnp.where(curve > 0, norm / curve, 0.0)
    rest = step * (ratio * start - first)
    direction = rest + bend * start
    image = step * (ratio * first - second) + bend * first + shrink * direction
    effects_ref[...] = step * start + step2 * direction
    residual_ref[...] = rest - step2 * image


def shards(dosage, band_width, marginal, penalty):
    groups, count = lax.axis_size("samp"), lax.axis_size("snp")
    samples, size, rows = dosage.shape[0] * groups, dosage.shape[1], marginal.shape[1]
    local = dosage.shape[0]
    start = marginal.T
    shrink = penalty[:, None]
    grid, coded_shape, own_shape = (rows, size), (rows, local + AUX), (rows, local)

    (sums,) = call(stats_kernel, [((8, size), jnp.float32)], band_width, dosage, smem=(0,))
    others = partners(sums, "samp", 1, 2)
    near = swap(sums, "snp", 1)
    others, near = lax.optimization_barrier((others, near))
    scaled, own, coded = call(
        functools.partial(first_kernel, samples),
        [(dosage.shape, jnp.bfloat16), (own_shape, jnp.float32), (coded_shape, jnp.int16)],
        band_width, sums, *others, dosage, start, smem=(0,),
    )

    def window(own, coded, extra, outs):
        outer = crossing(coded, 1)
        inner = crossing(coded, 0)
        far = forward(outer)
        inner, far = lax.optimization_barrier((inner, far))
        (give,) = call(
            functools.partial(give_kernel, count),
            [(own_shape, jnp.float32)],
            band_width, near, own, outer, inner, smem=(0,),
        )
        given = swap(give, "snp", 1)
        return call(
            functools.partial(window_kernel, samples, count),
            outs,
            band_width, own, outer, inner, far, given, scaled, *extra, smem=(0,),
        )

    (z,) = window(own, coded, (), [(grid, jnp.float32)])
    first, parts, own, coded = call(
        functools.partial(next_kernel, samples, groups),
        [(grid, jnp.float32), ((rows, AUX), jnp.float32), (own_shape, jnp.float32), (coded_shape, jnp.int16)],
        band_width, z, *partners(z, "samp", 1, 2), start, scaled, smem=(0,),
    )
    sums, z = window(own, coded, (parts,), [((rows, AUX), jnp.float32), (grid, jnp.float32)])
    zs = [z, *partners(z, "samp", 1, 2)]
    sums = sums + swap(sums, "snp", 1)
    bit = 2
    while bit < count:
        if 2 * bit < count:
            sums = total([sums, *partners(sums, "snp", bit, 2 * bit)])
        else:
            sums = sums + swap(sums, "snp", bit)
        bit *= 4
    effects, residual = call(
        functools.partial(last_kernel, samples),
        [(grid, jnp.float32), (grid, jnp.float32)],
        shrink, sums, *partners(sums, "samp", 1, 2), *zs, start, first,
    )
    return (effects.T, residual.T)


def solution(mesh):
    in_specs = (P("samp", "snp"), P("snp"), P("snp", None), P())
    out_specs = (P("snp", None), P("snp", None))
    return jax.shard_map(shards, mesh=mesh, in_specs=in_specs, out_specs=out_specs, check_vma=False)
```

```python
import functools

import jax
import jax.numpy as jnp
from jax import lax
from jax.experimental import pallas as pl
from jax.experimental.pallas import tpu as pltpu
from jax.sharding import PartitionSpec as P


AUX = 128
CHUNK = 512
UNIT = 14
ROWS = 128


def swap(value, axis, bits):
    return lax.ppermute(value, axis, [(i, i ^ bits) for i in range(lax.axis_size(axis))])


def crossing(value, rising):
    count = lax.axis_size("snp")
    pairs = []
    for i in range(count):
        target = i + 2 if i % 2 == rising else i - 2
        pairs.append((i, target if 0 <= target < count else i ^ 1))
    return lax.ppermute(value, "snp", pairs)


def distant(value):
    count = lax.axis_size("snp")
    both = [(i, i + 3) for i in range(1, count - 3, 2)] + [(0, 2), (count - 3, count - 1)]
    return lax.ppermute(value, "snp", both + [(j, i) for i, j in both])


def shifted(value):
    count = lax.axis_size("snp")
    return lax.ppermute(value, "snp", [(i, (i + 2) % count) for i in range(count)])


def partners(value, axis, low, high):
    return [swap(value, axis, k) for k in (low, high, low + high)]


def total(parts):
    own, one, two, three = parts
    return (own + one) + (two + three)


def call(body, out_shape, *args):
    specs = [pl.BlockSpec(memory_space=pltpu.VMEM) for _ in args]
    outs = [jax.ShapeDtypeStruct(shape, kind) for shape, kind in out_shape]
    return pl.pallas_call(
        body,
        out_shape=outs,
        in_specs=specs,
        out_specs=[pl.BlockSpec(memory_space=pltpu.VMEM) for _ in outs],
        compiler_params=pltpu.CompilerParams(vmem_limit_bytes=32 << 20),
    )(*args)


def two_terms(value):
    high = value.astype(jnp.bfloat16)
    low = (value - high.astype(jnp.float32)).astype(jnp.bfloat16)
    return jnp.concatenate([high, low], 0)


def stats_kernel(width_ref, dosage_ref, sums_ref):
    acc = jnp.zeros((8, dosage_ref.shape[1]), jnp.float32)
    square = acc
    for k in range(0, dosage_ref.shape[0], ROWS):
        part = dosage_ref[pl.ds(k, ROWS)].astype(jnp.float32)
        part = part.reshape(ROWS // 8, 8, part.shape[1])
        acc = acc + jnp.sum(part, 0)
        square = square + jnp.sum(part * part, 0)
    row = lax.broadcasted_iota(jnp.int32, (8, 1), 0)
    first = jnp.sum(acc, 0, keepdims=True)
    second = jnp.sum(square, 0, keepdims=True)
    width = width_ref[...].astype(jnp.float32).reshape(1, 1)
    sums_ref[...] = jnp.where(row == 0, first, jnp.where(row == 1, second, width))


def finish(coded_ref, exponent, width):
    lane = lax.broadcasted_iota(jnp.int32, (coded_ref.shape[0], AUX), 1)
    extra = jnp.where(lane == 0, exponent, jnp.where(lane == 1, width, 0.0))
    coded_ref[:, pl.ds(coded_ref.shape[1] - AUX, AUX)] = extra.astype(jnp.int32).astype(jnp.int16)


def fixed(value):
    return jnp.clip(jnp.round(value), -32767.0, 32767.0).astype(jnp.int32).astype(jnp.int16)


def encode(own_ref, coded_ref, width):
    peak = jnp.max(jnp.abs(own_ref[...]), 1, keepdims=True)
    exponent = jnp.floor(jnp.log2(jnp.maximum(peak, 1e-30)))
    scale = jnp.exp2(UNIT - exponent)
    for k in range(0, own_ref.shape[1], CHUNK):
        coded_ref[:, pl.ds(k, CHUNK)] = fixed(own_ref[:, pl.ds(k, CHUNK)] * scale)
    finish(coded_ref, exponent, width)


def aux(coded_ref):
    extra = coded_ref[:, pl.ds(coded_ref.shape[1] - AUX, AUX)].astype(jnp.int32).astype(jnp.float32)
    return extra[:, :1], extra[:, 1:2]


def unit(exponent, use):
    return jnp.where(use, jnp.exp2(exponent - UNIT), 0.0)


def values(coded_ref, k):
    return coded_ref[:, pl.ds(k, CHUNK)].astype(jnp.int32).astype(jnp.float32)


def project(value, scaled_ref, own_ref):
    rows = value.shape[0]
    terms = two_terms(value)
    for k in range(0, scaled_ref.shape[0], CHUNK):
        both = lax.dot_general(
            terms, scaled_ref[pl.ds(k, CHUNK)], (((1,), (1,)), ((), ())), preferred_element_type=jnp.float32
        )
        own_ref[:, pl.ds(k, CHUNK)] = both[:rows] + both[rows:]


def first_kernel(samples, s0, s1, s2, s3, dosage_ref, start_ref, scaled_ref, own_ref, coded_ref):
    sums = total([s[0:2] for s in (s0, s1, s2, s3)])
    width = s0[2:3, 0:1]
    center = sums[0:1] / samples
    spread = sums[1:2] / samples - center * center
    factor = lax.rsqrt(spread + 1e-05)
    for k in range(0, dosage_ref.shape[0], CHUNK):
        part = dosage_ref[pl.ds(k, CHUNK)].astype(jnp.float32)
        scaled_ref[pl.ds(k, CHUNK)] = ((part - center) * factor).astype(jnp.bfloat16)
    project(start_ref[...], scaled_ref, own_ref)
    encode(own_ref, coded_ref, width)


def next_kernel(
    samples, groups, sums_ref, z0, z1, z2, z3, start_ref, scaled_ref, first_ref, parts_ref, own_ref, coded_ref
):
    first = total([z[...] for z in (z0, z1, z2, z3)]) / samples
    first_ref[...] = first
    start = start_ref[...]
    lane = lax.broadcasted_iota(jnp.int32, parts_ref.shape, 1)
    parts = jnp.zeros(parts_ref.shape, jnp.float32)
    for k, (a, b) in enumerate(((start, start), (start, first), (first, first))):
        parts = jnp.where(lane == k, jnp.sum(a * b, 1, keepdims=True) / groups, parts)
    parts_ref[...] = parts
    project(first, scaled_ref, own_ref)
    encode(own_ref, coded_ref, sums_ref[2:3, 0:1])


def place(count):
    index = lax.axis_index("snp")
    odd = (index & 1) == 1
    below, above = (index >= 2).astype(jnp.int32), (index < count - 2).astype(jnp.int32)
    outer = jnp.where(odd, below, above) == 1
    inner = jnp.where(odd, above, below) == 1
    far = jnp.where(odd, (index < count - 3).astype(jnp.int32), (index >= 3).astype(jnp.int32)) == 1
    return odd, outer, inner, far


def give_kernel(count, near_ref, own_ref, coded_ref, partner_ref, outer_ref, inner_ref):
    odd = place(count)[0]
    exponent, width = aux(coded_ref)
    partner_exponent, partner_width = aux(partner_ref)
    near = near_ref[2:3, 0:1]
    sent = jnp.maximum(exponent, partner_exponent) + 1.0
    scale = jnp.exp2(UNIT - sent)
    partner_scale = scale * jnp.exp2(partner_exponent - UNIT)
    flag = lambda value, least: (value >= least).astype(jnp.float32)
    up_own = flag(width, 2.0) * scale
    up_partner = flag(partner_width, jnp.where(odd, 3.0, 1.0)) * partner_scale
    down_own = flag(near, 2.0) * scale
    down_partner = flag(near, jnp.where(odd, 1.0, 3.0)) * partner_scale
    choose = lambda even_case, odd_case: jnp.where(odd, odd_case, even_case)
    outer_own, outer_partner = choose(down_own, up_own), choose(down_partner, up_partner)
    inner_own, inner_partner = choose(up_own, down_own), choose(up_partner, down_partner)
    for k in range(0, own_ref.shape[1], CHUNK):
        own, partner = own_ref[:, pl.ds(k, CHUNK)], values(partner_ref, k)
        outer_ref[:, pl.ds(k, CHUNK)] = fixed(own * outer_own + partner * outer_partner)
        inner_ref[:, pl.ds(k, CHUNK)] = fixed(own * inner_own + partner * inner_partner)
    finish(outer_ref, sent, width)
    finish(inner_ref, sent, width)


def window_kernel(samples, count, own_ref, coded_ref, partner_ref, outer_ref, inner_ref, far_ref, scaled_ref, *refs):
    odd, use_outer, use_inner, use_far = place(count)
    _, width = aux(coded_ref)
    partner_exponent, partner_width = aux(partner_ref)
    far_exponent, far_width = aux(far_ref)
    partner_scale = unit(partner_exponent, jnp.where(odd, partner_width, width) >= 1)
    outer_scale = unit(aux(outer_ref)[0], use_outer)
    inner_scale = unit(aux(inner_ref)[0], use_inner)
    far_scale = jnp.where(jnp.where(odd, width, far_width) >= 3, unit(far_exponent, use_far), 0.0)
    out_ref = refs[-1]
    rows = own_ref.shape[0]
    acc = jnp.zeros((2 * rows, scaled_ref.shape[1]), jnp.float32)
    curved = jnp.zeros((rows, CHUNK), jnp.float32)
    for k in range(0, own_ref.shape[1], CHUNK):
        own = own_ref[:, pl.ds(k, CHUNK)]
        mixed = (
            own
            + values(partner_ref, k) * partner_scale
            + values(outer_ref, k) * outer_scale
            + values(inner_ref, k) * inner_scale
            + values(far_ref, k) * far_scale
        )
        acc = acc + jnp.dot(
            two_terms(mixed), scaled_ref[pl.ds(k, CHUNK)], preferred_element_type=jnp.float32
        )
        curved = curved + own * mixed
    out_ref[...] = acc[:rows] + acc[rows:]
    if len(refs) == 3:
        parts_ref, sums_ref = refs[:2]
        lane = lax.broadcasted_iota(jnp.int32, parts_ref.shape, 1)
        sums = jnp.where(lane == 3, jnp.sum(curved, 1, keepdims=True) / samples, parts_ref[...])
        filled = jnp.concatenate([sums, jnp.zeros((AUX - rows, AUX), jnp.float32)], 0)
        sums_ref[...] = filled.T[:8]


def last_kernel(samples, shrink_ref, p0, p1, p2, p3, z0, z1, start_ref, first_ref, effects_ref, residual_ref):
    rows = shrink_ref.shape[0]
    flat = total([p[...] for p in (p0, p1, p2, p3)])
    parts = jnp.concatenate([flat, jnp.zeros((AUX - 8, AUX), jnp.float32)], 0).T[:rows]
    bb, bw, ww, wu = (parts[:, k : k + 1] for k in range(4))
    shrink = shrink_ref[...]
    start, first = start_ref[...], first_ref[...]
    second = (z0[...] + z1[...]) / samples
    ratio = bw / bb
    step = 1.0 / (ratio + shrink)
    norm = step * step * (ww - ratio * bw)
    bend = norm / bb
    curve = step * step * (ratio * (ratio * bw - 2.0 * ww) + wu) + shrink * norm - bend * norm / step
    step2 = jnp.where(curve > 0, norm / curve, 0.0)
    rest = step * (ratio * start - first)
    direction = rest + bend * start
    image = step * (ratio * first - second) + bend * first + shrink * direction
    effects_ref[...] = step * start + step2 * direction
    residual_ref[...] = rest - step2 * image


def snp_sum(value):
    count = lax.axis_size("snp")
    value = value + swap(value, "snp", 1)
    bit = 2
    while bit < count:
        if 2 * bit < count:
            value = total([value, *partners(value, "snp", bit, 2 * bit)])
        else:
            value = value + swap(value, "snp", bit)
        bit *= 4
    return value


def shards(dosage, band_width, marginal, penalty):
    groups, count = lax.axis_size("samp"), lax.axis_size("snp")
    local, size, rows = dosage.shape[0], dosage.shape[1], marginal.shape[1]
    samples = local * groups
    start = marginal.T
    shrink = penalty[:, None]
    grid, own_shape, flat = (rows, size), (rows, local), (8, AUX)
    coded_out = ((rows, local + AUX), jnp.int16)

    (sums,) = call(stats_kernel, [((8, size), jnp.float32)], band_width, dosage)
    others = partners(sums, "samp", 1, 2)
    near = shifted(sums)
    others, near = lax.optimization_barrier((others, near))
    scaled, own, coded = call(
        functools.partial(first_kernel, samples),
        [(dosage.shape, jnp.bfloat16), (own_shape, jnp.float32), coded_out],
        sums, *others, dosage, start,
    )

    def window(own, coded, extra, outs):
        far = distant(coded)
        partner = swap(coded, "snp", 1)
        outer, inner = call(
            functools.partial(give_kernel, count), [coded_out, coded_out], near, own, coded, partner
        )
        return call(
            functools.partial(window_kernel, samples, count), outs,
            own, coded, partner, crossing(outer, 1), crossing(inner, 0), far, scaled, *extra,
        )

    (z,) = window(own, coded, (), [(grid, jnp.float32)])
    first, parts, own, coded = call(
        functools.partial(next_kernel, samples, groups),
        [(grid, jnp.float32), ((rows, AUX), jnp.float32), (own_shape, jnp.float32), coded_out],
        sums, z, *partners(z, "samp", 1, 2), start, scaled,
    )
    parts, z = window(own, coded, (parts,), [(flat, jnp.float32), (grid, jnp.float32)])
    z = z + swap(z, "samp", 1)
    z, parts = lax.optimization_barrier((z, snp_sum(parts)))
    effects, residual = call(
        functools.partial(last_kernel, samples),
        [(grid, jnp.float32), (grid, jnp.float32)],
        shrink, parts, *partners(parts, "samp", 1, 2), z, swap(z, "samp", 2), start, first,
    )
    return (effects.T, residual.T)


def solution(mesh):
    in_specs = (P("samp", "snp"), P("snp"), P("snp", None), P())
    out_specs = (P("snp", None), P("snp", None))
    return jax.shard_map(shards, mesh=mesh, in_specs=in_specs, out_specs=out_specs, check_vma=False)
```

```python
import functools

import jax
import jax.numpy as jnp
from jax import lax
from jax.experimental import pallas as pl
from jax.experimental.pallas import tpu as pltpu
from jax.sharding import PartitionSpec as P


AUX = 128
CHUNK = 512
UNIT = 14
ROWS = 128


def swap(value, axis, bits):
    return lax.ppermute(value, axis, [(i, i ^ bits) for i in range(lax.axis_size(axis))])


def crossing(value, rising):
    count = lax.axis_size("snp")
    pairs = []
    for i in range(count):
        target = i + 2 if i % 2 == rising else i - 2
        pairs.append((i, target if 0 <= target < count else i ^ 1))
    return lax.ppermute(value, "snp", pairs)


def distant(value):
    count = lax.axis_size("snp")
    both = [(i, i + 3) for i in range(1, count - 3, 2)] + [(0, 2), (count - 3, count - 1)]
    return lax.ppermute(value, "snp", both + [(j, i) for i, j in both])


def shifted(value):
    count = lax.axis_size("snp")
    return lax.ppermute(value, "snp", [(i, (i + 2) % count) for i in range(count)])


def partners(value, axis, low, high):
    return [swap(value, axis, k) for k in (low, high, low + high)]


def total(parts):
    own, one, two, three = parts
    return (own + one) + (two + three)


def call(body, out_shape, *args):
    specs = [pl.BlockSpec(memory_space=pltpu.VMEM) for _ in args]
    outs = [jax.ShapeDtypeStruct(shape, kind) for shape, kind in out_shape]
    return pl.pallas_call(
        body,
        out_shape=outs,
        in_specs=specs,
        out_specs=[pl.BlockSpec(memory_space=pltpu.VMEM) for _ in outs],
        compiler_params=pltpu.CompilerParams(vmem_limit_bytes=32 << 20),
    )(*args)


def two_terms(value):
    high = value.astype(jnp.bfloat16)
    low = (value - high.astype(jnp.float32)).astype(jnp.bfloat16)
    return jnp.concatenate([high, low], 0)


def stats_kernel(dosage_ref, sums_ref):
    acc = jnp.zeros((8, dosage_ref.shape[1]), jnp.float32)
    square = acc
    for k in range(0, dosage_ref.shape[0], ROWS):
        part = dosage_ref[pl.ds(k, ROWS)].astype(jnp.float32)
        part = part.reshape(ROWS // 8, 8, part.shape[1])
        acc = acc + jnp.sum(part, 0)
        square = square + jnp.sum(part * part, 0)
    row = lax.broadcasted_iota(jnp.int32, (8, 1), 0)
    first = jnp.sum(acc, 0, keepdims=True)
    second = jnp.sum(square, 0, keepdims=True)
    sums_ref[...] = jnp.where(row == 0, first, second)


def finish(coded_ref, *columns):
    lane = lax.broadcasted_iota(jnp.int32, (coded_ref.shape[0], AUX), 1)
    extra = jnp.zeros(lane.shape, jnp.float32)
    for k, column in enumerate(columns):
        extra = jnp.where(lane == k, column, extra)
    coded_ref[:, pl.ds(coded_ref.shape[1] - AUX, AUX)] = extra.astype(jnp.int32).astype(jnp.int16)


def fixed(value):
    return jnp.clip(jnp.round(value), -32767.0, 32767.0).astype(jnp.int32).astype(jnp.int16)


def scale_of(peak):
    exponent = jnp.floor(jnp.log2(jnp.maximum(peak, 1e-30)))
    return exponent, jnp.exp2(UNIT - exponent)


def encode(own_ref, coded_ref, width):
    exponent, scale = scale_of(jnp.max(jnp.abs(own_ref[...]), 1, keepdims=True))
    for k in range(0, own_ref.shape[1], CHUNK):
        coded_ref[:, pl.ds(k, CHUNK)] = fixed(own_ref[:, pl.ds(k, CHUNK)] * scale)
    finish(coded_ref, exponent, width)


def split(value):
    exponent, scale = scale_of(jnp.abs(value))
    high = jnp.round(value * scale * 0.5)
    low = jnp.round((value * scale * 0.5 - high) * 2.0**UNIT)
    return exponent, high, low


def aux(coded_ref):
    extra = coded_ref[:, pl.ds(coded_ref.shape[1] - AUX, AUX)].astype(jnp.int32).astype(jnp.float32)
    return [extra[:, k : k + 1] for k in range(4)]


def unit(exponent, use=True):
    return jnp.where(use, jnp.exp2(exponent - UNIT), 0.0)


def grid_values(coded_ref):
    size = coded_ref.shape[1] - AUX
    return coded_ref[:, pl.ds(0, size)].astype(jnp.int32).astype(jnp.float32) * unit(aux(coded_ref)[0])


def values(coded_ref, k):
    return coded_ref[:, pl.ds(k, CHUNK)].astype(jnp.int32).astype(jnp.float32)


def project(value, scaled_ref, own_ref):
    rows = value.shape[0]
    terms = two_terms(value)
    for k in range(0, scaled_ref.shape[0], CHUNK):
        both = lax.dot_general(
            terms, scaled_ref[pl.ds(k, CHUNK)], (((1,), (1,)), ((), ())), preferred_element_type=jnp.float32
        )
        own_ref[:, pl.ds(k, CHUNK)] = both[:rows] + both[rows:]


def first_kernel(samples, wide_ref, s0, s1, s2, s3, dosage_ref, start_ref, scaled_ref, own_ref, coded_ref):
    sums = total([s[0:2] for s in (s0, s1, s2, s3)])
    center = sums[0:1] / samples
    spread = sums[1:2] / samples - center * center
    factor = lax.rsqrt(spread + 1e-05)
    for k in range(0, dosage_ref.shape[0], CHUNK):
        part = dosage_ref[pl.ds(k, CHUNK)].astype(jnp.float32)
        scaled_ref[pl.ds(k, CHUNK)] = ((part - center) * factor).astype(jnp.bfloat16)
    project(start_ref[...], scaled_ref, own_ref)
    encode(own_ref, coded_ref, wide_ref[0:1, 0:1])


def next_kernel(
    samples, wide_ref, z0, z1, z2, z3, start_ref, scaled_ref, first_ref, parts_ref, own_ref, coded_ref
):
    first = total([grid_values(z) for z in (z0, z1, z2, z3)]) / samples
    first_ref[...] = first
    start = start_ref[...]
    lane = lax.broadcasted_iota(jnp.int32, parts_ref.shape, 1)
    parts = jnp.zeros(parts_ref.shape, jnp.float32)
    for k, (a, b) in enumerate(((start, start), (start, first), (first, first))):
        parts = jnp.where(lane == k, jnp.sum(a * b, 1, keepdims=True), parts)
    parts_ref[...] = parts
    project(first, scaled_ref, own_ref)
    encode(own_ref, coded_ref, wide_ref[0:1, 0:1])


def place(count):
    index = lax.axis_index("snp")
    odd = (index & 1) == 1
    below, above = (index >= 2).astype(jnp.int32), (index < count - 2).astype(jnp.int32)
    outer = jnp.where(odd, below, above) == 1
    inner = jnp.where(odd, above, below) == 1
    far = jnp.where(odd, (index < count - 3).astype(jnp.int32), (index >= 3).astype(jnp.int32)) == 1
    return odd, outer, inner, far


def give_kernel(count, near_ref, own_ref, coded_ref, partner_ref, outer_ref, inner_ref):
    odd = place(count)[0]
    exponent, width = aux(coded_ref)[:2]
    partner_exponent, partner_width = aux(partner_ref)[:2]
    near = near_ref[0:1, 0:1]
    sent = jnp.maximum(exponent, partner_exponent) + 1.0
    scale = jnp.exp2(UNIT - sent)
    partner_scale = scale * jnp.exp2(partner_exponent - UNIT)
    flag = lambda value, least: (value >= least).astype(jnp.float32)
    up_own = flag(width, 2.0) * scale
    up_partner = flag(partner_width, jnp.where(odd, 3.0, 1.0)) * partner_scale
    down_own = flag(near, 2.0) * scale
    down_partner = flag(near, jnp.where(odd, 1.0, 3.0)) * partner_scale
    choose = lambda even_case, odd_case: jnp.where(odd, odd_case, even_case)
    outer_own, outer_partner = choose(down_own, up_own), choose(down_partner, up_partner)
    inner_own, inner_partner = choose(up_own, down_own), choose(up_partner, down_partner)
    for k in range(0, own_ref.shape[1], CHUNK):
        own, partner = own_ref[:, pl.ds(k, CHUNK)], values(partner_ref, k)
        outer_ref[:, pl.ds(k, CHUNK)] = fixed(own * outer_own + partner * outer_partner)
        inner_ref[:, pl.ds(k, CHUNK)] = fixed(own * inner_own + partner * inner_partner)
    finish(outer_ref, sent, width)
    finish(inner_ref, sent, width)


def window_kernel(samples, count, own_ref, coded_ref, partner_ref, outer_ref, inner_ref, far_ref, scaled_ref, sent_ref):
    odd, use_outer, use_inner, use_far = place(count)
    width = aux(coded_ref)[1]
    partner_exponent, partner_width = aux(partner_ref)[:2]
    far_exponent, far_width = aux(far_ref)[:2]
    partner_scale = unit(partner_exponent, jnp.where(odd, partner_width, width) >= 1)
    outer_scale = unit(aux(outer_ref)[0], use_outer)
    inner_scale = unit(aux(inner_ref)[0], use_inner)
    far_scale = jnp.where(jnp.where(odd, width, far_width) >= 3, unit(far_exponent, use_far), 0.0)
    rows = own_ref.shape[0]
    acc = jnp.zeros((2 * rows, scaled_ref.shape[1]), jnp.float32)
    curved = jnp.zeros((rows, CHUNK), jnp.float32)
    for k in range(0, own_ref.shape[1], CHUNK):
        own = own_ref[:, pl.ds(k, CHUNK)]
        mixed = (
            own
            + values(partner_ref, k) * partner_scale
            + values(outer_ref, k) * outer_scale
            + values(inner_ref, k) * inner_scale
            + values(far_ref, k) * far_scale
        )
        acc = acc + jnp.dot(
            two_terms(mixed), scaled_ref[pl.ds(k, CHUNK)], preferred_element_type=jnp.float32
        )
        curved = curved + own * mixed
    z = acc[:rows] + acc[rows:]
    exponent, scale = scale_of(jnp.max(jnp.abs(z), 1, keepdims=True))
    sent_ref[:, pl.ds(0, z.shape[1])] = fixed(z * scale)
    finish(sent_ref, exponent, *split(jnp.sum(curved, 1, keepdims=True) / samples))


def collect_kernel(parts_ref, z0, z1, z2, z3, flat_ref):
    terms = []
    for z in (z0, z1, z2, z3):
        _, exponent, high, low = aux(z)
        terms.append((high + low * 2.0**-UNIT) * 2.0 * unit(exponent))
    lane = lax.broadcasted_iota(jnp.int32, parts_ref.shape, 1)
    parts = jnp.where(lane == 3, total(terms), parts_ref[...])
    filled = jnp.concatenate([parts, jnp.zeros((AUX - parts.shape[0], AUX), jnp.float32)], 0)
    flat_ref[...] = filled.T[:8]


def last_kernel(samples, shrink_ref, p0, p1, p2, p3, z0, z1, z2, z3, start_ref, first_ref, effects_ref, residual_ref):
    rows = shrink_ref.shape[0]
    flat = total([p[...] for p in (p0, p1, p2, p3)])
    parts = jnp.concatenate([flat, jnp.zeros((AUX - 8, AUX), jnp.float32)], 0).T[:rows]
    bb, bw, ww, wu = (parts[:, k : k + 1] for k in range(4))
    shrink = shrink_ref[...]
    start, first = start_ref[...], first_ref[...]
    second = total([grid_values(z) for z in (z0, z1, z2, z3)]) / samples
    ratio = bw / bb
    step = 1.0 / (ratio + shrink)
    norm = step * step * (ww - ratio * bw)
    bend = norm / bb
    curve = step * step * (ratio * (ratio * bw - 2.0 * ww) + wu) + shrink * norm - bend * norm / step
    step2 = jnp.where(curve > 0, norm / curve, 0.0)
    rest = step * (ratio * start - first)
    direction = rest + bend * start
    image = step * (ratio * first - second) + bend * first + shrink * direction
    effects_ref[...] = step * start + step2 * direction
    residual_ref[...] = rest - step2 * image


def snp_parts(value):
    count = lax.axis_size("snp")
    value = value + swap(value, "snp", 1)
    bit = 2
    while 4 * bit < count:
        value = total([value, *partners(value, "snp", bit, 2 * bit)])
        bit *= 4
    if 2 * bit < count:
        return [value, *partners(value, "snp", bit, 2 * bit)]
    return [value, swap(value, "snp", bit), jnp.zeros_like(value), jnp.zeros_like(value)]


def shards(dosage, band_width, marginal, penalty):
    groups, count = lax.axis_size("samp"), lax.axis_size("snp")
    local, size, rows = dosage.shape[0], dosage.shape[1], marginal.shape[1]
    samples = local * groups
    start = marginal.T
    shrink = penalty[:, None]
    grid, own_shape = (rows, size), (rows, local)
    own_out, coded_out = (own_shape, jnp.float32), ((rows, local + AUX), jnp.int16)

    sent_out = ((rows, size + AUX), jnp.int16)

    (sums,) = call(stats_kernel, [((8, size), jnp.float32)], dosage)
    one, two, three = partners(sums, "samp", 1, 2)
    one, band_width = lax.optimization_barrier((one, band_width))
    wide = jnp.broadcast_to(band_width.astype(jnp.float32)[:, None], (8, AUX))
    near = shifted(wide)
    two, three, near = lax.optimization_barrier((two, three, near))
    scaled, own, coded = call(
        functools.partial(first_kernel, samples),
        [(dosage.shape, jnp.bfloat16), own_out, coded_out],
        wide, sums, one, two, three, dosage, start,
    )

    def window(own, coded):
        far = distant(coded)
        partner = swap(coded, "snp", 1)
        outer, inner = call(
            functools.partial(give_kernel, count), [coded_out, coded_out], near, own, coded, partner
        )
        (z,) = call(
            functools.partial(window_kernel, samples, count), [sent_out],
            own, coded, partner, crossing(outer, 1), crossing(inner, 0), far, scaled,
        )
        return [z, *partners(z, "samp", 1, 2)]

    first, parts, own, coded = call(
        functools.partial(next_kernel, samples),
        [(grid, jnp.float32), ((rows, AUX), jnp.float32), own_out, coded_out],
        wide, *window(own, coded), start, scaled,
    )
    zs = window(own, coded)
    (flat,) = call(collect_kernel, [((8, AUX), jnp.float32)], parts, *zs)
    parts = snp_parts(flat)
    effects, residual = call(
        functools.partial(last_kernel, samples),
        [(grid, jnp.float32), (grid, jnp.float32)],
        shrink, *parts, *zs, start, first,
    )
    return (effects.T, residual.T)


def solution(mesh):
    in_specs = (P("samp", "snp"), P("snp"), P("snp", None), P())
    out_specs = (P("snp", None), P("snp", None))
    return jax.shard_map(shards, mesh=mesh, in_specs=in_specs, out_specs=out_specs, check_vma=False)
```

```python
import functools

import jax
import jax.numpy as jnp
from jax import lax
from jax.experimental import pallas as pl
from jax.experimental.pallas import tpu as pltpu
from jax.sharding import PartitionSpec as P


AUX = 128
CHUNK = 512
UNIT = 14
ROWS = 128


def swap(value, axis, bits):
    return lax.ppermute(value, axis, [(i, i ^ bits) for i in range(lax.axis_size(axis))])


def between(value, offset):
    count = lax.axis_size("snp")
    pairs = []
    for i in range(count):
        target = ((i // 2 + offset ^ 1) - offset) * 2 + i % 2
        pairs.append((i, target if 0 <= target < count else i ^ 1))
    return lax.ppermute(value, "snp", pairs)


def distant(value):
    rows, count = lax.axis_size("samp"), lax.axis_size("snp")
    pairs = []
    for row in range(rows):
        for i in range(count):
            target = i + 3 if i % 2 else i - 3
            inside = 0 <= target < count
            pairs.append((row * count + i, row * count + target if inside else (row ^ 1) * count + i))
    return lax.ppermute(value, ("samp", "snp"), pairs)


def shifted(value):
    count = lax.axis_size("snp")
    return lax.ppermute(value, "snp", [(i, (i + 2) % count) for i in range(count)])


def partners(value, axis, low, high):
    return [swap(value, axis, k) for k in (low, high, low + high)]


def total(parts):
    own, one, two, three = parts
    return (own + one) + (two + three)


def call(body, out_shape, *args):
    specs = [pl.BlockSpec(memory_space=pltpu.VMEM) for _ in args]
    outs = [jax.ShapeDtypeStruct(shape, kind) for shape, kind in out_shape]
    return pl.pallas_call(
        body,
        out_shape=outs,
        in_specs=specs,
        out_specs=[pl.BlockSpec(memory_space=pltpu.VMEM) for _ in outs],
        compiler_params=pltpu.CompilerParams(vmem_limit_bytes=32 << 20),
    )(*args)


def two_terms(value):
    high = value.astype(jnp.bfloat16)
    low = (value - high.astype(jnp.float32)).astype(jnp.bfloat16)
    return jnp.concatenate([high, low], 0)


def stats_kernel(dosage_ref, sums_ref):
    acc = jnp.zeros((8, dosage_ref.shape[1]), jnp.float32)
    square = acc
    for k in range(0, dosage_ref.shape[0], ROWS):
        part = dosage_ref[pl.ds(k, ROWS)].astype(jnp.float32)
        part = part.reshape(ROWS // 8, 8, part.shape[1])
        acc = acc + jnp.sum(part, 0)
        square = square + jnp.sum(part * part, 0)
    row = lax.broadcasted_iota(jnp.int32, (8, 1), 0)
    first = jnp.sum(acc, 0, keepdims=True)
    second = jnp.sum(square, 0, keepdims=True)
    sums_ref[...] = jnp.where(row == 0, first, second)


def finish(coded_ref, *columns):
    lane = lax.broadcasted_iota(jnp.int32, (coded_ref.shape[0], AUX), 1)
    extra = jnp.zeros(lane.shape, jnp.float32)
    for k, column in enumerate(columns):
        extra = jnp.where(lane == k, column, extra)
    coded_ref[:, pl.ds(coded_ref.shape[1] - AUX, AUX)] = extra.astype(jnp.int32).astype(jnp.int16)


def fixed(value):
    return jnp.clip(jnp.round(value), -32767.0, 32767.0).astype(jnp.int32).astype(jnp.int16)


def scale_of(peak):
    exponent = jnp.floor(jnp.log2(jnp.maximum(peak, 1e-30)))
    return exponent, jnp.exp2(UNIT - exponent)


def encode(own_ref, coded_ref, width):
    exponent, scale = scale_of(jnp.max(jnp.abs(own_ref[...]), 1, keepdims=True))
    for k in range(0, own_ref.shape[1], CHUNK):
        coded_ref[:, pl.ds(k, CHUNK)] = fixed(own_ref[:, pl.ds(k, CHUNK)] * scale)
    finish(coded_ref, exponent, width)


def split(value):
    exponent, scale = scale_of(jnp.abs(value))
    high = jnp.round(value * scale * 0.5)
    low = jnp.round((value * scale * 0.5 - high) * 2.0**UNIT)
    return exponent, high, low


def aux(coded_ref):
    extra = coded_ref[:, pl.ds(coded_ref.shape[1] - AUX, AUX)].astype(jnp.int32).astype(jnp.float32)
    return [extra[:, k : k + 1] for k in range(4)]


def unit(exponent, use=True):
    return jnp.where(use, jnp.exp2(exponent - UNIT), 0.0)


def grid_values(coded_ref):
    size = coded_ref.shape[1] - AUX
    return coded_ref[:, pl.ds(0, size)].astype(jnp.int32).astype(jnp.float32) * unit(aux(coded_ref)[0])


def values(coded_ref, k):
    return coded_ref[:, pl.ds(k, CHUNK)].astype(jnp.int32).astype(jnp.float32)


def project(value, scaled_ref, own_ref):
    rows = value.shape[0]
    terms = two_terms(value)
    for k in range(0, scaled_ref.shape[0], CHUNK):
        both = lax.dot_general(
            terms, scaled_ref[pl.ds(k, CHUNK)], (((1,), (1,)), ((), ())), preferred_element_type=jnp.float32
        )
        own_ref[:, pl.ds(k, CHUNK)] = both[:rows] + both[rows:]


def first_kernel(samples, wide_ref, s0, s1, s2, s3, dosage_ref, start_ref, scaled_ref, own_ref, coded_ref):
    sums = total([s[0:2] for s in (s0, s1, s2, s3)])
    center = sums[0:1] / samples
    spread = sums[1:2] / samples - center * center
    factor = lax.rsqrt(spread + 1e-05)
    for k in range(0, dosage_ref.shape[0], CHUNK):
        part = dosage_ref[pl.ds(k, CHUNK)].astype(jnp.float32)
        scaled_ref[pl.ds(k, CHUNK)] = ((part - center) * factor).astype(jnp.bfloat16)
    project(start_ref[...], scaled_ref, own_ref)
    encode(own_ref, coded_ref, wide_ref[0:1, 0:1])


def next_kernel(
    samples, wide_ref, z0, z1, z2, z3, start_ref, scaled_ref, first_ref, parts_ref, own_ref, coded_ref
):
    first = total([grid_values(z) for z in (z0, z1, z2, z3)]) / samples
    first_ref[...] = first
    start = start_ref[...]
    lane = lax.broadcasted_iota(jnp.int32, parts_ref.shape, 1)
    parts = jnp.zeros(parts_ref.shape, jnp.float32)
    for k, (a, b) in enumerate(((start, start), (start, first), (first, first))):
        parts = jnp.where(lane == k, jnp.sum(a * b, 1, keepdims=True), parts)
    parts_ref[...] = parts
    project(first, scaled_ref, own_ref)
    encode(own_ref, coded_ref, wide_ref[0:1, 0:1])


def place(count):
    index = lax.axis_index("snp")
    odd, pair = (index & 1) == 1, index >> 1
    rises = (pair & 1) == 0
    above, below = (pair < count // 2 - 1).astype(jnp.int32), (pair > 0).astype(jnp.int32)
    first = jnp.where(rises, above, below) == 1
    second = jnp.where(rises, below, above) == 1
    far = jnp.where(odd, (index < count - 3).astype(jnp.int32), (index >= 3).astype(jnp.int32)) == 1
    return odd, rises, first, second, far


def give_kernel(count, near_ref, own_ref, coded_ref, partner_ref, first_ref, second_ref):
    odd, rises = place(count)[:2]
    exponent, width = aux(coded_ref)[:2]
    partner_exponent, partner_width = aux(partner_ref)[:2]
    near = near_ref[0:1, 0:1]
    sent = jnp.maximum(exponent, partner_exponent) + 1.0
    scale = jnp.exp2(UNIT - sent)
    partner_scale = scale * jnp.exp2(partner_exponent - UNIT)
    flag = lambda value, least: (value >= least).astype(jnp.float32)
    up_own = flag(width, 2.0) * scale
    up_partner = flag(partner_width, jnp.where(odd, 3.0, 1.0)) * partner_scale
    down_own = flag(near, 2.0) * scale
    down_partner = flag(near, jnp.where(odd, 1.0, 3.0)) * partner_scale
    choose = lambda one, two: jnp.where(rises, one, two)
    first_own, first_partner = choose(up_own, down_own), choose(up_partner, down_partner)
    second_own, second_partner = choose(down_own, up_own), choose(down_partner, up_partner)
    for k in range(0, own_ref.shape[1], CHUNK):
        own, partner = own_ref[:, pl.ds(k, CHUNK)], values(partner_ref, k)
        first_ref[:, pl.ds(k, CHUNK)] = fixed(own * first_own + partner * first_partner)
        second_ref[:, pl.ds(k, CHUNK)] = fixed(own * second_own + partner * second_partner)
    finish(first_ref, sent, width)
    finish(second_ref, sent, width)


def window_kernel(samples, count, own_ref, coded_ref, partner_ref, first_ref, second_ref, far_ref, scaled_ref, sent_ref):
    odd, _, use_first, use_second, use_far = place(count)
    width = aux(coded_ref)[1]
    partner_exponent, partner_width = aux(partner_ref)[:2]
    far_exponent, far_width = aux(far_ref)[:2]
    partner_scale = unit(partner_exponent, jnp.where(odd, partner_width, width) >= 1)
    first_scale = unit(aux(first_ref)[0], use_first)
    second_scale = unit(aux(second_ref)[0], use_second)
    far_scale = jnp.where(jnp.where(odd, width, far_width) >= 3, unit(far_exponent, use_far), 0.0)
    rows = own_ref.shape[0]
    acc = jnp.zeros((2 * rows, scaled_ref.shape[1]), jnp.float32)
    curved = jnp.zeros((rows, CHUNK), jnp.float32)
    for k in range(0, own_ref.shape[1], CHUNK):
        own = own_ref[:, pl.ds(k, CHUNK)]
        mixed = (
            own
            + values(partner_ref, k) * partner_scale
            + values(first_ref, k) * first_scale
            + values(second_ref, k) * second_scale
            + values(far_ref, k) * far_scale
        )
        acc = acc + jnp.dot(
            two_terms(mixed), scaled_ref[pl.ds(k, CHUNK)], preferred_element_type=jnp.float32
        )
        curved = curved + own * mixed
    z = acc[:rows] + acc[rows:]
    exponent, scale = scale_of(jnp.max(jnp.abs(z), 1, keepdims=True))
    sent_ref[:, pl.ds(0, z.shape[1])] = fixed(z * scale)
    finish(sent_ref, exponent, *split(jnp.sum(curved, 1, keepdims=True) / samples))


def collect_kernel(parts_ref, z0, z1, z2, z3, flat_ref):
    terms = []
    for z in (z0, z1, z2, z3):
        _, exponent, high, low = aux(z)
        terms.append((high + low * 2.0**-UNIT) * 2.0 * unit(exponent))
    lane = lax.broadcasted_iota(jnp.int32, parts_ref.shape, 1)
    parts = jnp.where(lane == 3, total(terms), parts_ref[...])
    filled = jnp.concatenate([parts, jnp.zeros((AUX - parts.shape[0], AUX), jnp.float32)], 0)
    flat_ref[...] = filled.T[:8]


def last_kernel(samples, shrink_ref, p0, p1, p2, p3, z0, z1, z2, z3, start_ref, first_ref, effects_ref, residual_ref):
    rows = shrink_ref.shape[0]
    flat = total([p[...] for p in (p0, p1, p2, p3)])
    parts = jnp.concatenate([flat, jnp.zeros((AUX - 8, AUX), jnp.float32)], 0).T[:rows]
    bb, bw, ww, wu = (parts[:, k : k + 1] for k in range(4))
    shrink = shrink_ref[...]
    start, first = start_ref[...], first_ref[...]
    second = total([grid_values(z) for z in (z0, z1, z2, z3)]) / samples
    ratio = bw / bb
    step = 1.0 / (ratio + shrink)
    norm = step * step * (ww - ratio * bw)
    bend = norm / bb
    curve = step * step * (ratio * (ratio * bw - 2.0 * ww) + wu) + shrink * norm - bend * norm / step
    step2 = jnp.where(curve > 0, norm / curve, 0.0)
    rest = step * (ratio * start - first)
    direction = rest + bend * start
    image = step * (ratio * first - second) + bend * first + shrink * direction
    effects_ref[...] = step * start + step2 * direction
    residual_ref[...] = rest - step2 * image


def snp_parts(value):
    count = lax.axis_size("snp")
    value = value + swap(value, "snp", 1)
    bit = 2
    while 4 * bit < count:
        value = total([value, *partners(value, "snp", bit, 2 * bit)])
        bit *= 4
    if 2 * bit < count:
        return [value, *partners(value, "snp", bit, 2 * bit)]
    return [value, swap(value, "snp", bit), jnp.zeros_like(value), jnp.zeros_like(value)]


def shards(dosage, band_width, marginal, penalty):
    groups, count = lax.axis_size("samp"), lax.axis_size("snp")
    local, size, rows = dosage.shape[0], dosage.shape[1], marginal.shape[1]
    samples = local * groups
    start = marginal.T
    shrink = penalty[:, None]
    grid, own_shape = (rows, size), (rows, local)
    own_out, coded_out = (own_shape, jnp.float32), ((rows, local + AUX), jnp.int16)

    sent_out = ((rows, size + AUX), jnp.int16)

    (sums,) = call(stats_kernel, [((8, size), jnp.float32)], dosage)
    one, two, three = partners(sums, "samp", 1, 2)
    one, band_width = lax.optimization_barrier((one, band_width))
    wide = jnp.broadcast_to(band_width.astype(jnp.float32)[:, None], (8, AUX))
    near = shifted(wide)
    two, three, near = lax.optimization_barrier((two, three, near))
    scaled, own, coded = call(
        functools.partial(first_kernel, samples),
        [(dosage.shape, jnp.bfloat16), own_out, coded_out],
        wide, sums, one, two, three, dosage, start,
    )

    def window(own, coded):
        far = distant(coded)
        partner = swap(coded, "snp", 1)
        one, two = call(
            functools.partial(give_kernel, count), [coded_out, coded_out], near, own, coded, partner
        )
        two = between(two, 1)
        one = between(one, 0)
        (z,) = call(
            functools.partial(window_kernel, samples, count), [sent_out],
            own, coded, partner, one, two, far, scaled,
        )
        return [z, *partners(z, "samp", 1, 2)]

    first, parts, own, coded = call(
        functools.partial(next_kernel, samples),
        [(grid, jnp.float32), ((rows, AUX), jnp.float32), own_out, coded_out],
        wide, *window(own, coded), start, scaled,
    )
    zs = window(own, coded)
    (flat,) = call(collect_kernel, [((8, AUX), jnp.float32)], parts, *zs)
    parts = snp_parts(flat)
    effects, residual = call(
        functools.partial(last_kernel, samples),
        [(grid, jnp.float32), (grid, jnp.float32)],
        shrink, *parts, *zs, start, first,
    )
    return (effects.T, residual.T)


def solution(mesh):
    in_specs = (P("samp", "snp"), P("snp"), P("snp", None), P())
    out_specs = (P("snp", None), P("snp", None))
    return jax.shard_map(shards, mesh=mesh, in_specs=in_specs, out_specs=out_specs, check_vma=False)
```

```python
import functools

import jax
import jax.numpy as jnp
from jax import lax
from jax.experimental import pallas as pl
from jax.experimental.pallas import tpu as pltpu
from jax.sharding import PartitionSpec as P


AUX = 128
CHUNK = 512
UNIT = 14
ROWS = 128


def swap(value, axis, bits):
    return lax.ppermute(value, axis, [(i, i ^ bits) for i in range(lax.axis_size(axis))])


def crossing(value, rising):
    count = lax.axis_size("snp")
    pairs = []
    for i in range(count):
        target = i + 2 if i % 2 == rising else i - 2
        pairs.append((i, target if 0 <= target < count else i ^ 1))
    return lax.ppermute(value, "snp", pairs)


def adjacent(value):
    rows, count = lax.axis_size("samp"), lax.axis_size("snp")
    pairs = []
    for row in range(rows):
        for i in range(count):
            target = i + 1 if i % 2 else i - 1
            inside = 0 <= target < count
            pairs.append((row * count + i, row * count + target if inside else (row ^ 1) * count + i))
    return lax.ppermute(value, ("samp", "snp"), pairs)


def shifted(value):
    count = lax.axis_size("snp")
    return lax.ppermute(value, "snp", [(i, (i + 2) % count) for i in range(count)])


def partners(value, axis, low, high):
    return [swap(value, axis, k) for k in (low, high, low + high)]


def total(parts):
    own, one, two, three = parts
    return (own + one) + (two + three)


def call(body, out_shape, *args):
    specs = [pl.BlockSpec(memory_space=pltpu.VMEM) for _ in args]
    outs = [jax.ShapeDtypeStruct(shape, kind) for shape, kind in out_shape]
    return pl.pallas_call(
        body,
        out_shape=outs,
        in_specs=specs,
        out_specs=[pl.BlockSpec(memory_space=pltpu.VMEM) for _ in outs],
        compiler_params=pltpu.CompilerParams(vmem_limit_bytes=32 << 20),
    )(*args)


def two_terms(value):
    high = value.astype(jnp.bfloat16)
    low = (value - high.astype(jnp.float32)).astype(jnp.bfloat16)
    return jnp.concatenate([high, low], 0)


def stats_kernel(dosage_ref, sums_ref):
    acc = jnp.zeros((8, dosage_ref.shape[1]), jnp.float32)
    square = acc
    for k in range(0, dosage_ref.shape[0], ROWS):
        part = dosage_ref[pl.ds(k, ROWS)].astype(jnp.float32)
        part = part.reshape(ROWS // 8, 8, part.shape[1])
        acc = acc + jnp.sum(part, 0)
        square = square + jnp.sum(part * part, 0)
    row = lax.broadcasted_iota(jnp.int32, (8, 1), 0)
    first = jnp.sum(acc, 0, keepdims=True)
    second = jnp.sum(square, 0, keepdims=True)
    sums_ref[...] = jnp.where(row == 0, first, second)


def finish(coded_ref, *columns):
    lane = lax.broadcasted_iota(jnp.int32, (coded_ref.shape[0], AUX), 1)
    extra = jnp.zeros(lane.shape, jnp.float32)
    for k, column in enumerate(columns):
        extra = jnp.where(lane == k, column, extra)
    coded_ref[:, pl.ds(coded_ref.shape[1] - AUX, AUX)] = extra.astype(jnp.int32).astype(jnp.int16)


def fixed(value):
    return jnp.clip(jnp.round(value), -32767.0, 32767.0).astype(jnp.int32).astype(jnp.int16)


def scale_of(peak):
    exponent = jnp.floor(jnp.log2(jnp.maximum(peak, 1e-30)))
    return exponent, jnp.exp2(UNIT - exponent)


def encode(own_ref, coded_ref, width):
    exponent, scale = scale_of(jnp.max(jnp.abs(own_ref[...]), 1, keepdims=True))
    for k in range(0, own_ref.shape[1], CHUNK):
        coded_ref[:, pl.ds(k, CHUNK)] = fixed(own_ref[:, pl.ds(k, CHUNK)] * scale)
    finish(coded_ref, exponent, width)


def split(value):
    exponent, scale = scale_of(jnp.abs(value))
    high = jnp.round(value * scale * 0.5)
    low = jnp.round((value * scale * 0.5 - high) * 2.0**UNIT)
    return exponent, high, low


def aux(coded_ref):
    extra = coded_ref[:, pl.ds(coded_ref.shape[1] - AUX, AUX)].astype(jnp.int32).astype(jnp.float32)
    return [extra[:, k : k + 1] for k in range(4)]


def unit(exponent, use=True):
    return jnp.where(use, jnp.exp2(exponent - UNIT), 0.0)


def grid_values(coded_ref):
    size = coded_ref.shape[1] - AUX
    return coded_ref[:, pl.ds(0, size)].astype(jnp.int32).astype(jnp.float32) * unit(aux(coded_ref)[0])


def values(coded_ref, k):
    return coded_ref[:, pl.ds(k, CHUNK)].astype(jnp.int32).astype(jnp.float32)


def project(value, scaled_ref, own_ref):
    rows = value.shape[0]
    terms = two_terms(value)
    for k in range(0, scaled_ref.shape[0], CHUNK):
        both = lax.dot_general(
            terms, scaled_ref[pl.ds(k, CHUNK)], (((1,), (1,)), ((), ())), preferred_element_type=jnp.float32
        )
        own_ref[:, pl.ds(k, CHUNK)] = both[:rows] + both[rows:]


def first_kernel(samples, wide_ref, s0, s1, s2, s3, dosage_ref, start_ref, scaled_ref, own_ref, coded_ref):
    sums = total([s[0:2] for s in (s0, s1, s2, s3)])
    center = sums[0:1] / samples
    spread = sums[1:2] / samples - center * center
    factor = lax.rsqrt(spread + 1e-05)
    for k in range(0, dosage_ref.shape[0], CHUNK):
        part = dosage_ref[pl.ds(k, CHUNK)].astype(jnp.float32)
        scaled_ref[pl.ds(k, CHUNK)] = ((part - center) * factor).astype(jnp.bfloat16)
    project(start_ref[...], scaled_ref, own_ref)
    encode(own_ref, coded_ref, wide_ref[0:1, 0:1])


def next_kernel(
    samples, wide_ref, z0, z1, z2, z3, start_ref, scaled_ref, first_ref, parts_ref, own_ref, coded_ref
):
    first = total([grid_values(z) for z in (z0, z1, z2, z3)]) / samples
    first_ref[...] = first
    start = start_ref[...]
    lane = lax.broadcasted_iota(jnp.int32, parts_ref.shape, 1)
    parts = jnp.zeros(parts_ref.shape, jnp.float32)
    for k, (a, b) in enumerate(((start, start), (start, first), (first, first))):
        parts = jnp.where(lane == k, jnp.sum(a * b, 1, keepdims=True), parts)
    parts_ref[...] = parts
    project(first, scaled_ref, own_ref)
    encode(own_ref, coded_ref, wide_ref[0:1, 0:1])


def place(count):
    index = lax.axis_index("snp")
    odd = (index & 1) == 1
    below, above = (index >= 2).astype(jnp.int32), (index < count - 2).astype(jnp.int32)
    side = jnp.where(odd, above, below) == 1
    across = jnp.where(odd, below, above) == 1
    return odd, side, across


def give_kernel(count, up, near_ref, own_ref, coded_ref, other_ref, sent_ref):
    odd, side, _ = place(count)
    exponent, width = aux(coded_ref)[:2]
    other_exponent, other_width = aux(other_ref)[:2]
    near = near_ref[0:1, 0:1]
    sent = jnp.maximum(exponent, other_exponent) + 1.0
    scale = jnp.exp2(UNIT - sent)
    rises = odd if up else jnp.logical_not(odd)
    known = True if up else side
    own_scale = jnp.where(jnp.where(rises, width, near) >= 2, scale, 0.0)
    other_scale = jnp.where(jnp.where(rises, other_width, near) >= 3, scale * unit(other_exponent, known), 0.0)
    for k in range(0, own_ref.shape[1], CHUNK):
        sent_ref[:, pl.ds(k, CHUNK)] = fixed(own_ref[:, pl.ds(k, CHUNK)] * own_scale + values(other_ref, k) * other_scale)
    finish(sent_ref, sent, width)


def window_kernel(samples, count, own_ref, coded_ref, partner_ref, next_ref, same_ref, cross_ref, scaled_ref, sent_ref):
    odd, side, across = place(count)
    width = aux(coded_ref)[1]
    partner_exponent, partner_width = aux(partner_ref)[:2]
    next_exponent, next_width = aux(next_ref)[:2]
    partner_scale = unit(partner_exponent, jnp.where(odd, partner_width, width) >= 1)
    next_scale = jnp.where(jnp.where(odd, width, next_width) >= 1, unit(next_exponent, side), 0.0)
    same_scale = unit(aux(same_ref)[0], side)
    cross_scale = unit(aux(cross_ref)[0], across)
    rows = own_ref.shape[0]
    acc = jnp.zeros((2 * rows, scaled_ref.shape[1]), jnp.float32)
    curved = jnp.zeros((rows, CHUNK), jnp.float32)
    for k in range(0, own_ref.shape[1], CHUNK):
        own = own_ref[:, pl.ds(k, CHUNK)]
        mixed = (
            own
            + values(partner_ref, k) * partner_scale
            + values(next_ref, k) * next_scale
            + values(same_ref, k) * same_scale
            + values(cross_ref, k) * cross_scale
        )
        acc = acc + jnp.dot(
            two_terms(mixed), scaled_ref[pl.ds(k, CHUNK)], preferred_element_type=jnp.float32
        )
        curved = curved + own * mixed
    z = acc[:rows] + acc[rows:]
    exponent, scale = scale_of(jnp.max(jnp.abs(z), 1, keepdims=True))
    sent_ref[:, pl.ds(0, z.shape[1])] = fixed(z * scale)
    finish(sent_ref, exponent, *split(jnp.sum(curved, 1, keepdims=True) / samples))


def collect_kernel(parts_ref, z0, z1, z2, z3, flat_ref):
    terms = []
    for z in (z0, z1, z2, z3):
        _, exponent, high, low = aux(z)
        terms.append((high + low * 2.0**-UNIT) * 2.0 * unit(exponent))
    lane = lax.broadcasted_iota(jnp.int32, parts_ref.shape, 1)
    parts = jnp.where(lane == 3, total(terms), parts_ref[...])
    filled = jnp.concatenate([parts, jnp.zeros((AUX - parts.shape[0], AUX), jnp.float32)], 0)
    flat_ref[...] = filled.T[:8]


def last_kernel(samples, shrink_ref, p0, p1, p2, p3, z0, z1, z2, z3, start_ref, first_ref, effects_ref, residual_ref):
    rows = shrink_ref.shape[0]
    flat = total([p[...] for p in (p0, p1, p2, p3)])
    parts = jnp.concatenate([flat, jnp.zeros((AUX - 8, AUX), jnp.float32)], 0).T[:rows]
    bb, bw, ww, wu = (parts[:, k : k + 1] for k in range(4))
    shrink = shrink_ref[...]
    start, first = start_ref[...], first_ref[...]
    second = total([grid_values(z) for z in (z0, z1, z2, z3)]) / samples
    ratio = bw / bb
    step = 1.0 / (ratio + shrink)
    norm = step * step * (ww - ratio * bw)
    bend = norm / bb
    curve = step * step * (ratio * (ratio * bw - 2.0 * ww) + wu) + shrink * norm - bend * norm / step
    step2 = jnp.where(curve > 0, norm / curve, 0.0)
    rest = step * (ratio * start - first)
    direction = rest + bend * start
    image = step * (ratio * first - second) + bend * first + shrink * direction
    effects_ref[...] = step * start + step2 * direction
    residual_ref[...] = rest - step2 * image


def snp_parts(value):
    count = lax.axis_size("snp")
    value = value + swap(value, "snp", 1)
    bit = 2
    while 4 * bit < count:
        value = total([value, *partners(value, "snp", bit, 2 * bit)])
        bit *= 4
    if 2 * bit < count:
        return [value, *partners(value, "snp", bit, 2 * bit)]
    return [value, swap(value, "snp", bit), jnp.zeros_like(value), jnp.zeros_like(value)]


def shards(dosage, band_width, marginal, penalty):
    groups, count = lax.axis_size("samp"), lax.axis_size("snp")
    local, size, rows = dosage.shape[0], dosage.shape[1], marginal.shape[1]
    samples = local * groups
    start = marginal.T
    shrink = penalty[:, None]
    grid, own_shape = (rows, size), (rows, local)
    own_out, coded_out = (own_shape, jnp.float32), ((rows, local + AUX), jnp.int16)

    sent_out = ((rows, size + AUX), jnp.int16)

    (sums,) = call(stats_kernel, [((8, size), jnp.float32)], dosage)
    one, two, three = partners(sums, "samp", 1, 2)
    one, band_width = lax.optimization_barrier((one, band_width))
    wide = jnp.broadcast_to(band_width.astype(jnp.float32)[:, None], (8, AUX))
    near = shifted(wide)
    two, three, near = lax.optimization_barrier((two, three, near))
    scaled, own, coded = call(
        functools.partial(first_kernel, samples),
        [(dosage.shape, jnp.bfloat16), own_out, coded_out],
        wide, sums, one, two, three, dosage, start,
    )

    def give(up, *args):
        return call(functools.partial(give_kernel, count, up), [coded_out], near, *args)[0]

    def window(own, coded):
        beside = adjacent(coded)
        partner = swap(coded, "snp", 1)
        cross = crossing(give(1, own, coded, partner), 1)
        same = crossing(give(0, own, coded, beside), 0)
        (z,) = call(
            functools.partial(window_kernel, samples, count), [sent_out],
            own, coded, partner, beside, same, cross, scaled,
        )
        return [z, *partners(z, "samp", 1, 2)]

    first, parts, own, coded = call(
        functools.partial(next_kernel, samples),
        [(grid, jnp.float32), ((rows, AUX), jnp.float32), own_out, coded_out],
        wide, *window(own, coded), start, scaled,
    )
    zs = window(own, coded)
    (flat,) = call(collect_kernel, [((8, AUX), jnp.float32)], parts, *zs)
    parts = snp_parts(flat)
    effects, residual = call(
        functools.partial(last_kernel, samples),
        [(grid, jnp.float32), (grid, jnp.float32)],
        shrink, *parts, *zs, start, first,
    )
    return (effects.T, residual.T)


def solution(mesh):
    in_specs = (P("samp", "snp"), P("snp"), P("snp", None), P())
    out_specs = (P("snp", None), P("snp", None))
    return jax.shard_map(shards, mesh=mesh, in_specs=in_specs, out_specs=out_specs, check_vma=False)
```

```python
import functools

import jax
import jax.numpy as jnp
from jax import lax
from jax.experimental import pallas as pl
from jax.experimental.pallas import tpu as pltpu
from jax.sharding import PartitionSpec as P


AUX = 128
LESS = 96
CHUNK = 512
UNIT = 14
ROWS = 128


def swap(value, axis, bits):
    return lax.ppermute(value, axis, [(i, i ^ bits) for i in range(lax.axis_size(axis))])


def crossing(value, rising):
    count = lax.axis_size("snp")
    pairs = []
    for i in range(count):
        target = i + 2 if i % 2 == rising else i - 2
        pairs.append((i, target if 0 <= target < count else i ^ 1))
    return lax.ppermute(value, "snp", pairs)


def adjacent(value):
    rows, count = lax.axis_size("samp"), lax.axis_size("snp")
    pairs = []
    for row in range(rows):
        for i in range(count):
            target = i + 1 if i % 2 else i - 1
            inside = 0 <= target < count
            pairs.append((row * count + i, row * count + target if inside else (row ^ 1) * count + i))
    return lax.ppermute(value, ("samp", "snp"), pairs)


def shifted(value):
    count = lax.axis_size("snp")
    return lax.ppermute(value, "snp", [(i, (i + 2) % count) for i in range(count)])


def partners(value, axis, low, high):
    return [swap(value, axis, k) for k in (low, high, low + high)]


def total(parts):
    own, one, two, three = parts
    return (own + one) + (two + three)


def call(body, out_shape, *args):
    specs = [pl.BlockSpec(memory_space=pltpu.VMEM) for _ in args]
    outs = [jax.ShapeDtypeStruct(shape, kind) for shape, kind in out_shape]
    return pl.pallas_call(
        body,
        out_shape=outs,
        in_specs=specs,
        out_specs=[pl.BlockSpec(memory_space=pltpu.VMEM) for _ in outs],
        compiler_params=pltpu.CompilerParams(vmem_limit_bytes=32 << 20),
    )(*args)


def two_terms(value):
    high = value.astype(jnp.bfloat16)
    low = (value - high.astype(jnp.float32)).astype(jnp.bfloat16)
    return jnp.concatenate([high, low], 0)


def wide_kernel(width_ref, wide_ref):
    wide_ref[...] = jnp.full(wide_ref.shape, width_ref[0].astype(jnp.float32))


def stats_kernel(dosage_ref, sums_ref):
    acc = jnp.zeros((8, dosage_ref.shape[1]), jnp.float32)
    square = acc
    for k in range(0, dosage_ref.shape[0], ROWS):
        part = dosage_ref[pl.ds(k, ROWS)].astype(jnp.float32)
        part = part.reshape(ROWS // 8, 8, part.shape[1])
        acc = acc + jnp.sum(part, 0)
        square = square + jnp.sum(part * part, 0)
    row = lax.broadcasted_iota(jnp.int32, (8, 1), 0)
    first = jnp.sum(acc, 0, keepdims=True)
    second = jnp.sum(square, 0, keepdims=True)
    sums_ref[...] = jnp.where(row == 0, first, second)


def finish(coded_ref, *columns):
    count = coded_ref.shape[1] % AUX or AUX
    lane = lax.broadcasted_iota(jnp.int32, (coded_ref.shape[0], count), 1)
    extra = jnp.zeros(lane.shape, jnp.float32)
    for k, column in enumerate(columns):
        extra = jnp.where(lane == k, column, extra)
    coded_ref[:, pl.ds(coded_ref.shape[1] - count, count)] = extra.astype(jnp.int32).astype(jnp.int16)


def fixed(value):
    return jnp.clip(jnp.round(value), -32767.0, 32767.0).astype(jnp.int32).astype(jnp.int16)


def scale_of(peak):
    exponent = jnp.floor(jnp.log2(jnp.maximum(peak, 1e-30)))
    return exponent, jnp.exp2(UNIT - exponent)


def encode(own_ref, coded_ref, shared_ref, width):
    exponent, scale = scale_of(jnp.max(jnp.abs(own_ref[...]), 1, keepdims=True))
    for k in range(0, own_ref.shape[1], CHUNK):
        value = fixed(own_ref[:, pl.ds(k, CHUNK)] * scale)
        coded_ref[:, pl.ds(k, CHUNK)] = value
        shared_ref[:, pl.ds(k, CHUNK)] = value
    finish(coded_ref, exponent, width)
    finish(shared_ref, exponent, width)


def split(value):
    exponent, scale = scale_of(jnp.abs(value))
    high = jnp.round(value * scale * 0.5)
    low = jnp.round((value * scale * 0.5 - high) * 2.0**UNIT)
    return exponent, high, low


def aux(coded_ref):
    count = coded_ref.shape[1] % AUX or AUX
    extra = coded_ref[:, pl.ds(coded_ref.shape[1] - count, count)].astype(jnp.int32).astype(jnp.float32)
    return [extra[:, k : k + 1] for k in range(4)]


def unit(exponent, use=True):
    return jnp.where(use, jnp.exp2(exponent - UNIT), 0.0)


def grid_values(coded_ref):
    size = coded_ref.shape[1] - AUX
    return coded_ref[:, pl.ds(0, size)].astype(jnp.int32).astype(jnp.float32) * unit(aux(coded_ref)[0])


def values(coded_ref, k):
    return coded_ref[:, pl.ds(k, CHUNK)].astype(jnp.int32).astype(jnp.float32)


def project(value, turned_ref, own_ref):
    rows = value.shape[0]
    terms = two_terms(value)
    for k in range(0, turned_ref.shape[1], CHUNK):
        both = jnp.dot(terms, turned_ref[:, pl.ds(k, CHUNK)], preferred_element_type=jnp.float32)
        own_ref[:, pl.ds(k, CHUNK)] = both[:rows] + both[rows:]


def first_kernel(samples, wide_ref, s0, s1, s2, s3, dosage_ref, start_ref, scaled_ref, turned_ref, own_ref, coded_ref, shared_ref):
    sums = total([s[0:2] for s in (s0, s1, s2, s3)])
    center = sums[0:1] / samples
    spread = sums[1:2] / samples - center * center
    factor = lax.rsqrt(spread + 1e-05)
    for k in range(0, dosage_ref.shape[0], CHUNK):
        part = dosage_ref[pl.ds(k, CHUNK)].astype(jnp.float32)
        part = ((part - center) * factor).astype(jnp.bfloat16)
        scaled_ref[pl.ds(k, CHUNK)] = part
        turned_ref[:, pl.ds(k, CHUNK)] = part.T
    project(start_ref[...], turned_ref, own_ref)
    encode(own_ref, coded_ref, shared_ref, wide_ref[0:1, 0:1])


def next_kernel(
    samples, wide_ref, z0, z1, z2, z3, start_ref, turned_ref, first_ref, parts_ref, own_ref, coded_ref, shared_ref
):
    first = total([grid_values(z) for z in (z0, z1, z2, z3)]) / samples
    first_ref[...] = first
    start = start_ref[...]
    lane = lax.broadcasted_iota(jnp.int32, parts_ref.shape, 1)
    parts = jnp.zeros(parts_ref.shape, jnp.float32)
    for k, (a, b) in enumerate(((start, start), (start, first), (first, first))):
        parts = jnp.where(lane == k, jnp.sum(a * b, 1, keepdims=True), parts)
    parts_ref[...] = parts
    project(first, turned_ref, own_ref)
    encode(own_ref, coded_ref, shared_ref, wide_ref[0:1, 0:1])


def place(count):
    index = lax.axis_index("snp")
    odd = (index & 1) == 1
    below, above = (index >= 2).astype(jnp.int32), (index < count - 2).astype(jnp.int32)
    side = jnp.where(odd, above, below) == 1
    across = jnp.where(odd, below, above) == 1
    return odd, side, across


def give_kernel(count, up, near_ref, own_ref, coded_ref, other_ref, sent_ref):
    odd, side, _ = place(count)
    exponent, width = aux(coded_ref)[:2]
    other_exponent, other_width = aux(other_ref)[:2]
    near = near_ref[0:1, 0:1]
    sent = jnp.maximum(exponent, other_exponent) + 1.0
    scale = jnp.exp2(UNIT - sent)
    rises = odd if up else jnp.logical_not(odd)
    known = True if up else side
    own_scale = jnp.where(jnp.where(rises, width, near) >= 2, scale, 0.0)
    other_scale = jnp.where(jnp.where(rises, other_width, near) >= 3, scale * unit(other_exponent, known), 0.0)
    for k in range(0, own_ref.shape[1], CHUNK):
        sent_ref[:, pl.ds(k, CHUNK)] = fixed(own_ref[:, pl.ds(k, CHUNK)] * own_scale + values(other_ref, k) * other_scale)
    finish(sent_ref, sent, width)


def window_kernel(samples, count, own_ref, coded_ref, partner_ref, next_ref, same_ref, cross_ref, scaled_ref, sent_ref):
    odd, side, across = place(count)
    width = aux(coded_ref)[1]
    partner_exponent, partner_width = aux(partner_ref)[:2]
    next_exponent, next_width = aux(next_ref)[:2]
    partner_scale = unit(partner_exponent, jnp.where(odd, partner_width, width) >= 1)
    next_scale = jnp.where(jnp.where(odd, width, next_width) >= 1, unit(next_exponent, side), 0.0)
    same_scale = unit(aux(same_ref)[0], side)
    cross_scale = unit(aux(cross_ref)[0], across)
    rows = own_ref.shape[0]
    acc = jnp.zeros((2 * rows, scaled_ref.shape[1]), jnp.float32)
    curved = jnp.zeros((rows, CHUNK), jnp.float32)
    for k in range(0, own_ref.shape[1], CHUNK):
        own = own_ref[:, pl.ds(k, CHUNK)]
        mixed = (
            own
            + values(partner_ref, k) * partner_scale
            + values(next_ref, k) * next_scale
            + values(same_ref, k) * same_scale
            + values(cross_ref, k) * cross_scale
        )
        acc = acc + jnp.dot(
            two_terms(mixed), scaled_ref[pl.ds(k, CHUNK)], preferred_element_type=jnp.float32
        )
        curved = curved + own * mixed
    z = acc[:rows] + acc[rows:]
    exponent, scale = scale_of(jnp.max(jnp.abs(z), 1, keepdims=True))
    sent_ref[:, pl.ds(0, z.shape[1])] = fixed(z * scale)
    finish(sent_ref, exponent, *split(jnp.sum(curved, 1, keepdims=True) / samples))


def collect_kernel(parts_ref, z0, z1, z2, z3, flat_ref):
    terms = []
    for z in (z0, z1, z2, z3):
        _, exponent, high, low = aux(z)
        terms.append((high + low * 2.0**-UNIT) * 2.0 * unit(exponent))
    lane = lax.broadcasted_iota(jnp.int32, parts_ref.shape, 1)
    parts = jnp.where(lane == 3, total(terms), parts_ref[...])
    filled = jnp.concatenate([parts, jnp.zeros((AUX - parts.shape[0], AUX), jnp.float32)], 0)
    flat_ref[...] = filled.T[:8]


def last_kernel(samples, shrink_ref, p0, p1, p2, p3, z0, z1, z2, z3, start_ref, first_ref, effects_ref, residual_ref):
    rows = shrink_ref.shape[0]
    flat = total([p[...] for p in (p0, p1, p2, p3)])
    parts = jnp.concatenate([flat, jnp.zeros((AUX - 8, AUX), jnp.float32)], 0).T[:rows]
    bb, bw, ww, wu = (parts[:, k : k + 1] for k in range(4))
    shrink = shrink_ref[...]
    start, first = start_ref[...], first_ref[...]
    second = total([grid_values(z) for z in (z0, z1, z2, z3)]) / samples
    ratio = bw / bb
    step = 1.0 / (ratio + shrink)
    norm = step * step * (ww - ratio * bw)
    bend = norm / bb
    curve = step * step * (ratio * (ratio * bw - 2.0 * ww) + wu) + shrink * norm - bend * norm / step
    step2 = jnp.where(curve > 0, norm / curve, 0.0)
    rest = step * (ratio * start - first)
    direction = rest + bend * start
    image = step * (ratio * first - second) + bend * first + shrink * direction
    effects_ref[...] = step * start + step2 * direction
    residual_ref[...] = rest - step2 * image


def snp_parts(value):
    count = lax.axis_size("snp")
    value = value + swap(value, "snp", 1)
    bit = 2
    while 4 * bit < count:
        value = total([value, *others(value, bit)])
        bit *= 4
    if 2 * bit < count:
        return [value, *others(value, bit)]
    return [value, swap(value, "snp", bit ^ 1), jnp.zeros_like(value), jnp.zeros_like(value)]


def others(value, bit):
    return [swap(value, "snp", k ^ 1) for k in (bit, 2 * bit, 3 * bit)]


def shards(dosage, band_width, marginal, penalty):
    groups, count = lax.axis_size("samp"), lax.axis_size("snp")
    local, size, rows = dosage.shape[0], dosage.shape[1], marginal.shape[1]
    samples = local * groups
    start = marginal.T
    shrink = penalty[:, None]
    grid, own_shape = (rows, size), (rows, local)
    own_out, coded_out = (own_shape, jnp.float32), ((rows, local + AUX), jnp.int16)
    shared_out = ((rows, local + LESS), jnp.int16)

    sent_out = ((rows, size + AUX), jnp.int16)

    (sums,) = call(stats_kernel, [((8, size), jnp.float32)], dosage)
    one, two, three = partners(sums, "samp", 1, 2)
    one, band_width = lax.optimization_barrier((one, band_width))
    wide = pl.pallas_call(
        wide_kernel,
        out_shape=jax.ShapeDtypeStruct((8, size + AUX), jnp.float32),
        in_specs=[pl.BlockSpec(memory_space=pltpu.SMEM)],
        out_specs=pl.BlockSpec(memory_space=pltpu.VMEM),
        cost_estimate=pl.CostEstimate(flops=10**10, bytes_accessed=10**8, transcendentals=0),
    )(band_width)
    near = shifted(wide)
    two, three, near = lax.optimization_barrier((two, three, near))
    scaled, turned, own, coded, shared = call(
        functools.partial(first_kernel, samples),
        [(dosage.shape, jnp.bfloat16), (dosage.shape[::-1], jnp.bfloat16), own_out, coded_out, shared_out],
        wide, sums, one, two, three, dosage, start,
    )

    def give(up, *args):
        return call(functools.partial(give_kernel, count, up), [coded_out], near, *args)[0]

    def window(own, coded, shared):
        beside = adjacent(coded)
        partner = swap(shared, "snp", 1)
        cross = crossing(give(1, own, coded, partner), 1)
        same = crossing(give(0, own, coded, beside), 0)
        (z,) = call(
            functools.partial(window_kernel, samples, count), [sent_out],
            own, coded, partner, beside, same, cross, scaled,
        )
        return [z, *partners(z, "samp", 1, 2)]

    first, parts, own, coded, shared = call(
        functools.partial(next_kernel, samples),
        [(grid, jnp.float32), ((rows, AUX), jnp.float32), own_out, coded_out, shared_out],
        wide, *window(own, coded, shared), start, turned,
    )
    zs = window(own, coded, shared)
    (flat,) = call(collect_kernel, [((8, AUX), jnp.float32)], parts, *zs)
    parts = snp_parts(flat)
    effects, residual = call(
        functools.partial(last_kernel, samples),
        [(grid, jnp.float32), (grid, jnp.float32)],
        shrink, *parts, *zs, start, first,
    )
    return (effects.T, residual.T)


def solution(mesh):
    in_specs = (P("samp", "snp"), P("snp"), P("snp", None), P())
    out_specs = (P("snp", None), P("snp", None))
    return jax.shard_map(shards, mesh=mesh, in_specs=in_specs, out_specs=out_specs, check_vma=False)
```

```python
import functools

import jax
import jax.numpy as jnp
from jax import lax
from jax.experimental import pallas as pl
from jax.experimental.pallas import tpu as pltpu
from jax.sharding import PartitionSpec as P


AUX = 128
LESS = 96
CHUNK = 512
UNIT = 14
ROWS = 128


def swap(value, axis, bits):
    return lax.ppermute(value, axis, [(i, i ^ bits) for i in range(lax.axis_size(axis))])


def crossing(value, rising):
    count = lax.axis_size("snp")
    pairs = []
    for i in range(count):
        target = i + 2 if i % 2 == rising else i - 2
        pairs.append((i, target if 0 <= target < count else i ^ 1))
    return lax.ppermute(value, "snp", pairs)


def adjacent(value):
    rows, count = lax.axis_size("samp"), lax.axis_size("snp")
    pairs = []
    for row in range(rows):
        for i in range(count):
            target = i + 1 if i % 2 else i - 1
            inside = 0 <= target < count
            pairs.append((row * count + i, row * count + target if inside else (row ^ 1) * count + i))
    return lax.ppermute(value, ("samp", "snp"), pairs)


def shifted(value):
    count = lax.axis_size("snp")
    return lax.ppermute(value, "snp", [(i, (i + 2) % count) for i in range(count)])


def partners(value, axis, low, high):
    return [swap(value, axis, k) for k in (low, high, low + high)]


def total(parts):
    own, one, two, three = parts
    return (own + one) + (two + three)


def call(body, out_shape, *args):
    specs = [pl.BlockSpec(memory_space=pltpu.VMEM) for _ in args]
    outs = [jax.ShapeDtypeStruct(shape, kind) for shape, kind in out_shape]
    return pl.pallas_call(
        body,
        out_shape=outs,
        in_specs=specs,
        out_specs=[pl.BlockSpec(memory_space=pltpu.VMEM) for _ in outs],
        compiler_params=pltpu.CompilerParams(vmem_limit_bytes=32 << 20),
    )(*args)


def two_terms(value):
    high = value.astype(jnp.bfloat16)
    low = (value - high.astype(jnp.float32)).astype(jnp.bfloat16)
    return jnp.concatenate([high, low], 0)


def wide_kernel(width_ref, wide_ref):
    wide_ref[...] = jnp.full(wide_ref.shape, width_ref[0].astype(jnp.float32))


def stats_kernel(dosage_ref, sums_ref, brief_ref):
    acc = jnp.zeros((8, dosage_ref.shape[1]), jnp.float32)
    square = acc
    for k in range(0, dosage_ref.shape[0], ROWS):
        part = dosage_ref[pl.ds(k, ROWS)].astype(jnp.float32)
        part = part.reshape(ROWS // 8, 8, part.shape[1])
        acc = acc + jnp.sum(part, 0)
        square = square + jnp.sum(part * part, 0)
    row = lax.broadcasted_iota(jnp.int32, (8, 1), 0)
    first = jnp.sum(acc, 0, keepdims=True)
    second = jnp.sum(square, 0, keepdims=True)
    both = jnp.where(row == 0, first, second)
    sums_ref[...] = both
    brief_ref[...] = both[:2]


def finish(coded_ref, *columns):
    count = coded_ref.shape[1] % AUX or AUX
    lane = lax.broadcasted_iota(jnp.int32, (coded_ref.shape[0], count), 1)
    extra = jnp.zeros(lane.shape, jnp.float32)
    for k, column in enumerate(columns):
        extra = jnp.where(lane == k, column, extra)
    coded_ref[:, pl.ds(coded_ref.shape[1] - count, count)] = extra.astype(jnp.int32).astype(jnp.int16)


def fixed(value):
    return jnp.clip(jnp.round(value), -32767.0, 32767.0).astype(jnp.int32).astype(jnp.int16)


def scale_of(peak):
    exponent = jnp.floor(jnp.log2(jnp.maximum(peak, 1e-30)))
    return exponent, jnp.exp2(UNIT - exponent)


def encode(own_ref, coded_ref, shared_ref, width):
    exponent, scale = scale_of(jnp.max(jnp.abs(own_ref[...]), 1, keepdims=True))
    for k in range(0, own_ref.shape[1], CHUNK):
        value = fixed(own_ref[:, pl.ds(k, CHUNK)] * scale)
        coded_ref[:, pl.ds(k, CHUNK)] = value
        shared_ref[:, pl.ds(k, CHUNK)] = value
    finish(coded_ref, exponent, width)
    finish(shared_ref, exponent, width)


def split(value):
    exponent, scale = scale_of(jnp.abs(value))
    high = jnp.round(value * scale * 0.5)
    low = jnp.round((value * scale * 0.5 - high) * 2.0**UNIT)
    return exponent, high, low


def aux(coded_ref):
    count = coded_ref.shape[1] % AUX or AUX
    extra = coded_ref[:, pl.ds(coded_ref.shape[1] - count, count)].astype(jnp.int32).astype(jnp.float32)
    return [extra[:, k : k + 1] for k in range(4)]


def unit(exponent, use=True):
    return jnp.where(use, jnp.exp2(exponent - UNIT), 0.0)


def grid_values(coded_ref):
    size = coded_ref.shape[1] - AUX
    return coded_ref[:, pl.ds(0, size)].astype(jnp.int32).astype(jnp.float32) * unit(aux(coded_ref)[0])


def values(coded_ref, k):
    return coded_ref[:, pl.ds(k, CHUNK)].astype(jnp.int32).astype(jnp.float32)


def project(value, turned_ref, own_ref):
    rows = value.shape[0]
    terms = two_terms(value)
    for k in range(0, turned_ref.shape[1], CHUNK):
        both = jnp.dot(terms, turned_ref[:, pl.ds(k, CHUNK)], preferred_element_type=jnp.float32)
        own_ref[:, pl.ds(k, CHUNK)] = both[:rows] + both[rows:]


def first_kernel(samples, wide_ref, s0, s1, s2, s3, dosage_ref, start_ref, scaled_ref, turned_ref, own_ref, coded_ref, shared_ref):
    sums = total([s[0:2] for s in (s0, s1, s2, s3)])
    center = sums[0:1] / samples
    spread = sums[1:2] / samples - center * center
    factor = lax.rsqrt(spread + 1e-05)
    for k in range(0, dosage_ref.shape[0], CHUNK):
        part = dosage_ref[pl.ds(k, CHUNK)].astype(jnp.float32)
        part = ((part - center) * factor).astype(jnp.bfloat16)
        scaled_ref[pl.ds(k, CHUNK)] = part
        turned_ref[:, pl.ds(k, CHUNK)] = part.T
    project(start_ref[...], turned_ref, own_ref)
    encode(own_ref, coded_ref, shared_ref, wide_ref[0:1, 0:1])


def next_kernel(
    samples, wide_ref, z0, z1, z2, z3, start_ref, turned_ref, first_ref, parts_ref, own_ref, coded_ref, shared_ref
):
    first = total([grid_values(z) for z in (z0, z1, z2, z3)]) / samples
    first_ref[...] = first
    start = start_ref[...]
    lane = lax.broadcasted_iota(jnp.int32, parts_ref.shape, 1)
    parts = jnp.zeros(parts_ref.shape, jnp.float32)
    for k, (a, b) in enumerate(((start, start), (start, first), (first, first))):
        parts = jnp.where(lane == k, jnp.sum(a * b, 1, keepdims=True), parts)
    parts_ref[...] = parts
    project(first, turned_ref, own_ref)
    encode(own_ref, coded_ref, shared_ref, wide_ref[0:1, 0:1])


def place(count):
    index = lax.axis_index("snp")
    odd = (index & 1) == 1
    below, above = (index >= 2).astype(jnp.int32), (index < count - 2).astype(jnp.int32)
    side = jnp.where(odd, above, below) == 1
    across = jnp.where(odd, below, above) == 1
    return odd, side, across


def give_kernel(count, up, near_ref, own_ref, coded_ref, other_ref, sent_ref):
    odd, side, _ = place(count)
    exponent, width = aux(coded_ref)[:2]
    other_exponent, other_width = aux(other_ref)[:2]
    near = near_ref[0:1, 0:1]
    sent = jnp.maximum(exponent, other_exponent) + 1.0
    scale = jnp.exp2(UNIT - sent)
    rises = odd if up else jnp.logical_not(odd)
    known = True if up else side
    own_scale = jnp.where(jnp.where(rises, width, near) >= 2, scale, 0.0)
    other_scale = jnp.where(jnp.where(rises, other_width, near) >= 3, scale * unit(other_exponent, known), 0.0)
    for k in range(0, own_ref.shape[1], CHUNK):
        sent_ref[:, pl.ds(k, CHUNK)] = fixed(own_ref[:, pl.ds(k, CHUNK)] * own_scale + values(other_ref, k) * other_scale)
    finish(sent_ref, sent, width)


def window_kernel(samples, count, own_ref, coded_ref, partner_ref, next_ref, same_ref, cross_ref, scaled_ref, sent_ref):
    odd, side, across = place(count)
    width = aux(coded_ref)[1]
    partner_exponent, partner_width = aux(partner_ref)[:2]
    next_exponent, next_width = aux(next_ref)[:2]
    partner_scale = unit(partner_exponent, jnp.where(odd, partner_width, width) >= 1)
    next_scale = jnp.where(jnp.where(odd, width, next_width) >= 1, unit(next_exponent, side), 0.0)
    same_scale = unit(aux(same_ref)[0], side)
    cross_scale = unit(aux(cross_ref)[0], across)
    rows = own_ref.shape[0]
    acc = jnp.zeros((2 * rows, scaled_ref.shape[1]), jnp.float32)
    curved = jnp.zeros((rows, CHUNK), jnp.float32)
    for k in range(0, own_ref.shape[1], CHUNK):
        own = own_ref[:, pl.ds(k, CHUNK)]
        mixed = (
            own
            + values(partner_ref, k) * partner_scale
            + values(next_ref, k) * next_scale
            + values(same_ref, k) * same_scale
            + values(cross_ref, k) * cross_scale
        )
        acc = acc + jnp.dot(
            two_terms(mixed), scaled_ref[pl.ds(k, CHUNK)], preferred_element_type=jnp.float32
        )
        curved = curved + own * mixed
    z = acc[:rows] + acc[rows:]
    exponent, scale = scale_of(jnp.max(jnp.abs(z), 1, keepdims=True))
    sent_ref[:, pl.ds(0, z.shape[1])] = fixed(z * scale)
    finish(sent_ref, exponent, *split(jnp.sum(curved, 1, keepdims=True) / samples))


def collect_kernel(parts_ref, z0, z1, z2, z3, flat_ref):
    terms = []
    for z in (z0, z1, z2, z3):
        _, exponent, high, low = aux(z)
        terms.append((high + low * 2.0**-UNIT) * 2.0 * unit(exponent))
    lane = lax.broadcasted_iota(jnp.int32, parts_ref.shape, 1)
    parts = jnp.where(lane == 3, total(terms), parts_ref[...])
    filled = jnp.concatenate([parts, jnp.ones((AUX - parts.shape[0], AUX), jnp.float32)], 0)
    flat_ref[...] = filled.T[:8]


def last_kernel(samples, shrink_ref, p0, p1, p2, p3, z0, z1, z2, z3, start_ref, first_ref, effects_ref, residual_ref):
    rows = start_ref.shape[0]
    flat = total([p[0:4] for p in (p0, p1, p2, p3)])
    bb, bw, ww, wu = (flat[k : k + 1] for k in range(4))
    shrink = shrink_ref[...]
    ratio = bw / bb
    step = 1.0 / (ratio + shrink)
    square = step * step
    norm = square * (ww - ratio * bw)
    bend = norm / bb
    curve = square * (ratio * (ratio * bw - 2.0 * ww) + wu) + shrink * norm - bend * norm * (ratio + shrink)
    step2 = jnp.where(curve > 0, norm / curve, 0.0)
    lead = step * ratio + bend
    coefficients = (
        step + step2 * lead,
        -step2 * step,
        step * ratio - step2 * shrink * lead,
        -step - step2 * (lead - shrink * step),
        step2 * step,
    )
    row = lax.broadcasted_iota(jnp.int32, (AUX, AUX), 0)
    table = jnp.zeros((AUX, AUX), jnp.float32)
    for k, value in enumerate(coefficients):
        table = jnp.where(row == k, value, table)
    table = table.T[:rows]
    e_start, e_first, r_start, r_first, r_second = (table[:, k : k + 1] for k in range(5))
    start, first = start_ref[...], first_ref[...]
    effects_ref[...] = e_start * start + e_first * first
    second = total([grid_values(z) for z in (z0, z1, z2, z3)]) / samples
    residual_ref[...] = r_start * start + r_first * first + r_second * second


def snp_parts(value):
    count = lax.axis_size("snp")
    value = value + swap(value, "snp", 1)
    bit = 2
    while 4 * bit < count:
        value = jnp.pad(total([part[:4] for part in (value, *others(value, bit))]), ((0, 4), (0, 0)))
        bit *= 4
    if 2 * bit < count:
        return [value, *others(value, bit)]
    return [value, swap(value, "snp", bit ^ 1), jnp.zeros_like(value), jnp.zeros_like(value)]


def others(value, bit):
    return [swap(value[:rows], "snp", k ^ 1) for k, rows in ((bit, 4), (2 * bit, 6), (3 * bit, 8))]


def shards(dosage, band_width, marginal, penalty):
    groups, count = lax.axis_size("samp"), lax.axis_size("snp")
    local, size, rows = dosage.shape[0], dosage.shape[1], marginal.shape[1]
    samples = local * groups
    start = marginal.T
    shrink = jnp.pad(penalty, (0, AUX - rows), constant_values=1.0)[None]
    grid, own_shape = (rows, size), (rows, local)
    own_out, coded_out = (own_shape, jnp.float32), ((rows, local + AUX), jnp.int16)
    shared_out = ((rows, local + LESS), jnp.int16)

    sent_out = ((rows, size + AUX), jnp.int16)

    sums, brief = call(stats_kernel, [((8, size), jnp.float32), ((2, size), jnp.float32)], dosage)
    one, two, three = swap(brief, "samp", 1), swap(brief, "samp", 2), swap(sums, "samp", 3)
    one, band_width = lax.optimization_barrier((one, band_width))
    wide = pl.pallas_call(
        wide_kernel,
        out_shape=jax.ShapeDtypeStruct((8, size + AUX), jnp.float32),
        in_specs=[pl.BlockSpec(memory_space=pltpu.SMEM)],
        out_specs=pl.BlockSpec(memory_space=pltpu.VMEM),
        cost_estimate=pl.CostEstimate(flops=10**10, bytes_accessed=10**8, transcendentals=0),
    )(band_width)
    near = shifted(wide)
    two, three, near = lax.optimization_barrier((two, three, near))
    scaled, turned, own, coded, shared = call(
        functools.partial(first_kernel, samples),
        [(dosage.shape, jnp.bfloat16), (dosage.shape[::-1], jnp.bfloat16), own_out, coded_out, shared_out],
        wide, sums, one, two, three, dosage, start,
    )

    def give(up, *args):
        return call(functools.partial(give_kernel, count, up), [coded_out], near, *args)[0]

    def window(own, coded, shared):
        beside = adjacent(coded)
        partner = swap(shared, "snp", 1)
        cross = crossing(give(1, own, coded, partner), 1)
        same = crossing(give(0, own, coded, beside), 0)
        (z,) = call(
            functools.partial(window_kernel, samples, count), [sent_out],
            own, coded, partner, beside, same, cross, scaled,
        )
        return [z, *partners(z, "samp", 1, 2)]

    first, parts, own, coded, shared = call(
        functools.partial(next_kernel, samples),
        [(grid, jnp.float32), ((rows, AUX), jnp.float32), own_out, coded_out, shared_out],
        wide, *window(own, coded, shared), start, turned,
    )
    zs = window(own, coded, shared)
    (flat,) = call(collect_kernel, [((8, AUX), jnp.float32)], parts, *zs)
    parts = snp_parts(flat)
    effects, residual = call(
        functools.partial(last_kernel, samples),
        [(grid, jnp.float32), (grid, jnp.float32)],
        shrink, *parts, *zs, start, first,
    )
    return (effects.T, residual.T)


def solution(mesh):
    in_specs = (P("samp", "snp"), P("snp"), P("snp", None), P())
    out_specs = (P("snp", None), P("snp", None))
    return jax.shard_map(shards, mesh=mesh, in_specs=in_specs, out_specs=out_specs, check_vma=False)
```

```python
import functools

import jax
import jax.numpy as jnp
from jax import lax
from jax.experimental import pallas as pl
from jax.experimental.pallas import tpu as pltpu
from jax.sharding import PartitionSpec as P


AUX = 128
LESS = 96
CHUNK = 512
UNIT = 14
ROWS = 128


def swap(value, axis, bits):
    return lax.ppermute(value, axis, [(i, i ^ bits) for i in range(lax.axis_size(axis))])


def crossing(value, rising):
    count = lax.axis_size("snp")
    pairs = []
    for i in range(count):
        target = i + 2 if i % 2 == rising else i - 2
        pairs.append((i, target if 0 <= target < count else i ^ 1))
    return lax.ppermute(value, "snp", pairs)


def adjacent(value):
    rows, count = lax.axis_size("samp"), lax.axis_size("snp")
    pairs = []
    for row in range(rows):
        for i in range(count):
            target = i + 1 if i % 2 else i - 1
            inside = 0 <= target < count
            pairs.append((row * count + i, row * count + target if inside else (row ^ 1) * count + i))
    return lax.ppermute(value, ("samp", "snp"), pairs)


def shifted(value):
    count = lax.axis_size("snp")
    return lax.ppermute(value, "snp", [(i, (i + 2) % count) for i in range(count)])


def partners(value, axis, low, high):
    return [swap(value, axis, k) for k in (low, high, low + high)]


def total(parts):
    own, one, two, three = parts
    return (own + one) + (two + three)


def call(body, out_shape, *args):
    specs = [pl.BlockSpec(memory_space=pltpu.VMEM) for _ in args]
    outs = [jax.ShapeDtypeStruct(shape, kind) for shape, kind in out_shape]
    return pl.pallas_call(
        body,
        out_shape=outs,
        in_specs=specs,
        out_specs=[pl.BlockSpec(memory_space=pltpu.VMEM) for _ in outs],
        compiler_params=pltpu.CompilerParams(vmem_limit_bytes=32 << 20),
    )(*args)


def two_terms(value):
    high = value.astype(jnp.bfloat16)
    low = (value - high.astype(jnp.float32)).astype(jnp.bfloat16)
    return jnp.concatenate([high, low], 0)


def wide_kernel(width_ref, wide_ref):
    wide_ref[...] = jnp.full(wide_ref.shape, width_ref[0].astype(jnp.float32))


def stats_kernel(dosage_ref, sums_ref, brief_ref):
    acc = jnp.zeros((8, dosage_ref.shape[1]), jnp.float32)
    square = acc
    for k in range(0, dosage_ref.shape[0], ROWS):
        part = dosage_ref[pl.ds(k, ROWS)].astype(jnp.float32)
        part = part.reshape(ROWS // 8, 8, part.shape[1])
        acc = acc + jnp.sum(part, 0)
        square = square + jnp.sum(part * part, 0)
    row = lax.broadcasted_iota(jnp.int32, (8, 1), 0)
    first = jnp.sum(acc, 0, keepdims=True)
    second = jnp.sum(square, 0, keepdims=True)
    both = jnp.where(row == 0, first, second)
    sums_ref[...] = both
    brief_ref[...] = both[:2]


def finish(coded_ref, *columns):
    count = coded_ref.shape[1] % AUX or AUX
    lane = lax.broadcasted_iota(jnp.int32, (coded_ref.shape[0], count), 1)
    extra = jnp.zeros(lane.shape, jnp.float32)
    for k, column in enumerate(columns):
        extra = jnp.where(lane == k, column, extra)
    coded_ref[:, pl.ds(coded_ref.shape[1] - count, count)] = extra.astype(jnp.int32).astype(jnp.int16)


def fixed(value):
    return jnp.clip(jnp.round(value), -32767.0, 32767.0).astype(jnp.int32).astype(jnp.int16)


def scale_of(peak):
    exponent = jnp.floor(jnp.log2(jnp.maximum(peak, 1e-30)))
    return exponent, jnp.exp2(UNIT - exponent)


def encode(own_ref, coded_ref, shared_ref, width):
    exponent, scale = scale_of(jnp.max(jnp.abs(own_ref[...]), 1, keepdims=True))
    for k in range(0, own_ref.shape[1], CHUNK):
        value = fixed(own_ref[:, pl.ds(k, CHUNK)] * scale)
        coded_ref[:, pl.ds(k, CHUNK)] = value
        shared_ref[:, pl.ds(k, CHUNK)] = value
    finish(coded_ref, exponent, width)
    finish(shared_ref, exponent, width)


def split(value):
    exponent, scale = scale_of(jnp.abs(value))
    high = jnp.round(value * scale * 0.5)
    low = jnp.round((value * scale * 0.5 - high) * 2.0**UNIT)
    return exponent, high, low


def aux(coded_ref):
    count = coded_ref.shape[1] % AUX or AUX
    extra = coded_ref[:, pl.ds(coded_ref.shape[1] - count, count)].astype(jnp.int32).astype(jnp.float32)
    return [extra[:, k : k + 1] for k in range(4)]


def unit(exponent, use=True):
    return jnp.where(use, jnp.exp2(exponent - UNIT), 0.0)


def grid_values(coded_ref):
    size = coded_ref.shape[1] - (coded_ref.shape[1] % AUX or AUX)
    return coded_ref[:, pl.ds(0, size)].astype(jnp.int32).astype(jnp.float32) * unit(aux(coded_ref)[0])


def values(coded_ref, k):
    return coded_ref[:, pl.ds(k, CHUNK)].astype(jnp.int32).astype(jnp.float32)


def project(value, turned_ref, own_ref):
    rows = value.shape[0]
    terms = two_terms(value)
    for k in range(0, turned_ref.shape[1], CHUNK):
        both = jnp.dot(terms, turned_ref[:, pl.ds(k, CHUNK)], preferred_element_type=jnp.float32)
        own_ref[:, pl.ds(k, CHUNK)] = both[:rows] + both[rows:]


def first_kernel(samples, wide_ref, s0, s1, s2, s3, dosage_ref, start_ref, scaled_ref, turned_ref, own_ref, coded_ref, shared_ref):
    sums = total([s[0:2] for s in (s0, s1, s2, s3)])
    center = sums[0:1] / samples
    spread = sums[1:2] / samples - center * center
    factor = lax.rsqrt(spread + 1e-05)
    for k in range(0, dosage_ref.shape[0], CHUNK):
        part = dosage_ref[pl.ds(k, CHUNK)].astype(jnp.float32)
        part = ((part - center) * factor).astype(jnp.bfloat16)
        scaled_ref[pl.ds(k, CHUNK)] = part
        turned_ref[:, pl.ds(k, CHUNK)] = part.T
    project(start_ref[...], turned_ref, own_ref)
    encode(own_ref, coded_ref, shared_ref, wide_ref[0:1, 0:1])


def next_kernel(
    samples, wide_ref, z0, z1, z2, z3, start_ref, turned_ref, first_ref, parts_ref, own_ref, coded_ref, shared_ref
):
    first = total([grid_values(z) for z in (z0, z1, z2, z3)]) / samples
    first_ref[...] = first
    start = start_ref[...]
    lane = lax.broadcasted_iota(jnp.int32, parts_ref.shape, 1)
    parts = jnp.zeros(parts_ref.shape, jnp.float32)
    for k, (a, b) in enumerate(((start, start), (start, first), (first, first))):
        parts = jnp.where(lane == k, jnp.sum(a * b, 1, keepdims=True), parts)
    parts_ref[...] = parts
    project(first, turned_ref, own_ref)
    encode(own_ref, coded_ref, shared_ref, wide_ref[0:1, 0:1])


def place(count):
    index = lax.axis_index("snp")
    odd = (index & 1) == 1
    below, above = (index >= 2).astype(jnp.int32), (index < count - 2).astype(jnp.int32)
    side = jnp.where(odd, above, below) == 1
    across = jnp.where(odd, below, above) == 1
    return odd, side, across


def give_kernel(count, up, near_ref, own_ref, coded_ref, other_ref, sent_ref):
    odd, side, _ = place(count)
    exponent, width = aux(coded_ref)[:2]
    other_exponent, other_width = aux(other_ref)[:2]
    near = near_ref[0:1, 0:1]
    sent = jnp.maximum(exponent, other_exponent) + 1.0
    scale = jnp.exp2(UNIT - sent)
    rises = odd if up else jnp.logical_not(odd)
    known = True if up else side
    own_scale = jnp.where(jnp.where(rises, width, near) >= 2, scale, 0.0)
    other_scale = jnp.where(jnp.where(rises, other_width, near) >= 3, scale * unit(other_exponent, known), 0.0)
    for k in range(0, own_ref.shape[1], CHUNK):
        sent_ref[:, pl.ds(k, CHUNK)] = fixed(own_ref[:, pl.ds(k, CHUNK)] * own_scale + values(other_ref, k) * other_scale)
    finish(sent_ref, sent, width)


def window_kernel(samples, count, own_ref, coded_ref, partner_ref, next_ref, same_ref, cross_ref, scaled_ref, sent_ref, brief_ref):
    odd, side, across = place(count)
    width = aux(coded_ref)[1]
    partner_exponent, partner_width = aux(partner_ref)[:2]
    next_exponent, next_width = aux(next_ref)[:2]
    partner_scale = unit(partner_exponent, jnp.where(odd, partner_width, width) >= 1)
    next_scale = jnp.where(jnp.where(odd, width, next_width) >= 1, unit(next_exponent, side), 0.0)
    same_scale = unit(aux(same_ref)[0], side)
    cross_scale = unit(aux(cross_ref)[0], across)
    rows = own_ref.shape[0]
    acc = jnp.zeros((2 * rows, scaled_ref.shape[1]), jnp.float32)
    curved = jnp.zeros((rows, CHUNK), jnp.float32)
    for k in range(0, own_ref.shape[1], CHUNK):
        own = own_ref[:, pl.ds(k, CHUNK)]
        mixed = (
            own
            + values(partner_ref, k) * partner_scale
            + values(next_ref, k) * next_scale
            + values(same_ref, k) * same_scale
            + values(cross_ref, k) * cross_scale
        )
        acc = acc + jnp.dot(
            two_terms(mixed), scaled_ref[pl.ds(k, CHUNK)], preferred_element_type=jnp.float32
        )
        curved = curved + own * mixed
    z = acc[:rows] + acc[rows:]
    exponent, scale = scale_of(jnp.max(jnp.abs(z), 1, keepdims=True))
    columns = exponent, *split(jnp.sum(curved, 1, keepdims=True) / samples)
    z = fixed(z * scale)
    for ref in (sent_ref, brief_ref):
        ref[:, pl.ds(0, z.shape[1])] = z
        finish(ref, *columns)


def collect_kernel(parts_ref, z0, z1, z2, z3, flat_ref):
    terms = []
    for z in (z0, z1, z2, z3):
        _, exponent, high, low = aux(z)
        terms.append((high + low * 2.0**-UNIT) * 2.0 * unit(exponent))
    lane = lax.broadcasted_iota(jnp.int32, parts_ref.shape, 1)
    parts = jnp.where(lane == 3, total(terms), parts_ref[...])
    filled = jnp.concatenate([parts, jnp.ones((AUX - parts.shape[0], AUX), jnp.float32)], 0)
    flat_ref[...] = filled.T[:8]


def last_kernel(samples, shrink_ref, p0, p1, p2, p3, z0, z1, z2, z3, start_ref, first_ref, effects_ref, residual_ref):
    rows = start_ref.shape[0]
    flat = total([p[0:4] for p in (p0, p1, p2, p3)])
    bb, bw, ww, wu = (flat[k : k + 1] for k in range(4))
    shrink = shrink_ref[...]
    ratio = bw / bb
    step = 1.0 / (ratio + shrink)
    square = step * step
    norm = square * (ww - ratio * bw)
    bend = norm / bb
    curve = square * (ratio * (ratio * bw - 2.0 * ww) + wu) + shrink * norm - bend * norm * (ratio + shrink)
    step2 = jnp.where(curve > 0, norm / curve, 0.0)
    lead = step * ratio + bend
    coefficients = (
        step + step2 * lead,
        -step2 * step,
        step * ratio - step2 * shrink * lead,
        -step - step2 * (lead - shrink * step),
        step2 * step,
    )
    row = lax.broadcasted_iota(jnp.int32, (AUX, AUX), 0)
    table = jnp.zeros((AUX, AUX), jnp.float32)
    for k, value in enumerate(coefficients):
        table = jnp.where(row == k, value, table)
    table = table.T[:rows]
    e_start, e_first, r_start, r_first, r_second = (table[:, k : k + 1] for k in range(5))
    start, first = start_ref[...], first_ref[...]
    effects_ref[...] = e_start * start + e_first * first
    second = total([grid_values(z) for z in (z0, z1, z2, z3)]) / samples
    residual_ref[...] = r_start * start + r_first * first + r_second * second


def snp_parts(value):
    count = lax.axis_size("snp")
    value = value + swap(value, "snp", 1)
    bit = 2
    while 4 * bit < count:
        value = jnp.pad(total([part[:4] for part in (value, *others(value, bit))]), ((0, 4), (0, 0)))
        bit *= 4
    if 2 * bit < count:
        return [value, *others(value, bit)]
    return [value, swap(value, "snp", bit ^ 1), jnp.zeros_like(value), jnp.zeros_like(value)]


def others(value, bit):
    return [swap(value[:rows], "snp", k ^ 1) for k, rows in ((bit, 4), (2 * bit, 6), (3 * bit, 8))]


def shards(dosage, band_width, marginal, penalty):
    groups, count = lax.axis_size("samp"), lax.axis_size("snp")
    local, size, rows = dosage.shape[0], dosage.shape[1], marginal.shape[1]
    samples = local * groups
    start = marginal.T
    shrink = jnp.pad(penalty, (0, AUX - rows), constant_values=1.0)[None]
    grid, own_shape = (rows, size), (rows, local)
    own_out, coded_out = (own_shape, jnp.float32), ((rows, local + AUX), jnp.int16)
    shared_out = ((rows, local + LESS), jnp.int16)

    sent_out, brief_out = ((rows, size + AUX), jnp.int16), ((rows, size + LESS), jnp.int16)

    sums, brief = call(stats_kernel, [((8, size), jnp.float32), ((2, size), jnp.float32)], dosage)
    one, two, three = swap(brief, "samp", 1), swap(brief, "samp", 2), swap(sums, "samp", 3)
    one, band_width = lax.optimization_barrier((one, band_width))
    wide = pl.pallas_call(
        wide_kernel,
        out_shape=jax.ShapeDtypeStruct((8, size + AUX), jnp.float32),
        in_specs=[pl.BlockSpec(memory_space=pltpu.SMEM)],
        out_specs=pl.BlockSpec(memory_space=pltpu.VMEM),
        cost_estimate=pl.CostEstimate(flops=10**10, bytes_accessed=10**8, transcendentals=0),
    )(band_width)
    near = shifted(wide)
    two, three, near = lax.optimization_barrier((two, three, near))
    scaled, turned, own, coded, shared = call(
        functools.partial(first_kernel, samples),
        [(dosage.shape, jnp.bfloat16), (dosage.shape[::-1], jnp.bfloat16), own_out, coded_out, shared_out],
        wide, sums, one, two, three, dosage, start,
    )

    def give(up, *args):
        return call(functools.partial(give_kernel, count, up), [coded_out], near, *args)[0]

    def window(own, coded, shared):
        beside = adjacent(coded)
        partner = swap(shared, "snp", 1)
        cross = crossing(give(1, own, coded, partner), 1)
        same = crossing(give(0, own, coded, beside), 0)
        z, brief = call(
            functools.partial(window_kernel, samples, count), [sent_out, brief_out],
            own, coded, partner, beside, same, cross, scaled,
        )
        return [z, swap(brief, "samp", 1), swap(brief, "samp", 2), swap(z, "samp", 3)]

    first, parts, own, coded, shared = call(
        functools.partial(next_kernel, samples),
        [(grid, jnp.float32), ((rows, AUX), jnp.float32), own_out, coded_out, shared_out],
        wide, *window(own, coded, shared), start, turned,
    )
    zs = window(own, coded, shared)
    (flat,) = call(collect_kernel, [((8, AUX), jnp.float32)], parts, *zs)
    parts = snp_parts(flat)
    effects, residual = call(
        functools.partial(last_kernel, samples),
        [(grid, jnp.float32), (grid, jnp.float32)],
        shrink, *parts, *zs, start, first,
    )
    return (effects.T, residual.T)


def solution(mesh):
    in_specs = (P("samp", "snp"), P("snp"), P("snp", None), P())
    out_specs = (P("snp", None), P("snp", None))
    return jax.shard_map(shards, mesh=mesh, in_specs=in_specs, out_specs=out_specs, check_vma=False)
```

```python
import functools

import jax
import jax.numpy as jnp
from jax import lax
from jax.experimental import pallas as pl
from jax.experimental.pallas import tpu as pltpu
from jax.sharding import PartitionSpec as P


AUX = 128
LESS = 96
LEAST = 64
CHUNK = 512
UNIT = 14
ROWS = 256


def swap(value, axis, bits):
    return lax.ppermute(value, axis, [(i, i ^ bits) for i in range(lax.axis_size(axis))])


def crossing(value, rising):
    count = lax.axis_size("snp")
    pairs = []
    for i in range(count):
        target = i + 2 if i % 2 == rising else i - 2
        pairs.append((i, target if 0 <= target < count else i ^ 1))
    return lax.ppermute(value, "snp", pairs)


def adjacent(value):
    rows, count = lax.axis_size("samp"), lax.axis_size("snp")
    pairs = []
    for row in range(rows):
        for i in range(count):
            target = i + 1 if i % 2 else i - 1
            inside = 0 <= target < count
            pairs.append((row * count + i, row * count + target if inside else (row ^ 1) * count + i))
    return lax.ppermute(value, ("samp", "snp"), pairs)


def shifted(value):
    count = lax.axis_size("snp")
    return lax.ppermute(value, "snp", [(i, (i + 2) % count) for i in range(count)])


def partners(value, axis, low, high):
    return [swap(value, axis, k) for k in (low, high, low + high)]


def total(parts):
    own, one, two, three = parts
    return (own + one) + (two + three)


def call(body, out_shape, *args):
    specs = [pl.BlockSpec(memory_space=pltpu.VMEM) for _ in args]
    outs = [jax.ShapeDtypeStruct(shape, kind) for shape, kind in out_shape]
    return pl.pallas_call(
        body,
        out_shape=outs,
        in_specs=specs,
        out_specs=[pl.BlockSpec(memory_space=pltpu.VMEM) for _ in outs],
        compiler_params=pltpu.CompilerParams(vmem_limit_bytes=32 << 20),
    )(*args)


def two_terms(value):
    high = value.astype(jnp.bfloat16)
    low = (value - high.astype(jnp.float32)).astype(jnp.bfloat16)
    return jnp.concatenate([high, low], 0)


def wide_kernel(width_ref, wide_ref):
    wide_ref[...] = jnp.full(wide_ref.shape, width_ref[0].astype(jnp.float32))


def stats_kernel(dosage_ref, sums_ref, brief_ref):
    acc = jnp.zeros((8, dosage_ref.shape[1]), jnp.float32)
    square = acc
    for k in range(0, dosage_ref.shape[0], ROWS):
        part = dosage_ref[pl.ds(k, ROWS)].astype(jnp.float32)
        part = part.reshape(ROWS // 8, 8, part.shape[1])
        acc = acc + jnp.sum(part, 0)
        square = square + jnp.sum(part * part, 0)
    row = lax.broadcasted_iota(jnp.int32, (8, 1), 0)
    first = jnp.sum(acc, 0, keepdims=True)
    second = jnp.sum(square, 0, keepdims=True)
    both = jnp.where(row == 0, first, second)
    sums_ref[...] = both
    brief_ref[...] = both[:2]


def finish(coded_ref, *columns):
    count = coded_ref.shape[1] % AUX or AUX
    lane = lax.broadcasted_iota(jnp.int32, (coded_ref.shape[0], count), 1)
    extra = jnp.zeros(lane.shape, jnp.float32)
    for k, column in enumerate(columns):
        extra = jnp.where(lane == k, column, extra)
    coded_ref[:, pl.ds(coded_ref.shape[1] - count, count)] = extra.astype(jnp.int32).astype(jnp.int16)


def fixed(value):
    return jnp.clip(jnp.round(value), -32767.0, 32767.0).astype(jnp.int32).astype(jnp.int16)


def scale_of(peak):
    exponent = jnp.floor(jnp.log2(jnp.maximum(peak, 1e-30)))
    return exponent, jnp.exp2(UNIT - exponent)


def encode(own_ref, coded_ref, shared_ref, width):
    exponent, scale = scale_of(jnp.max(jnp.abs(own_ref[...]), 1, keepdims=True))
    for k in range(0, own_ref.shape[1], CHUNK):
        value = fixed(own_ref[:, pl.ds(k, CHUNK)] * scale)
        coded_ref[:, pl.ds(k, CHUNK)] = value
        shared_ref[:, pl.ds(k, CHUNK)] = value
    finish(coded_ref, exponent, width)
    finish(shared_ref, exponent, width)


def split(value):
    exponent, scale = scale_of(jnp.abs(value))
    high = jnp.round(value * scale * 0.5)
    low = jnp.round((value * scale * 0.5 - high) * 2.0**UNIT)
    return exponent, high, low


def aux(coded_ref):
    count = coded_ref.shape[1] % AUX or AUX
    extra = coded_ref[:, pl.ds(coded_ref.shape[1] - count, count)].astype(jnp.int32).astype(jnp.float32)
    return [extra[:, k : k + 1] for k in range(4)]


def unit(exponent, use=True):
    return jnp.where(use, jnp.exp2(exponent - UNIT), 0.0)


def grid_values(coded_ref):
    size = coded_ref.shape[1] - (coded_ref.shape[1] % AUX or AUX)
    return coded_ref[:, pl.ds(0, size)].astype(jnp.int32).astype(jnp.float32) * unit(aux(coded_ref)[0])


def values(coded_ref, k):
    return coded_ref[:, pl.ds(k, CHUNK)].astype(jnp.int32).astype(jnp.float32)


def project(value, turned_ref, own_ref):
    rows = value.shape[0]
    terms = two_terms(value)
    for k in range(0, turned_ref.shape[1], CHUNK):
        both = jnp.dot(terms, turned_ref[:, pl.ds(k, CHUNK)], preferred_element_type=jnp.float32)
        own_ref[:, pl.ds(k, CHUNK)] = both[:rows] + both[rows:]


def first_kernel(samples, wide_ref, s0, s1, s2, s3, dosage_ref, start_ref, scaled_ref, turned_ref, own_ref, coded_ref, shared_ref):
    sums = total([s[0:2] for s in (s0, s1, s2, s3)])
    center = sums[0:1] / samples
    spread = sums[1:2] / samples - center * center
    factor = lax.rsqrt(spread + 1e-05)
    for k in range(0, dosage_ref.shape[0], CHUNK):
        part = dosage_ref[pl.ds(k, CHUNK)].astype(jnp.float32)
        part = ((part - center) * factor).astype(jnp.bfloat16)
        scaled_ref[pl.ds(k, CHUNK)] = part
        turned_ref[:, pl.ds(k, CHUNK)] = part.T
    project(start_ref[...], turned_ref, own_ref)
    encode(own_ref, coded_ref, shared_ref, wide_ref[0:1, 0:1])


def next_kernel(
    samples, wide_ref, z0, z1, z2, z3, start_ref, turned_ref, first_ref, parts_ref, own_ref, coded_ref, shared_ref
):
    first = total([grid_values(z) for z in (z0, z1, z2, z3)]) / samples
    first_ref[...] = first
    start = start_ref[...]
    lane = lax.broadcasted_iota(jnp.int32, parts_ref.shape, 1)
    parts = jnp.zeros(parts_ref.shape, jnp.float32)
    for k, (a, b) in enumerate(((start, start), (start, first), (first, first))):
        parts = jnp.where(lane == k, jnp.sum(a * b, 1, keepdims=True), parts)
    parts_ref[...] = parts
    project(first, turned_ref, own_ref)
    encode(own_ref, coded_ref, shared_ref, wide_ref[0:1, 0:1])


def place(count):
    index = lax.axis_index("snp")
    odd = (index & 1) == 1
    below, above = (index >= 2).astype(jnp.int32), (index < count - 2).astype(jnp.int32)
    side = jnp.where(odd, above, below) == 1
    across = jnp.where(odd, below, above) == 1
    return odd, side, across


def give_kernel(count, up, near_ref, own_ref, coded_ref, other_ref, sent_ref):
    odd, side, _ = place(count)
    exponent, width = aux(coded_ref)[:2]
    other_exponent, other_width = aux(other_ref)[:2]
    near = near_ref[0:1, 0:1]
    sent = jnp.maximum(exponent, other_exponent) + 1.0
    scale = jnp.exp2(UNIT - sent)
    rises = odd if up else jnp.logical_not(odd)
    known = True if up else side
    own_scale = jnp.where(jnp.where(rises, width, near) >= 2, scale, 0.0)
    other_scale = jnp.where(jnp.where(rises, other_width, near) >= 3, scale * unit(other_exponent, known), 0.0)
    for k in range(0, own_ref.shape[1], CHUNK):
        sent_ref[:, pl.ds(k, CHUNK)] = fixed(own_ref[:, pl.ds(k, CHUNK)] * own_scale + values(other_ref, k) * other_scale)
    finish(sent_ref, sent, width)


def early_kernel(count, own_ref, coded_ref, partner_ref, next_ref, early_ref):
    odd, side, _ = place(count)
    width = aux(coded_ref)[1]
    partner_exponent, partner_width = aux(partner_ref)[:2]
    next_exponent, next_width = aux(next_ref)[:2]
    partner_scale = unit(partner_exponent, jnp.where(odd, partner_width, width) >= 1)
    next_scale = jnp.where(jnp.where(odd, width, next_width) >= 1, unit(next_exponent, side), 0.0)
    for k in range(0, own_ref.shape[1], CHUNK):
        early_ref[:, pl.ds(k, CHUNK)] = (
            own_ref[:, pl.ds(k, CHUNK)]
            + values(partner_ref, k) * partner_scale
            + values(next_ref, k) * next_scale
        )


def window_kernel(samples, count, own_ref, early_ref, same_ref, cross_ref, scaled_ref, *sent_refs):
    _, side, across = place(count)
    same_scale = unit(aux(same_ref)[0], side)
    cross_scale = unit(aux(cross_ref)[0], across)
    rows = own_ref.shape[0]
    acc = jnp.zeros((2 * rows, scaled_ref.shape[1]), jnp.float32)
    curved = jnp.zeros((rows, CHUNK), jnp.float32)
    for k in range(0, own_ref.shape[1], CHUNK):
        mixed = early_ref[:, pl.ds(k, CHUNK)] + values(same_ref, k) * same_scale + values(cross_ref, k) * cross_scale
        acc = acc + jnp.dot(
            two_terms(mixed), scaled_ref[pl.ds(k, CHUNK)], preferred_element_type=jnp.float32
        )
        curved = curved + own_ref[:, pl.ds(k, CHUNK)] * mixed
    z = acc[:rows] + acc[rows:]
    exponent, scale = scale_of(jnp.max(jnp.abs(z), 1, keepdims=True))
    columns = exponent, *split(jnp.sum(curved, 1, keepdims=True) / samples)
    z = fixed(z * scale)
    for ref in sent_refs:
        ref[:, pl.ds(0, z.shape[1])] = z
        finish(ref, *columns)


def collect_kernel(parts_ref, z0, z1, z2, z3, flat_ref):
    terms = []
    for z in (z0, z1, z2, z3):
        _, exponent, high, low = aux(z)
        terms.append((high + low * 2.0**-UNIT) * 2.0 * unit(exponent))
    lane = lax.broadcasted_iota(jnp.int32, parts_ref.shape, 1)
    parts = jnp.where(lane == 3, total(terms), parts_ref[...])
    filled = jnp.concatenate([parts, jnp.ones((AUX - parts.shape[0], AUX), jnp.float32)], 0)
    flat_ref[...] = filled.T[:8]


def second_kernel(samples, z0, z1, z2, z3, second_ref):
    second_ref[...] = total([grid_values(z) for z in (z0, z1, z2, z3)]) / samples


def last_kernel(shrink_ref, p0, p1, p2, p3, second_ref, start_ref, first_ref, effects_ref, residual_ref):
    rows = start_ref.shape[0]
    flat = total([p[0:4] for p in (p0, p1, p2, p3)])
    bb, bw, ww, wu = (flat[k : k + 1] for k in range(4))
    shrink = shrink_ref[...]
    ratio = bw / bb
    step = 1.0 / (ratio + shrink)
    square = step * step
    norm = square * (ww - ratio * bw)
    bend = norm / bb
    curve = square * (ratio * (ratio * bw - 2.0 * ww) + wu) + shrink * norm - bend * norm * (ratio + shrink)
    step2 = jnp.where(curve > 0, norm / curve, 0.0)
    lead = step * ratio + bend
    coefficients = (
        step + step2 * lead,
        -step2 * step,
        step * ratio - step2 * shrink * lead,
        -step - step2 * (lead - shrink * step),
        step2 * step,
    )
    row = lax.broadcasted_iota(jnp.int32, (AUX, AUX), 0)
    table = jnp.zeros((AUX, AUX), jnp.float32)
    for k, value in enumerate(coefficients):
        table = jnp.where(row == k, value, table)
    table = table.T[:rows]
    e_start, e_first, r_start, r_first, r_second = (table[:, k : k + 1] for k in range(5))
    start, first = start_ref[...], first_ref[...]
    effects_ref[...] = e_start * start + e_first * first
    residual_ref[...] = r_start * start + r_first * first + r_second * second_ref[...]


def snp_parts(value):
    count = lax.axis_size("snp")
    value = value + swap(value, "snp", 1)
    bit = 2
    while 4 * bit < count:
        value = jnp.pad(total([part[:4] for part in (value, *others(value, bit))]), ((0, 4), (0, 0)))
        bit *= 4
    if 2 * bit < count:
        return [value, *others(value, bit)]
    return [value, swap(value, "snp", bit ^ 1), jnp.zeros_like(value), jnp.zeros_like(value)]


def others(value, bit):
    return [swap(value[:rows], "snp", k ^ 1) for k, rows in ((bit, 4), (2 * bit, 6), (3 * bit, 8))]


def shards(dosage, band_width, marginal, penalty):
    groups, count = lax.axis_size("samp"), lax.axis_size("snp")
    local, size, rows = dosage.shape[0], dosage.shape[1], marginal.shape[1]
    samples = local * groups
    start = marginal.T
    shrink = jnp.pad(penalty, (0, AUX - rows), constant_values=1.0)[None]
    grid, own_shape = (rows, size), (rows, local)
    own_out, coded_out = (own_shape, jnp.float32), ((rows, local + AUX), jnp.int16)
    shared_out = ((rows, local + LESS), jnp.int16)

    sent_outs = [((rows, size + lanes), jnp.int16) for lanes in (AUX, LESS, LEAST)]

    sums, brief = call(stats_kernel, [((8, size), jnp.float32), ((2, size), jnp.float32)], dosage)
    one, two, three = swap(brief, "samp", 1), swap(brief, "samp", 2), swap(sums, "samp", 3)
    one, band_width = lax.optimization_barrier((one, band_width))
    wide = pl.pallas_call(
        wide_kernel,
        out_shape=jax.ShapeDtypeStruct((8, size + AUX), jnp.float32),
        in_specs=[pl.BlockSpec(memory_space=pltpu.SMEM)],
        out_specs=pl.BlockSpec(memory_space=pltpu.VMEM),
        cost_estimate=pl.CostEstimate(flops=10**10, bytes_accessed=10**8, transcendentals=0),
    )(band_width)
    near = shifted(wide)
    two, three, near = lax.optimization_barrier((two, three, near))
    scaled, turned, own, coded, shared = call(
        functools.partial(first_kernel, samples),
        [(dosage.shape, jnp.bfloat16), (dosage.shape[::-1], jnp.bfloat16), own_out, coded_out, shared_out],
        wide, sums, one, two, three, dosage, start,
    )

    def give(up, *args):
        return call(functools.partial(give_kernel, count, up), [coded_out], near, *args)[0]

    def window(own, coded, shared):
        beside = adjacent(coded)
        partner = swap(shared, "snp", 1)
        cross = crossing(give(1, own, coded, partner), 1)
        same = crossing(give(0, own, coded, beside), 0)
        (early,) = call(functools.partial(early_kernel, count), [own_out], own, coded, partner, beside)
        z, brief, least = call(
            functools.partial(window_kernel, samples, count), sent_outs,
            own, early, same, cross, scaled,
        )
        return [z, swap(brief, "samp", 1), swap(least, "samp", 2), swap(z, "samp", 3)]

    first, parts, own, coded, shared = call(
        functools.partial(next_kernel, samples),
        [(grid, jnp.float32), ((rows, AUX), jnp.float32), own_out, coded_out, shared_out],
        wide, *window(own, coded, shared), start, turned,
    )
    zs = window(own, coded, shared)
    (flat,) = call(collect_kernel, [((8, AUX), jnp.float32)], parts, *zs)
    parts = snp_parts(flat)
    (second,) = call(functools.partial(second_kernel, samples), [(grid, jnp.float32)], *zs)
    effects, residual = call(
        last_kernel,
        [(grid, jnp.float32), (grid, jnp.float32)],
        shrink, *parts, second, start, first,
    )
    return (effects.T, residual.T)


def solution(mesh):
    in_specs = (P("samp", "snp"), P("snp"), P("snp", None), P())
    out_specs = (P("snp", None), P("snp", None))
    return jax.shard_map(shards, mesh=mesh, in_specs=in_specs, out_specs=out_specs, check_vma=False)
```

```python
import functools

import jax
import jax.numpy as jnp
from jax import lax
from jax.experimental import pallas as pl
from jax.experimental.pallas import tpu as pltpu
from jax.sharding import PartitionSpec as P


AUX = 128
LESS = 96
LEAST = 64
CHUNK = 512
UNIT = 14
ROWS = 256


def swap(value, axis, bits):
    return lax.ppermute(value, axis, [(i, i ^ bits) for i in range(lax.axis_size(axis))])


def crossing(value, rising):
    count = lax.axis_size("snp")
    pairs = []
    for i in range(count):
        target = i + 2 if i % 2 == rising else i - 2
        pairs.append((i, target if 0 <= target < count else i ^ 1))
    return lax.ppermute(value, "snp", pairs)


def adjacent(value):
    rows, count = lax.axis_size("samp"), lax.axis_size("snp")
    pairs = []
    for row in range(rows):
        for i in range(count):
            target = i + 1 if i % 2 else i - 1
            inside = 0 <= target < count
            pairs.append((row * count + i, row * count + target if inside else (row ^ 1) * count + i))
    return lax.ppermute(value, ("samp", "snp"), pairs)


def shifted(value):
    count = lax.axis_size("snp")
    return lax.ppermute(value, "snp", [(i, (i + 2) % count) for i in range(count)])


def partners(value, axis, low, high):
    return [swap(value, axis, k) for k in (low, high, low + high)]


def total(parts):
    own, one, two, three = parts
    return (own + one) + (two + three)


def call(body, out_shape, *args):
    specs = [pl.BlockSpec(memory_space=pltpu.VMEM) for _ in args]
    outs = [jax.ShapeDtypeStruct(shape, kind) for shape, kind in out_shape]
    return pl.pallas_call(
        body,
        out_shape=outs,
        in_specs=specs,
        out_specs=[pl.BlockSpec(memory_space=pltpu.VMEM) for _ in outs],
        compiler_params=pltpu.CompilerParams(vmem_limit_bytes=32 << 20),
    )(*args)


def two_terms(value):
    high = value.astype(jnp.bfloat16)
    low = (value - high.astype(jnp.float32)).astype(jnp.bfloat16)
    return jnp.concatenate([high, low], 0)


def wide_kernel(width_ref, wide_ref):
    wide_ref[...] = jnp.full(wide_ref.shape, width_ref[0].astype(jnp.float32))


def stats_kernel(dosage_ref, sums_ref, brief_ref):
    acc = jnp.zeros((8, dosage_ref.shape[1]), jnp.float32)
    square = acc
    for k in range(0, dosage_ref.shape[0], ROWS):
        part = dosage_ref[pl.ds(k, ROWS)].astype(jnp.float32)
        part = part.reshape(ROWS // 8, 8, part.shape[1])
        acc = acc + jnp.sum(part, 0)
        square = square + jnp.sum(part * part, 0)
    row = lax.broadcasted_iota(jnp.int32, (8, 1), 0)
    first = jnp.sum(acc, 0, keepdims=True)
    second = jnp.sum(square, 0, keepdims=True)
    both = jnp.where(row == 0, first, second)
    sums_ref[...] = both
    brief_ref[...] = both[:2]


def finish(coded_ref, *columns):
    count = coded_ref.shape[1] % AUX or AUX
    lane = lax.broadcasted_iota(jnp.int32, (coded_ref.shape[0], count), 1)
    extra = jnp.zeros(lane.shape, jnp.float32)
    for k, column in enumerate(columns):
        extra = jnp.where(lane == k, column, extra)
    coded_ref[:, pl.ds(coded_ref.shape[1] - count, count)] = extra.astype(jnp.int32).astype(jnp.int16)


def fixed(value):
    return jnp.clip(jnp.round(value), -32767.0, 32767.0).astype(jnp.int32).astype(jnp.int16)


def scale_of(peak):
    exponent = jnp.floor(jnp.log2(jnp.maximum(peak, 1e-30)))
    return exponent, jnp.exp2(UNIT - exponent)


def encode(own_ref, coded_ref, shared_ref, width):
    exponent, scale = scale_of(jnp.max(jnp.abs(own_ref[...]), 1, keepdims=True))
    for k in range(0, own_ref.shape[1], CHUNK):
        value = fixed(own_ref[:, pl.ds(k, CHUNK)] * scale)
        coded_ref[:, pl.ds(k, CHUNK)] = value
        shared_ref[:, pl.ds(k, CHUNK)] = value
    finish(coded_ref, exponent, width)
    finish(shared_ref, exponent, width)


def split(value):
    exponent, scale = scale_of(jnp.abs(value))
    high = jnp.round(value * scale * 0.5)
    low = jnp.round((value * scale * 0.5 - high) * 2.0**UNIT)
    return exponent, high, low


def aux(coded_ref):
    count = coded_ref.shape[1] % AUX or AUX
    extra = coded_ref[:, pl.ds(coded_ref.shape[1] - count, count)].astype(jnp.int32).astype(jnp.float32)
    return [extra[:, k : k + 1] for k in range(4)]


def unit(exponent, use=True):
    return jnp.where(use, jnp.exp2(exponent - UNIT), 0.0)


def grid_values(coded_ref):
    size = coded_ref.shape[1] - (coded_ref.shape[1] % AUX or AUX)
    return coded_ref[:, pl.ds(0, size)].astype(jnp.int32).astype(jnp.float32) * unit(aux(coded_ref)[0])


def values(coded_ref, k):
    return coded_ref[:, pl.ds(k, CHUNK)].astype(jnp.int32).astype(jnp.float32)


def project(value, turned_ref, own_ref):
    rows = value.shape[0]
    terms = two_terms(value)
    for k in range(0, turned_ref.shape[1], CHUNK):
        both = jnp.dot(terms, turned_ref[:, pl.ds(k, CHUNK)], preferred_element_type=jnp.float32)
        own_ref[:, pl.ds(k, CHUNK)] = both[:rows] + both[rows:]


def first_kernel(samples, wide_ref, s0, s1, s2, s3, dosage_ref, start_ref, scaled_ref, own_ref, coded_ref, shared_ref):
    sums = total([s[0:2] for s in (s0, s1, s2, s3)])
    center = sums[0:1] / samples
    spread = sums[1:2] / samples - center * center
    factor = lax.rsqrt(spread + 1e-05)
    for k in range(0, dosage_ref.shape[0], CHUNK):
        part = dosage_ref[pl.ds(k, CHUNK)].astype(jnp.float32)
        scaled_ref[pl.ds(k, CHUNK)] = ((part - center) * factor).astype(jnp.bfloat16)
    terms = two_terms(start_ref[...])
    rows = start_ref.shape[0]
    for k in range(0, dosage_ref.shape[0], CHUNK):
        both = lax.dot_general(
            terms, scaled_ref[pl.ds(k, CHUNK)], (((1,), (1,)), ((), ())), preferred_element_type=jnp.float32
        )
        own_ref[:, pl.ds(k, CHUNK)] = both[:rows] + both[rows:]
    encode(own_ref, coded_ref, shared_ref, wide_ref[0:1, 0:1])


def turn_kernel(scaled_ref, turned_ref):
    for k in range(0, scaled_ref.shape[0], CHUNK):
        turned_ref[:, pl.ds(k, CHUNK)] = scaled_ref[pl.ds(k, CHUNK)].T


def next_kernel(
    samples, wide_ref, z0, z1, z2, z3, start_ref, turned_ref, first_ref, parts_ref, own_ref, coded_ref, shared_ref
):
    first = total([grid_values(z) for z in (z0, z1, z2, z3)]) / samples
    first_ref[...] = first
    start = start_ref[...]
    lane = lax.broadcasted_iota(jnp.int32, parts_ref.shape, 1)
    parts = jnp.zeros(parts_ref.shape, jnp.float32)
    for k, (a, b) in enumerate(((start, start), (start, first), (first, first))):
        parts = jnp.where(lane == k, jnp.sum(a * b, 1, keepdims=True), parts)
    parts_ref[...] = parts
    project(first, turned_ref, own_ref)
    encode(own_ref, coded_ref, shared_ref, wide_ref[0:1, 0:1])


def place(count):
    index = lax.axis_index("snp")
    odd = (index & 1) == 1
    below, above = (index >= 2).astype(jnp.int32), (index < count - 2).astype(jnp.int32)
    side = jnp.where(odd, above, below) == 1
    across = jnp.where(odd, below, above) == 1
    return odd, side, across


def give_kernel(count, up, near_ref, own_ref, coded_ref, other_ref, sent_ref):
    odd, side, _ = place(count)
    exponent, width = aux(coded_ref)[:2]
    other_exponent, other_width = aux(other_ref)[:2]
    near = near_ref[0:1, 0:1]
    sent = jnp.maximum(exponent, other_exponent) + 1.0
    scale = jnp.exp2(UNIT - sent)
    rises = odd if up else jnp.logical_not(odd)
    known = True if up else side
    own_scale = jnp.where(jnp.where(rises, width, near) >= 2, scale, 0.0)
    other_scale = jnp.where(jnp.where(rises, other_width, near) >= 3, scale * unit(other_exponent, known), 0.0)
    for k in range(0, own_ref.shape[1], CHUNK):
        sent_ref[:, pl.ds(k, CHUNK)] = fixed(own_ref[:, pl.ds(k, CHUNK)] * own_scale + values(other_ref, k) * other_scale)
    finish(sent_ref, sent, width)


def early_kernel(count, own_ref, coded_ref, partner_ref, next_ref, early_ref):
    odd, side, _ = place(count)
    width = aux(coded_ref)[1]
    partner_exponent, partner_width = aux(partner_ref)[:2]
    next_exponent, next_width = aux(next_ref)[:2]
    partner_scale = unit(partner_exponent, jnp.where(odd, partner_width, width) >= 1)
    next_scale = jnp.where(jnp.where(odd, width, next_width) >= 1, unit(next_exponent, side), 0.0)
    for k in range(0, own_ref.shape[1], CHUNK):
        early_ref[:, pl.ds(k, CHUNK)] = (
            own_ref[:, pl.ds(k, CHUNK)]
            + values(partner_ref, k) * partner_scale
            + values(next_ref, k) * next_scale
        )


def window_kernel(samples, count, last, own_ref, early_ref, same_ref, cross_ref, scaled_ref, *sent_refs):
    _, side, across = place(count)
    same_scale = unit(aux(same_ref)[0], side)
    cross_scale = unit(aux(cross_ref)[0], across)
    rows = own_ref.shape[0]
    acc = jnp.zeros((2 * rows, scaled_ref.shape[1]), jnp.float32)
    curved = jnp.zeros((rows, CHUNK), jnp.float32)
    for k in range(0, own_ref.shape[1], CHUNK):
        mixed = early_ref[:, pl.ds(k, CHUNK)] + values(same_ref, k) * same_scale + values(cross_ref, k) * cross_scale
        acc = acc + jnp.dot(
            two_terms(mixed), scaled_ref[pl.ds(k, CHUNK)], preferred_element_type=jnp.float32
        )
        if last:
            curved = curved + own_ref[:, pl.ds(k, CHUNK)] * mixed
    z = acc[:rows] + acc[rows:]
    exponent, scale = scale_of(jnp.max(jnp.abs(z), 1, keepdims=True))
    columns = (exponent, *split(jnp.sum(curved, 1, keepdims=True) / samples)) if last else (exponent,)
    z = fixed(z * scale)
    for ref in sent_refs:
        ref[:, pl.ds(0, z.shape[1])] = z
        finish(ref, *columns)


def collect_kernel(parts_ref, z0, z1, z2, z3, flat_ref):
    terms = []
    for z in (z0, z1, z2, z3):
        _, exponent, high, low = aux(z)
        terms.append((high + low * 2.0**-UNIT) * 2.0 * unit(exponent))
    lane = lax.broadcasted_iota(jnp.int32, parts_ref.shape, 1)
    parts = jnp.where(lane == 3, total(terms), parts_ref[...])
    filled = jnp.concatenate([parts, jnp.ones((AUX - parts.shape[0], AUX), jnp.float32)], 0)
    flat_ref[...] = filled.T[:8]


def second_kernel(samples, z0, z1, z2, z3, second_ref):
    second_ref[...] = total([grid_values(z) for z in (z0, z1, z2, z3)]) / samples


def last_kernel(shrink_ref, p0, p1, p2, p3, second_ref, start_ref, first_ref, effects_ref, residual_ref):
    rows = start_ref.shape[0]
    flat = total([p[0:4] for p in (p0, p1, p2, p3)])
    bb, bw, ww, wu = (flat[k : k + 1] for k in range(4))
    shrink = shrink_ref[...]
    ratio = bw / bb
    step = 1.0 / (ratio + shrink)
    square = step * step
    norm = square * (ww - ratio * bw)
    bend = norm / bb
    curve = square * (ratio * (ratio * bw - 2.0 * ww) + wu) + shrink * norm - bend * norm * (ratio + shrink)
    step2 = jnp.where(curve > 0, norm / curve, 0.0)
    lead = step * ratio + bend
    coefficients = (
        step + step2 * lead,
        -step2 * step,
        step * ratio - step2 * shrink * lead,
        -step - step2 * (lead - shrink * step),
        step2 * step,
    )
    row = lax.broadcasted_iota(jnp.int32, (AUX, AUX), 0)
    table = jnp.zeros((AUX, AUX), jnp.float32)
    for k, value in enumerate(coefficients):
        table = jnp.where(row == k, value, table)
    table = table.T[:rows]
    e_start, e_first, r_start, r_first, r_second = (table[:, k : k + 1] for k in range(5))
    start, first = start_ref[...], first_ref[...]
    effects_ref[...] = e_start * start + e_first * first
    residual_ref[...] = r_start * start + r_first * first + r_second * second_ref[...]


def snp_parts(value):
    count = lax.axis_size("snp")
    value = value + swap(value, "snp", 1)
    bit = 2
    while 4 * bit < count:
        value = jnp.pad(total([part[:4] for part in (value, *others(value, bit))]), ((0, 4), (0, 0)))
        bit *= 4
    if 2 * bit < count:
        return [value, *others(value, bit)]
    return [value, swap(value, "snp", bit ^ 1), jnp.zeros_like(value), jnp.zeros_like(value)]


def others(value, bit):
    return [swap(value[:rows], "snp", k ^ 1) for k, rows in ((bit, 4), (2 * bit, 6), (3 * bit, 8))]


def shards(dosage, band_width, marginal, penalty):
    groups, count = lax.axis_size("samp"), lax.axis_size("snp")
    local, size, rows = dosage.shape[0], dosage.shape[1], marginal.shape[1]
    samples = local * groups
    start = marginal.T
    shrink = jnp.pad(penalty, (0, AUX - rows), constant_values=1.0)[None]
    grid, own_shape = (rows, size), (rows, local)
    own_out, coded_out = (own_shape, jnp.float32), ((rows, local + AUX), jnp.int16)
    shared_out = ((rows, local + LESS), jnp.int16)

    sent_outs = [((rows, size + lanes), jnp.int16) for lanes in (AUX, LESS, LEAST)]

    sums, brief = call(stats_kernel, [((8, size), jnp.float32), ((2, size), jnp.float32)], dosage)
    one, two, three = swap(brief, "samp", 1), swap(brief, "samp", 2), swap(sums, "samp", 3)
    one, band_width = lax.optimization_barrier((one, band_width))
    wide = pl.pallas_call(
        wide_kernel,
        out_shape=jax.ShapeDtypeStruct((8, size + AUX), jnp.float32),
        in_specs=[pl.BlockSpec(memory_space=pltpu.SMEM)],
        out_specs=pl.BlockSpec(memory_space=pltpu.VMEM),
        cost_estimate=pl.CostEstimate(flops=10**10, bytes_accessed=10**8, transcendentals=0),
    )(band_width)
    near = shifted(wide)
    two, three, near = lax.optimization_barrier((two, three, near))
    scaled, own, coded, shared = call(
        functools.partial(first_kernel, samples),
        [(dosage.shape, jnp.bfloat16), own_out, coded_out, shared_out],
        wide, sums, one, two, three, dosage, start,
    )

    (turned,) = call(turn_kernel, [(dosage.shape[::-1], jnp.bfloat16)], scaled)

    def give(up, *args):
        return call(functools.partial(give_kernel, count, up), [coded_out], near, *args)[0]

    def window(own, coded, shared, last):
        beside = adjacent(coded)
        partner = swap(shared, "snp", 1)
        cross = crossing(give(1, own, coded, partner), 1)
        same = crossing(give(0, own, coded, beside), 0)
        (early,) = call(functools.partial(early_kernel, count), [own_out], own, coded, partner, beside)
        z, brief, least = call(
            functools.partial(window_kernel, samples, count, last), sent_outs,
            own, early, same, cross, scaled,
        )
        return [z, swap(brief, "samp", 1), swap(least, "samp", 2), swap(z, "samp", 3)]

    first, parts, own, coded, shared = call(
        functools.partial(next_kernel, samples),
        [(grid, jnp.float32), ((rows, AUX), jnp.float32), own_out, coded_out, shared_out],
        wide, *window(own, coded, shared, False), start, turned,
    )
    zs = window(own, coded, shared, True)
    (flat,) = call(collect_kernel, [((8, AUX), jnp.float32)], parts, *zs)
    parts = snp_parts(flat)
    (second,) = call(functools.partial(second_kernel, samples), [(grid, jnp.float32)], *zs)
    effects, residual = call(
        last_kernel,
        [(grid, jnp.float32), (grid, jnp.float32)],
        shrink, *parts, second, start, first,
    )
    return (effects.T, residual.T)


def solution(mesh):
    in_specs = (P("samp", "snp"), P("snp"), P("snp", None), P())
    out_specs = (P("snp", None), P("snp", None))
    return jax.shard_map(shards, mesh=mesh, in_specs=in_specs, out_specs=out_specs, check_vma=False)
```

```python
import functools

import jax
import jax.numpy as jnp
from jax import lax
from jax.experimental import pallas as pl
from jax.experimental.pallas import tpu as pltpu
from jax.sharding import PartitionSpec as P


AUX = 128
LESS = 96
LEAST = 64
CHUNK = 512
UNIT = 14
ROWS = 256


def swap(value, axis, bits):
    return lax.ppermute(value, axis, [(i, i ^ bits) for i in range(lax.axis_size(axis))])


def crossing(value, rising):
    count = lax.axis_size("snp")
    pairs = []
    for i in range(count):
        target = i + 2 if i % 2 == rising else i - 2
        pairs.append((i, target if 0 <= target < count else i ^ 1))
    return lax.ppermute(value, "snp", pairs)


def adjacent(value):
    rows, count = lax.axis_size("samp"), lax.axis_size("snp")
    pairs = []
    for row in range(rows):
        for i in range(count):
            target = i + 1 if i % 2 else i - 1
            inside = 0 <= target < count
            pairs.append((row * count + i, row * count + target if inside else (row ^ 1) * count + i))
    return lax.ppermute(value, ("samp", "snp"), pairs)


def shifted(value):
    count = lax.axis_size("snp")
    return lax.ppermute(value, "snp", [(i, (i + 2) % count) for i in range(count)])


def partners(value, axis, low, high):
    return [swap(value, axis, k) for k in (low, high, low + high)]


def total(parts):
    own, one, two, three = parts
    return (own + one) + (two + three)


def call(body, out_shape, *args):
    specs = [pl.BlockSpec(memory_space=pltpu.VMEM) for _ in args]
    outs = [jax.ShapeDtypeStruct(shape, kind) for shape, kind in out_shape]
    return pl.pallas_call(
        body,
        out_shape=outs,
        in_specs=specs,
        out_specs=[pl.BlockSpec(memory_space=pltpu.VMEM) for _ in outs],
        compiler_params=pltpu.CompilerParams(vmem_limit_bytes=32 << 20),
    )(*args)


def two_terms(value):
    high = value.astype(jnp.bfloat16)
    low = (value - high.astype(jnp.float32)).astype(jnp.bfloat16)
    return jnp.concatenate([high, low], 0)


def wide_kernel(width_ref, wide_ref):
    wide_ref[...] = jnp.full(wide_ref.shape, width_ref[0].astype(jnp.float32))


def stats_kernel(dosage_ref, sums_ref, brief_ref):
    acc = jnp.zeros((8, dosage_ref.shape[1]), jnp.float32)
    square = acc
    for k in range(0, dosage_ref.shape[0], ROWS):
        part = dosage_ref[pl.ds(k, ROWS)].astype(jnp.float32)
        part = part.reshape(ROWS // 8, 8, part.shape[1])
        acc = acc + jnp.sum(part, 0)
        square = square + jnp.sum(part * part, 0)
    row = lax.broadcasted_iota(jnp.int32, (8, 1), 0)
    first = jnp.sum(acc, 0, keepdims=True)
    second = jnp.sum(square, 0, keepdims=True)
    both = jnp.where(row == 0, first, second)
    sums_ref[...] = both
    brief_ref[...] = both[:2]


def finish(coded_ref, *columns):
    count = coded_ref.shape[1] % AUX or AUX
    lane = lax.broadcasted_iota(jnp.int32, (coded_ref.shape[0], count), 1)
    extra = jnp.zeros(lane.shape, jnp.float32)
    for k, column in enumerate(columns):
        extra = jnp.where(lane == k, column, extra)
    coded_ref[:, pl.ds(coded_ref.shape[1] - count, count)] = extra.astype(jnp.int32).astype(jnp.int16)


def fixed(value):
    return jnp.clip(jnp.round(value), -32767.0, 32767.0).astype(jnp.int32).astype(jnp.int16)


def scale_of(peak):
    exponent = jnp.floor(jnp.log2(jnp.maximum(peak, 1e-30)))
    return exponent, jnp.exp2(UNIT - exponent)


def encode(own_ref, coded_ref, shared_ref, width):
    exponent, scale = scale_of(jnp.max(jnp.abs(own_ref[...]), 1, keepdims=True))
    for k in range(0, own_ref.shape[1], CHUNK):
        value = fixed(own_ref[:, pl.ds(k, CHUNK)] * scale)
        coded_ref[:, pl.ds(k, CHUNK)] = value
        shared_ref[:, pl.ds(k, CHUNK)] = value
    finish(coded_ref, exponent, width)
    finish(shared_ref, exponent, width)


def split(value):
    exponent, scale = scale_of(jnp.abs(value))
    high = jnp.round(value * scale * 0.5)
    low = jnp.round((value * scale * 0.5 - high) * 2.0**UNIT)
    return exponent, high, low


def aux(coded_ref):
    count = coded_ref.shape[1] % AUX or AUX
    extra = coded_ref[:, pl.ds(coded_ref.shape[1] - count, count)].astype(jnp.int32).astype(jnp.float32)
    return [extra[:, k : k + 1] for k in range(4)]


def unit(exponent, use=True):
    return jnp.where(use, jnp.exp2(exponent - UNIT), 0.0)


def grid_values(coded_ref):
    size = coded_ref.shape[1] - (coded_ref.shape[1] % AUX or AUX)
    return coded_ref[:, pl.ds(0, size)].astype(jnp.int32).astype(jnp.float32) * unit(aux(coded_ref)[0])


def values(coded_ref, k):
    return coded_ref[:, pl.ds(k, CHUNK)].astype(jnp.int32).astype(jnp.float32)


def project(value, turned_ref, own_ref):
    rows = value.shape[0]
    terms = two_terms(value)
    for k in range(0, turned_ref.shape[1], CHUNK):
        both = jnp.dot(terms, turned_ref[:, pl.ds(k, CHUNK)], preferred_element_type=jnp.float32)
        own_ref[:, pl.ds(k, CHUNK)] = both[:rows] + both[rows:]


def first_kernel(samples, wide_ref, s0, s1, s2, s3, dosage_ref, start_ref, scaled_ref, own_ref, coded_ref, shared_ref):
    sums = total([s[0:2] for s in (s0, s1, s2, s3)])
    center = sums[0:1] / samples
    spread = sums[1:2] / samples - center * center
    factor = lax.rsqrt(spread + 1e-05)
    for k in range(0, dosage_ref.shape[0], CHUNK):
        part = dosage_ref[pl.ds(k, CHUNK)].astype(jnp.float32)
        scaled_ref[pl.ds(k, CHUNK)] = ((part - center) * factor).astype(jnp.bfloat16)
    terms = two_terms(start_ref[...])
    rows = start_ref.shape[0]
    for k in range(0, dosage_ref.shape[0], CHUNK):
        both = lax.dot_general(
            terms, scaled_ref[pl.ds(k, CHUNK)], (((1,), (1,)), ((), ())), preferred_element_type=jnp.float32
        )
        own_ref[:, pl.ds(k, CHUNK)] = both[:rows] + both[rows:]
    encode(own_ref, coded_ref, shared_ref, wide_ref[0:1, 0:1])


def turn_kernel(scaled_ref, turned_ref):
    for k in range(0, scaled_ref.shape[0], CHUNK):
        turned_ref[:, pl.ds(k, CHUNK)] = scaled_ref[pl.ds(k, CHUNK)].T


def parts_kernel(start_ref, first_ref, parts_ref):
    first = first_ref[...]
    start = start_ref[...]
    lane = lax.broadcasted_iota(jnp.int32, parts_ref.shape, 1)
    parts = jnp.zeros(parts_ref.shape, jnp.float32)
    for k, (a, b) in enumerate(((start, start), (start, first), (first, first))):
        parts = jnp.where(lane == k, jnp.sum(a * b, 1, keepdims=True), parts)
    parts_ref[...] = parts


def next_kernel(
    samples, wide_ref, z0, z1, z2, z3, turned_ref, first_ref, own_ref, coded_ref, shared_ref
):
    first = total([grid_values(z) for z in (z0, z1, z2, z3)]) / samples
    first_ref[...] = first
    project(first, turned_ref, own_ref)
    encode(own_ref, coded_ref, shared_ref, wide_ref[0:1, 0:1])


def place(count):
    index = lax.axis_index("snp")
    odd = (index & 1) == 1
    below, above = (index >= 2).astype(jnp.int32), (index < count - 2).astype(jnp.int32)
    side = jnp.where(odd, above, below) == 1
    across = jnp.where(odd, below, above) == 1
    return odd, side, across


def give_kernel(count, up, near_ref, own_ref, coded_ref, other_ref, sent_ref):
    odd, side, _ = place(count)
    exponent, width = aux(coded_ref)[:2]
    other_exponent, other_width = aux(other_ref)[:2]
    near = near_ref[0:1, 0:1]
    sent = jnp.maximum(exponent, other_exponent) + 1.0
    scale = jnp.exp2(UNIT - sent)
    rises = odd if up else jnp.logical_not(odd)
    known = True if up else side
    own_scale = jnp.where(jnp.where(rises, width, near) >= 2, scale, 0.0)
    other_scale = jnp.where(jnp.where(rises, other_width, near) >= 3, scale * unit(other_exponent, known), 0.0)
    for k in range(0, own_ref.shape[1], CHUNK):
        sent_ref[:, pl.ds(k, CHUNK)] = fixed(own_ref[:, pl.ds(k, CHUNK)] * own_scale + values(other_ref, k) * other_scale)
    finish(sent_ref, sent, width)


def early_kernel(count, own_ref, coded_ref, partner_ref, next_ref, early_ref):
    odd, side, _ = place(count)
    width = aux(coded_ref)[1]
    partner_exponent, partner_width = aux(partner_ref)[:2]
    next_exponent, next_width = aux(next_ref)[:2]
    partner_scale = unit(partner_exponent, jnp.where(odd, partner_width, width) >= 1)
    next_scale = jnp.where(jnp.where(odd, width, next_width) >= 1, unit(next_exponent, side), 0.0)
    for k in range(0, own_ref.shape[1], CHUNK):
        early_ref[:, pl.ds(k, CHUNK)] = (
            own_ref[:, pl.ds(k, CHUNK)]
            + values(partner_ref, k) * partner_scale
            + values(next_ref, k) * next_scale
        )


def window_kernel(samples, count, last, own_ref, early_ref, same_ref, cross_ref, scaled_ref, *sent_refs):
    _, side, across = place(count)
    same_scale = unit(aux(same_ref)[0], side)
    cross_scale = unit(aux(cross_ref)[0], across)
    rows = own_ref.shape[0]
    acc = jnp.zeros((2 * rows, scaled_ref.shape[1]), jnp.float32)
    curved = jnp.zeros((rows, CHUNK), jnp.float32)
    for k in range(0, own_ref.shape[1], CHUNK):
        mixed = early_ref[:, pl.ds(k, CHUNK)] + values(same_ref, k) * same_scale + values(cross_ref, k) * cross_scale
        acc = acc + jnp.dot(
            two_terms(mixed), scaled_ref[pl.ds(k, CHUNK)], preferred_element_type=jnp.float32
        )
        if last:
            curved = curved + own_ref[:, pl.ds(k, CHUNK)] * mixed
    z = acc[:rows] + acc[rows:]
    exponent, scale = scale_of(jnp.max(jnp.abs(z), 1, keepdims=True))
    columns = (exponent, *split(jnp.sum(curved, 1, keepdims=True) / samples)) if last else (exponent,)
    z = fixed(z * scale)
    for ref in sent_refs:
        ref[:, pl.ds(0, z.shape[1])] = z
        finish(ref, *columns)


def collect_kernel(parts_ref, z0, z1, z2, z3, flat_ref):
    terms = []
    for z in (z0, z1, z2, z3):
        _, exponent, high, low = aux(z)
        terms.append((high + low * 2.0**-UNIT) * 2.0 * unit(exponent))
    lane = lax.broadcasted_iota(jnp.int32, parts_ref.shape, 1)
    parts = jnp.where(lane == 3, total(terms), parts_ref[...])
    filled = jnp.concatenate([parts, jnp.ones((AUX - parts.shape[0], AUX), jnp.float32)], 0)
    flat_ref[...] = filled.T[:8]


def second_kernel(samples, z0, z1, z2, z3, second_ref):
    second_ref[...] = total([grid_values(z) for z in (z0, z1, z2, z3)]) / samples


def last_kernel(shrink_ref, p0, p1, p2, p3, second_ref, start_ref, first_ref, effects_ref, residual_ref):
    rows = start_ref.shape[0]
    flat = total([p[0:4] for p in (p0, p1, p2, p3)])
    bb, bw, ww, wu = (flat[k : k + 1] for k in range(4))
    shrink = shrink_ref[...]
    ratio = bw / bb
    step = 1.0 / (ratio + shrink)
    square = step * step
    norm = square * (ww - ratio * bw)
    bend = norm / bb
    curve = square * (ratio * (ratio * bw - 2.0 * ww) + wu) + shrink * norm - bend * norm * (ratio + shrink)
    step2 = jnp.where(curve > 0, norm / curve, 0.0)
    lead = step * ratio + bend
    coefficients = (
        step + step2 * lead,
        -step2 * step,
        step * ratio - step2 * shrink * lead,
        -step - step2 * (lead - shrink * step),
        step2 * step,
    )
    row = lax.broadcasted_iota(jnp.int32, (AUX, AUX), 0)
    table = jnp.zeros((AUX, AUX), jnp.float32)
    for k, value in enumerate(coefficients):
        table = jnp.where(row == k, value, table)
    table = table.T[:rows]
    e_start, e_first, r_start, r_first, r_second = (table[:, k : k + 1] for k in range(5))
    start, first = start_ref[...], first_ref[...]
    effects_ref[...] = e_start * start + e_first * first
    residual_ref[...] = r_start * start + r_first * first + r_second * second_ref[...]


def snp_parts(value):
    count = lax.axis_size("snp")
    value = value + swap(value, "snp", 1)
    bit = 2
    while 4 * bit < count:
        value = jnp.pad(total([part[:4] for part in (value, *others(value, bit))]), ((0, 4), (0, 0)))
        bit *= 4
    if 2 * bit < count:
        return [value, *others(value, bit)]
    return [value, swap(value, "snp", bit ^ 1), jnp.zeros_like(value), jnp.zeros_like(value)]


def others(value, bit):
    return [swap(value[:rows], "snp", k ^ 1) for k, rows in ((bit, 4), (2 * bit, 6), (3 * bit, 8))]


def shards(dosage, band_width, marginal, penalty):
    groups, count = lax.axis_size("samp"), lax.axis_size("snp")
    local, size, rows = dosage.shape[0], dosage.shape[1], marginal.shape[1]
    samples = local * groups
    start = marginal.T
    shrink = jnp.pad(penalty, (0, AUX - rows), constant_values=1.0)[None]
    grid, own_shape = (rows, size), (rows, local)
    own_out, coded_out = (own_shape, jnp.float32), ((rows, local + AUX), jnp.int16)
    shared_out = ((rows, local + LESS), jnp.int16)

    sent_outs = [((rows, size + lanes), jnp.int16) for lanes in (AUX, LESS, LEAST)]

    sums, brief = call(stats_kernel, [((8, size), jnp.float32), ((2, size), jnp.float32)], dosage)
    one, two, three = swap(brief, "samp", 1), swap(brief, "samp", 2), swap(sums, "samp", 3)
    one, band_width = lax.optimization_barrier((one, band_width))
    wide = pl.pallas_call(
        wide_kernel,
        out_shape=jax.ShapeDtypeStruct((8, size + AUX), jnp.float32),
        in_specs=[pl.BlockSpec(memory_space=pltpu.SMEM)],
        out_specs=pl.BlockSpec(memory_space=pltpu.VMEM),
        cost_estimate=pl.CostEstimate(flops=10**10, bytes_accessed=10**8, transcendentals=0),
    )(band_width)
    near = shifted(wide)
    two, three, near = lax.optimization_barrier((two, three, near))
    scaled, own, coded, shared = call(
        functools.partial(first_kernel, samples),
        [(dosage.shape, jnp.bfloat16), own_out, coded_out, shared_out],
        wide, sums, one, two, three, dosage, start,
    )

    (turned,) = call(turn_kernel, [(dosage.shape[::-1], jnp.bfloat16)], scaled)

    def give(up, *args):
        return call(functools.partial(give_kernel, count, up), [coded_out], near, *args)[0]

    def window(own, coded, shared, last):
        beside = adjacent(coded)
        partner = swap(shared, "snp", 1)
        cross = crossing(give(1, own, coded, partner), 1)
        same = crossing(give(0, own, coded, beside), 0)
        (early,) = call(functools.partial(early_kernel, count), [own_out], own, coded, partner, beside)
        z, brief, least = call(
            functools.partial(window_kernel, samples, count, last), sent_outs,
            own, early, same, cross, scaled,
        )
        return [z, swap(brief, "samp", 1), swap(least, "samp", 2), swap(z, "samp", 3)]

    first, own, coded, shared = call(
        functools.partial(next_kernel, samples),
        [(grid, jnp.float32), own_out, coded_out, shared_out],
        wide, *window(own, coded, shared, False), turned,
    )
    (parts,) = call(parts_kernel, [((rows, AUX), jnp.float32)], start, first)
    zs = window(own, coded, shared, True)
    (flat,) = call(collect_kernel, [((8, AUX), jnp.float32)], parts, *zs)
    parts = snp_parts(flat)
    (second,) = call(functools.partial(second_kernel, samples), [(grid, jnp.float32)], *zs)
    effects, residual = call(
        last_kernel,
        [(grid, jnp.float32), (grid, jnp.float32)],
        shrink, *parts, second, start, first,
    )
    return (effects.T, residual.T)


def solution(mesh):
    in_specs = (P("samp", "snp"), P("snp"), P("snp", None), P())
    out_specs = (P("snp", None), P("snp", None))
    return jax.shard_map(shards, mesh=mesh, in_specs=in_specs, out_specs=out_specs, check_vma=False)
```

```python
import functools

import jax
import jax.numpy as jnp
from jax import lax
from jax.experimental import pallas as pl
from jax.experimental.pallas import tpu as pltpu
from jax.sharding import PartitionSpec as P


AUX = 128
LESS = 96
LEAST = 64
CHUNK = 512
UNIT = 14
SAFE = 1.0 - 2.0**-13
ROWS = 256


def swap(value, axis, bits):
    return lax.ppermute(value, axis, [(i, i ^ bits) for i in range(lax.axis_size(axis))])


def crossing(value, rising):
    count = lax.axis_size("snp")
    pairs = []
    for i in range(count):
        target = i + 2 if i % 2 == rising else i - 2
        pairs.append((i, target if 0 <= target < count else i ^ 1))
    return lax.ppermute(value, "snp", pairs)


def adjacent(value):
    rows, count = lax.axis_size("samp"), lax.axis_size("snp")
    pairs = []
    for row in range(rows):
        for i in range(count):
            target = i + 1 if i % 2 else i - 1
            inside = 0 <= target < count
            pairs.append((row * count + i, row * count + target if inside else (row ^ 1) * count + i))
    return lax.ppermute(value, ("samp", "snp"), pairs)


def shifted(value):
    count = lax.axis_size("snp")
    return lax.ppermute(value, "snp", [(i, (i + 2) % count) for i in range(count)])


def partners(value, axis, low, high):
    return [swap(value, axis, k) for k in (low, high, low + high)]


def total(parts):
    own, one, two, three = parts
    return (own + one) + (two + three)


def call(body, out_shape, *args):
    specs = [pl.BlockSpec(memory_space=pltpu.VMEM) for _ in args]
    outs = [jax.ShapeDtypeStruct(shape, kind) for shape, kind in out_shape]
    return pl.pallas_call(
        body,
        out_shape=outs,
        in_specs=specs,
        out_specs=[pl.BlockSpec(memory_space=pltpu.VMEM) for _ in outs],
        compiler_params=pltpu.CompilerParams(vmem_limit_bytes=32 << 20),
    )(*args)


def two_terms(value):
    high = value.astype(jnp.bfloat16)
    low = (value - high.astype(jnp.float32)).astype(jnp.bfloat16)
    return jnp.concatenate([high, low], 0)


def wide_kernel(width_ref, wide_ref):
    wide_ref[...] = jnp.full(wide_ref.shape, width_ref[0].astype(jnp.float32))


def stats_kernel(dosage_ref, sums_ref, brief_ref):
    acc = jnp.zeros((8, dosage_ref.shape[1]), jnp.float32)
    square = acc
    for k in range(0, dosage_ref.shape[0], ROWS):
        part = dosage_ref[pl.ds(k, ROWS)].astype(jnp.float32)
        part = part.reshape(ROWS // 8, 8, part.shape[1])
        acc = acc + jnp.sum(part, 0)
        square = square + jnp.sum(part * part, 0)
    row = lax.broadcasted_iota(jnp.int32, (8, 1), 0)
    first = jnp.sum(acc, 0, keepdims=True)
    second = jnp.sum(square, 0, keepdims=True)
    both = jnp.where(row == 0, first, second)
    sums_ref[...] = both
    brief_ref[...] = both[:2]


def finish(coded_ref, *columns):
    count = coded_ref.shape[1] % AUX or AUX
    lane = lax.broadcasted_iota(jnp.int32, (coded_ref.shape[0], count), 1)
    extra = jnp.zeros(lane.shape, jnp.float32)
    for k, column in enumerate(columns):
        extra = jnp.where(lane == k, column, extra)
    coded_ref[:, pl.ds(coded_ref.shape[1] - count, count)] = extra.astype(jnp.int32).astype(jnp.int16)


def fixed(value):
    return jnp.round(value).astype(jnp.int32).astype(jnp.int16)


def scale_of(peak):
    exponent = jnp.floor(jnp.log2(jnp.maximum(peak, 1e-30)))
    return exponent, jnp.exp2(UNIT - exponent) * SAFE


def encode(own_ref, coded_ref, shared_ref, width):
    exponent, scale = scale_of(jnp.max(jnp.abs(own_ref[...]), 1, keepdims=True))
    for k in range(0, own_ref.shape[1], CHUNK):
        value = fixed(own_ref[:, pl.ds(k, CHUNK)] * scale)
        coded_ref[:, pl.ds(k, CHUNK)] = value
        shared_ref[:, pl.ds(k, CHUNK)] = value
    finish(coded_ref, exponent, width)
    finish(shared_ref, exponent, width)


def split(value):
    exponent, scale = scale_of(jnp.abs(value))
    high = jnp.round(value * scale * 0.5)
    low = jnp.round((value * scale * 0.5 - high) * 2.0**UNIT)
    return exponent, high, low


def aux(coded_ref):
    count = coded_ref.shape[1] % AUX or AUX
    extra = coded_ref[:, pl.ds(coded_ref.shape[1] - count, count)].astype(jnp.int32).astype(jnp.float32)
    return [extra[:, k : k + 1] for k in range(4)]


def unit(exponent, use=True):
    return jnp.where(use, jnp.exp2(exponent - UNIT) / SAFE, 0.0)


def grid_values(coded_ref):
    size = coded_ref.shape[1] - (coded_ref.shape[1] % AUX or AUX)
    return coded_ref[:, pl.ds(0, size)].astype(jnp.int32).astype(jnp.float32) * unit(aux(coded_ref)[0])


def values(coded_ref, k):
    return coded_ref[:, pl.ds(k, CHUNK)].astype(jnp.int32).astype(jnp.float32)


def project(value, turned_ref, own_ref):
    rows = value.shape[0]
    terms = two_terms(value)
    for k in range(0, turned_ref.shape[1], CHUNK):
        both = jnp.dot(terms, turned_ref[:, pl.ds(k, CHUNK)], preferred_element_type=jnp.float32)
        own_ref[:, pl.ds(k, CHUNK)] = both[:rows] + both[rows:]


def first_kernel(samples, wide_ref, s0, s1, s2, s3, dosage_ref, start_ref, scaled_ref, own_ref, coded_ref, shared_ref):
    sums = total([s[0:2] for s in (s0, s1, s2, s3)])
    center = sums[0:1] / samples
    spread = sums[1:2] / samples - center * center
    factor = lax.rsqrt(spread + 1e-05)
    for k in range(0, dosage_ref.shape[0], CHUNK):
        part = dosage_ref[pl.ds(k, CHUNK)].astype(jnp.float32)
        scaled_ref[pl.ds(k, CHUNK)] = ((part - center) * factor).astype(jnp.bfloat16)
    terms = two_terms(start_ref[...])
    rows = start_ref.shape[0]
    for k in range(0, dosage_ref.shape[0], CHUNK):
        both = lax.dot_general(
            terms, scaled_ref[pl.ds(k, CHUNK)], (((1,), (1,)), ((), ())), preferred_element_type=jnp.float32
        )
        own_ref[:, pl.ds(k, CHUNK)] = both[:rows] + both[rows:]
    encode(own_ref, coded_ref, shared_ref, wide_ref[0:1, 0:1])


def turn_kernel(scaled_ref, turned_ref):
    for k in range(0, scaled_ref.shape[0], CHUNK):
        turned_ref[:, pl.ds(k, CHUNK)] = scaled_ref[pl.ds(k, CHUNK)].T


def parts_kernel(start_ref, first_ref, parts_ref):
    first = first_ref[...]
    start = start_ref[...]
    lane = lax.broadcasted_iota(jnp.int32, parts_ref.shape, 1)
    parts = jnp.zeros(parts_ref.shape, jnp.float32)
    for k, (a, b) in enumerate(((start, start), (start, first), (first, first))):
        parts = jnp.where(lane == k, jnp.sum(a * b, 1, keepdims=True), parts)
    parts_ref[...] = parts


def next_kernel(
    samples, wide_ref, z0, z1, z2, z3, turned_ref, first_ref, own_ref, coded_ref, shared_ref
):
    first = total([grid_values(z) for z in (z0, z1, z2, z3)]) / samples
    first_ref[...] = first
    project(first, turned_ref, own_ref)
    encode(own_ref, coded_ref, shared_ref, wide_ref[0:1, 0:1])


def place(count):
    index = lax.axis_index("snp")
    odd = (index & 1) == 1
    below, above = (index >= 2).astype(jnp.int32), (index < count - 2).astype(jnp.int32)
    side = jnp.where(odd, above, below) == 1
    across = jnp.where(odd, below, above) == 1
    return odd, side, across


def give_kernel(count, up, near_ref, own_ref, coded_ref, other_ref, sent_ref):
    odd, side, _ = place(count)
    exponent, width = aux(coded_ref)[:2]
    other_exponent, other_width = aux(other_ref)[:2]
    near = near_ref[0:1, 0:1]
    sent = jnp.maximum(exponent, other_exponent) + 1.0
    scale = jnp.exp2(UNIT - sent) * SAFE
    rises = odd if up else jnp.logical_not(odd)
    known = True if up else side
    own_scale = jnp.where(jnp.where(rises, width, near) >= 2, scale, 0.0)
    other_scale = jnp.where(jnp.where(rises, other_width, near) >= 3, scale * unit(other_exponent, known), 0.0)
    for k in range(0, own_ref.shape[1], CHUNK):
        sent_ref[:, pl.ds(k, CHUNK)] = fixed(own_ref[:, pl.ds(k, CHUNK)] * own_scale + values(other_ref, k) * other_scale)
    finish(sent_ref, sent, width)


def early_kernel(count, own_ref, coded_ref, partner_ref, next_ref, early_ref):
    odd, side, _ = place(count)
    width = aux(coded_ref)[1]
    partner_exponent, partner_width = aux(partner_ref)[:2]
    next_exponent, next_width = aux(next_ref)[:2]
    partner_scale = unit(partner_exponent, jnp.where(odd, partner_width, width) >= 1)
    next_scale = jnp.where(jnp.where(odd, width, next_width) >= 1, unit(next_exponent, side), 0.0)
    for k in range(0, own_ref.shape[1], CHUNK):
        early_ref[:, pl.ds(k, CHUNK)] = (
            own_ref[:, pl.ds(k, CHUNK)]
            + values(partner_ref, k) * partner_scale
            + values(next_ref, k) * next_scale
        )


def window_kernel(samples, count, last, own_ref, early_ref, same_ref, cross_ref, scaled_ref, *sent_refs):
    _, side, across = place(count)
    same_scale = unit(aux(same_ref)[0], side)
    cross_scale = unit(aux(cross_ref)[0], across)
    rows = own_ref.shape[0]
    acc = jnp.zeros((2 * rows, scaled_ref.shape[1]), jnp.float32)
    curved = jnp.zeros((rows, CHUNK), jnp.float32)
    for k in range(0, own_ref.shape[1], CHUNK):
        mixed = early_ref[:, pl.ds(k, CHUNK)] + values(same_ref, k) * same_scale + values(cross_ref, k) * cross_scale
        acc = acc + jnp.dot(
            two_terms(mixed), scaled_ref[pl.ds(k, CHUNK)], preferred_element_type=jnp.float32
        )
        if last:
            curved = curved + own_ref[:, pl.ds(k, CHUNK)] * mixed
    z = acc[:rows] + acc[rows:]
    exponent, scale = scale_of(jnp.max(jnp.abs(z), 1, keepdims=True))
    columns = (exponent, *split(jnp.sum(curved, 1, keepdims=True) / samples)) if last else (exponent,)
    z = fixed(z * scale)
    for ref in sent_refs:
        ref[:, pl.ds(0, z.shape[1])] = z
        finish(ref, *columns)


def collect_kernel(parts_ref, z0, z1, z2, z3, flat_ref):
    terms = []
    for z in (z0, z1, z2, z3):
        _, exponent, high, low = aux(z)
        terms.append((high + low * 2.0**-UNIT) * 2.0 * unit(exponent))
    lane = lax.broadcasted_iota(jnp.int32, parts_ref.shape, 1)
    parts = jnp.where(lane == 3, total(terms), parts_ref[...])
    filled = jnp.concatenate([parts, jnp.ones((AUX - parts.shape[0], AUX), jnp.float32)], 0)
    flat_ref[...] = filled.T[:8]


def second_kernel(samples, z0, z1, z2, z3, second_ref):
    second_ref[...] = total([grid_values(z) for z in (z0, z1, z2, z3)]) / samples


def last_kernel(shrink_ref, p0, p1, p2, p3, second_ref, start_ref, first_ref, effects_ref, residual_ref):
    rows = start_ref.shape[0]
    flat = total([p[0:4] for p in (p0, p1, p2, p3)])
    bb, bw, ww, wu = (flat[k : k + 1] for k in range(4))
    shrink = shrink_ref[...]
    ratio = bw / bb
    step = 1.0 / (ratio + shrink)
    square = step * step
    norm = square * (ww - ratio * bw)
    bend = norm / bb
    curve = square * (ratio * (ratio * bw - 2.0 * ww) + wu) + shrink * norm - bend * norm * (ratio + shrink)
    step2 = jnp.where(curve > 0, norm / curve, 0.0)
    lead = step * ratio + bend
    coefficients = (
        step + step2 * lead,
        -step2 * step,
        step * ratio - step2 * shrink * lead,
        -step - step2 * (lead - shrink * step),
        step2 * step,
    )
    row = lax.broadcasted_iota(jnp.int32, (AUX, AUX), 0)
    table = jnp.zeros((AUX, AUX), jnp.float32)
    for k, value in enumerate(coefficients):
        table = jnp.where(row == k, value, table)
    table = table.T[:rows]
    e_start, e_first, r_start, r_first, r_second = (table[:, k : k + 1] for k in range(5))
    start, first = start_ref[...], first_ref[...]
    effects_ref[...] = e_start * start + e_first * first
    residual_ref[...] = r_start * start + r_first * first + r_second * second_ref[...]


def snp_parts(value):
    count = lax.axis_size("snp")
    value = value + swap(value, "snp", 1)
    bit = 2
    while 4 * bit < count:
        value = jnp.pad(total([part[:4] for part in (value, *others(value, bit))]), ((0, 4), (0, 0)))
        bit *= 4
    if 2 * bit < count:
        return [value, *others(value, bit)]
    return [value, swap(value, "snp", bit ^ 1), jnp.zeros_like(value), jnp.zeros_like(value)]


def others(value, bit):
    return [swap(value[:rows], "snp", k ^ 1) for k, rows in ((bit, 4), (2 * bit, 6), (3 * bit, 8))]


def shards(dosage, band_width, marginal, penalty):
    groups, count = lax.axis_size("samp"), lax.axis_size("snp")
    local, size, rows = dosage.shape[0], dosage.shape[1], marginal.shape[1]
    samples = local * groups
    start = marginal.T
    shrink = jnp.pad(penalty, (0, AUX - rows), constant_values=1.0)[None]
    grid, own_shape = (rows, size), (rows, local)
    own_out, coded_out = (own_shape, jnp.float32), ((rows, local + AUX), jnp.int16)
    shared_out = ((rows, local + LESS), jnp.int16)

    sent_outs = [((rows, size + lanes), jnp.int16) for lanes in (AUX, LESS, LEAST)]

    sums, brief = call(stats_kernel, [((8, size), jnp.float32), ((2, size), jnp.float32)], dosage)
    one, two, three = swap(brief, "samp", 1), swap(brief, "samp", 2), swap(sums, "samp", 3)
    one, band_width = lax.optimization_barrier((one, band_width))
    wide = pl.pallas_call(
        wide_kernel,
        out_shape=jax.ShapeDtypeStruct((8, size + AUX), jnp.float32),
        in_specs=[pl.BlockSpec(memory_space=pltpu.SMEM)],
        out_specs=pl.BlockSpec(memory_space=pltpu.VMEM),
        cost_estimate=pl.CostEstimate(flops=10**10, bytes_accessed=10**8, transcendentals=0),
    )(band_width)
    near = shifted(wide)
    two, three, near = lax.optimization_barrier((two, three, near))
    scaled, own, coded, shared = call(
        functools.partial(first_kernel, samples),
        [(dosage.shape, jnp.bfloat16), own_out, coded_out, shared_out],
        wide, sums, one, two, three, dosage, start,
    )

    (turned,) = call(turn_kernel, [(dosage.shape[::-1], jnp.bfloat16)], scaled)

    def give(up, *args):
        return call(functools.partial(give_kernel, count, up), [coded_out], near, *args)[0]

    def window(own, coded, shared, last):
        beside = adjacent(coded)
        partner = swap(shared, "snp", 1)
        cross = crossing(give(1, own, coded, partner), 1)
        same = crossing(give(0, own, coded, beside), 0)
        (early,) = call(functools.partial(early_kernel, count), [own_out], own, coded, partner, beside)
        z, brief, least = call(
            functools.partial(window_kernel, samples, count, last), sent_outs,
            own, early, same, cross, scaled,
        )
        return [z, swap(brief, "samp", 1), swap(least, "samp", 2), swap(z, "samp", 3)]

    first, own, coded, shared = call(
        functools.partial(next_kernel, samples),
        [(grid, jnp.float32), own_out, coded_out, shared_out],
        wide, *window(own, coded, shared, False), turned,
    )
    (parts,) = call(parts_kernel, [((rows, AUX), jnp.float32)], start, first)
    zs = window(own, coded, shared, True)
    (flat,) = call(collect_kernel, [((8, AUX), jnp.float32)], parts, *zs)
    parts = snp_parts(flat)
    (second,) = call(functools.partial(second_kernel, samples), [(grid, jnp.float32)], *zs)
    effects, residual = call(
        last_kernel,
        [(grid, jnp.float32), (grid, jnp.float32)],
        shrink, *parts, second, start, first,
    )
    return (effects.T, residual.T)


def solution(mesh):
    in_specs = (P("samp", "snp"), P("snp"), P("snp", None), P())
    out_specs = (P("snp", None), P("snp", None))
    return jax.shard_map(shards, mesh=mesh, in_specs=in_specs, out_specs=out_specs, check_vma=False)
```
